256 devices in a mesh: gx: 32 (over x_hi, z, core), gy: 8 (over x_lo, y).
Axes of the slice: x: 4 (x_hi: 2, x_lo: 2; x = x_hi * 2 + x_lo), y: 4, z: 8, core: 2. Of those that a mesh axis runs over, the one named last changes fastest.
Arguments:
- forward: float32 [19, 1024, 4096], P(None, 'gx', 'gy'), may hold values from 0.02 to 0.12
- adjoint: float32 [19, 1024, 4096], P(None, 'gx', 'gy'), may hold values from -6 to 6
- design: float32 [1024, 4096], P('gx', 'gy'), may hold values from 0 to 0.6
- node_type: int32 [1024, 4096], P('gx', 'gy'), may hold values from 0 to 3
Outputs:
- adjoint_new: float32 [19, 1024, 4096], P(None, 'gx', 'gy')
- filtered: float32 [1024, 4096], P('gx', 'gy')
The draws below stay inside these ranges and needn't reach their ends.
Inputs may be any that keep to these rules, and one draw needn't show every extreme that they name: `node_type`: 0 fluid, 1 wall, 2 inlet, 3 outlet.
All inputs are finite; a program needn't handle non-finite values.
Results may differ from the reference program's by a relative error of at most 0.00019.
Values sent between devices are 32-bit elements; how exact they have to be, the bound alone decides.
No kernel may reach another device: no remote copies, remote signals or barrier semaphores. Data moves between devices by JAX's collectives and lax.ppermute only.
A program may use at most 64 MiB of HBM per device.

```python
import jax
import jax.numpy as jnp
import numpy as np
from jax import lax

NZ = 16
ITERS = 3
NX = 1024
NY = 256


def place_ends(entries, key, low, top_value):
    spot = [jax.random.randint(jax.random.fold_in(key, axis), (), 0, length) for axis, length in enumerate(entries.shape)]
    main_axis = entries.shape.index(max(entries.shape))
    beside = spot[:main_axis] + [(spot[main_axis] + 1) % entries.shape[main_axis]] + spot[main_axis + 1:]
    return entries.at[tuple(spot)].set(low).at[tuple(beside)].set(top_value)


def block_scale(own_key, extent, pieces, smallest, largest):
    loudness = 1.0
    for dim, shards_of in pieces:
        draws = jax.random.uniform(jax.random.fold_in(jax.random.fold_in(own_key, 6), dim), (shards_of,), jnp.float32, smallest / len(pieces), largest / len(pieces))
        loudness = loudness * jnp.repeat(jnp.exp(draws), extent[dim] // shards_of).reshape((-1,) + (1,) * (len(extent) - 1 - dim))
    return loudness


def centred(own_key, extent, deviation, limit, pieces=(), kind=jnp.bfloat16):
    drawn = jax.random.normal(own_key, extent, jnp.float32) * deviation
    if len(pieces) > 0:
        drawn = block_scale(own_key, extent, pieces, -0.22, 0.18) * drawn
    return jnp.clip(drawn, min=-limit, max=limit).astype(kind)


def setup_inputs(seed: int = 0) -> dict:
    keys = jax.random.split(jax.random.key(seed), 5)
    return {
        "forward": jnp.clip(0.02 + 0.09999999776482582 * jax.random.uniform(keys[0], (19, NX, NY * NZ), jnp.float32) ** block_scale(keys[0], (19, NX, NY * NZ), ((1, 32), (2, 8)), -0.2, 0.2), 0.02, 0.12),
        "adjoint": centred(keys[1], (19, NX, NY * NZ), 1.0, 6.0, ((1, 32), (2, 8)), jnp.float32),
        "design": jnp.clip(0.6 * jax.random.uniform(keys[2], (NX, NY * NZ), jnp.float32) ** block_scale(keys[2], (NX, NY * NZ), ((0, 32), (1, 8)), -0.2, 0.2), 0.0, 0.6),
        "node_type": place_ends(jax.random.randint(keys[3], (NX, NY * NZ), 0, 4), jax.random.fold_in(keys[3], 1), 0, 3).astype(jnp.int32),
    }


velocities = np.array([[0, 0, 0], [1, 0, 0], [-1, 0, 0], [0, 1, 0], [0, -1, 0], [0, 0, 1], [0, 0, -1],
                       [1, 1, 0], [-1, -1, 0], [1, -1, 0], [-1, 1, 0], [1, 0, 1], [-1, 0, -1], [1, 0, -1],
                       [-1, 0, 1], [0, 1, 1], [0, -1, -1], [0, 1, -1], [0, -1, 1]])
OPPOSITE = np.array([0, 2, 1, 4, 3, 6, 5, 8, 7, 10, 9, 12, 11, 14, 13, 16, 15, 18, 17], dtype=np.int32)
lattice_weights = np.array([1.0 / 3.0] + [1.0 / 18.0] * 6 + [1.0 / 36.0] * 12)
relax_rate = 1.25
radius_sq = 4.0


def adjoint_cell(read, forward, design, node_type):
    highest = lax.Precision.HIGHEST
    table = jnp.asarray(velocities, jnp.float32)
    weights = jnp.asarray(lattice_weights, jnp.float32)[:, None, None]
    density = jnp.sum(forward, axis=0)
    momentum = jnp.einsum("qk,qxw->kxw", table, forward, precision=highest)
    velocity = momentum / density
    projected = jnp.einsum("qk,kxw->qxw", table, velocity, precision=highest)
    speed_sq = jnp.sum(velocity * velocity, axis=0)
    equilibrium = weights * density * (1.0 + 3.0 * projected + 4.5 * projected * projected - 1.5 * speed_sq)
    collided = forward - relax_rate * (forward - equilibrium)
    is_fluid = node_type != 1
    sensitivity = jnp.where(is_fluid, jnp.sum(read * (collided[OPPOSITE] - collided), axis=0), 0.0)
    blended = (1.0 - design) * read + design * read[OPPOSITE]
    weighted = weights * blended
    zeroth = jnp.sum(weighted, axis=0)
    first_moment = jnp.einsum("qk,qxw->kxw", table, weighted, precision=highest)
    second = jnp.einsum("qk,qxw->kxw", table, weighted * projected, precision=highest)
    quadratic = jnp.sum(weighted * projected * projected, axis=0)
    combined = 3.0 * first_moment + 9.0 * second - 3.0 * velocity * zeroth
    projection = jnp.einsum("qk,kxw->qxw", table, combined, precision=highest)
    feq_adjoint = zeroth + projection - 4.5 * quadratic + 1.5 * speed_sq * zeroth
    relaxed = blended - relax_rate * (blended - feq_adjoint)
    source = (node_type == 2).astype(jnp.float32) - (node_type == 3).astype(jnp.float32)
    result = jnp.where(is_fluid, relaxed + source, read[OPPOSITE])
    return result, sensitivity


def stream_global(adjoint):
    grid = adjoint.reshape(19, NX, NY, NZ)
    depth_index = jnp.arange(NZ)
    pulled = []
    for member in range(19):
        step_x, step_y, step_z = [int(entry) for entry in velocities[member]]
        moved = jnp.roll(grid[member], -step_x, axis=0)
        moved = jnp.pad(moved, ((0, 0), (1, 1), (1, 1)))[:, 1 + step_y:1 + step_y + NY, 1 + step_z:1 + step_z + NZ]
        if step_z != 0:
            outside = (depth_index + step_z < 0) | (depth_index + step_z >= NZ)
            moved = jnp.where(outside, grid[int(OPPOSITE[member])], moved)
        pulled.append(moved.reshape(NX, NY * NZ))
    return jnp.stack(pulled)


def helmholtz(values):
    grid = values.reshape(NX, NY, NZ)
    padded = jnp.pad(grid, ((0, 0), (1, 1), (1, 1)))
    beside = jnp.roll(grid, 1, 0) + jnp.roll(grid, -1, 0)
    beside = beside + padded[:, 2:, 1:-1] + padded[:, :-2, 1:-1] + padded[:, 1:-1, 2:] + padded[:, 1:-1, :-2]
    return ((1.0 + 6.0 * radius_sq) * grid - radius_sq * beside).reshape(NX, NY * NZ)


def reference(forward, adjoint, design, node_type):
    read = stream_global(adjoint)
    adjoint_new, sensitivity = adjoint_cell(read, forward, design, node_type)
    filtered = jnp.zeros_like(sensitivity)
    residual = sensitivity
    direction = sensitivity
    norm_now = jnp.sum(residual * residual)
    for iteration in range(ITERS):
        applied = helmholtz(direction)
        step_size = norm_now / jnp.sum(direction * applied)
        filtered = filtered + step_size * direction
        residual = residual - step_size * applied
        norm_next = jnp.sum(residual * residual)
        direction = residual + (norm_next / norm_now) * direction
        norm_now = norm_next
    return adjoint_new, filtered
```

```python
import jax
import jax.numpy as jnp
import numpy as np
from jax import lax
from jax.sharding import PartitionSpec as P

NZ = 16
ITERS = 3


velocities = np.array(
    [
        [0, 0, 0],
        [1, 0, 0],
        [-1, 0, 0],
        [0, 1, 0],
        [0, -1, 0],
        [0, 0, 1],
        [0, 0, -1],
        [1, 1, 0],
        [-1, -1, 0],
        [1, -1, 0],
        [-1, 1, 0],
        [1, 0, 1],
        [-1, 0, -1],
        [1, 0, -1],
        [-1, 0, 1],
        [0, 1, 1],
        [0, -1, -1],
        [0, 1, -1],
        [0, -1, 1],
    ]
)
OPPOSITE = np.array(
    [0, 2, 1, 4, 3, 6, 5, 8, 7, 10, 9, 12, 11, 14, 13, 16, 15, 18, 17], dtype=np.int32
)
lattice_weights = np.array([1.0 / 3.0] + [1.0 / 18.0] * 6 + [1.0 / 36.0] * 12)
relax_rate = 1.25
radius_sq = 4.0


def padded_2(cells, sides, width, closed):
    for axis, dim in sides:
        count = lax.axis_size(axis)
        ends = count if closed else count - 1
        head = lax.slice_in_dim(cells, 0, width, axis=dim)
        tail = lax.slice_in_dim(cells, cells.shape[dim] - width, cells.shape[dim], axis=dim)
        cells = jnp.concatenate(
            [
                lax.ppermute(tail, axis, [(i, (i + 1) % count) for i in range(ends)]),
                cells,
                lax.ppermute(head, axis, [((i + 1) % count, i) for i in range(ends)]),
            ],
            axis=dim,
        )
    return cells


def adjoint_cell(read, forward, design, node_type):
    highest = lax.Precision.HIGHEST
    table = jnp.asarray(velocities, jnp.float32)
    weights = jnp.asarray(lattice_weights, jnp.float32)[:, None, None]
    density = jnp.sum(forward, axis=0)
    momentum = jnp.einsum("qk,qxw->kxw", table, forward, precision=highest)
    velocity = momentum / density
    projected = jnp.einsum("qk,kxw->qxw", table, velocity, precision=highest)
    speed_sq = jnp.sum(velocity * velocity, axis=0)
    equilibrium = (
        weights * density * (1.0 + 3.0 * projected + 4.5 * projected * projected - 1.5 * speed_sq)
    )
    collided = forward - relax_rate * (forward - equilibrium)
    is_fluid = node_type != 1
    sensitivity = jnp.where(is_fluid, jnp.sum(read * (collided[OPPOSITE] - collided), axis=0), 0.0)
    blended = (1.0 - design) * read + design * read[OPPOSITE]
    weighted = weights * blended
    zeroth = jnp.sum(weighted, axis=0)
    first_moment = jnp.einsum("qk,qxw->kxw", table, weighted, precision=highest)
    second = jnp.einsum("qk,qxw->kxw", table, weighted * projected, precision=highest)
    quadratic = jnp.sum(weighted * projected * projected, axis=0)
    combined = 3.0 * first_moment + 9.0 * second - 3.0 * velocity * zeroth
    projection = jnp.einsum("qk,kxw->qxw", table, combined, precision=highest)
    feq_adjoint = zeroth + projection - 4.5 * quadratic + 1.5 * speed_sq * zeroth
    relaxed = blended - relax_rate * (blended - feq_adjoint)
    source = (node_type == 2).astype(jnp.float32) - (node_type == 3).astype(jnp.float32)
    result = jnp.where(is_fluid, relaxed + source, read[OPPOSITE])
    return (result, sensitivity)


def gather_faces(adjoint):
    extended = padded_2(adjoint, (("gx", 1),), 1, True)
    return padded_2(extended, (("gy", 2),), NZ, False)


def pull_bordered(bordered, layers, columns):
    padded = jnp.pad(bordered, ((0, 0), (0, 0), (1, 1)))
    bounce = bordered[:, 1 : 1 + layers, NZ : NZ + columns]
    depth_index = jnp.arange(columns) % NZ
    pulled = []
    for member in range(19):
        step_x, step_y, step_z = [int(entry) for entry in velocities[member]]
        start = 1 + NZ + step_y * NZ + step_z
        moved = padded[member, 1 + step_x : 1 + step_x + layers, start : start + columns]
        if step_z != 0:
            outside = (depth_index + step_z < 0) | (depth_index + step_z >= NZ)
            moved = jnp.where(outside, bounce[int(OPPOSITE[member])], moved)
        pulled.append(moved)
    return jnp.stack(pulled)


def laplace(field, depth_index, inside):
    left = jnp.where(depth_index > 0, jnp.pad(field[:, :-1], ((0, 0), (1, 0))), 0.0)
    right = jnp.where(depth_index < NZ - 1, jnp.pad(field[:, 1:], ((0, 0), (0, 1))), 0.0)
    center = field[1:-1, NZ:-NZ]
    total = field[:-2, NZ:-NZ] + field[2:, NZ:-NZ]
    total = total + field[1:-1, : -2 * NZ] + field[1:-1, 2 * NZ :]
    total = total + left[1:-1, NZ:-NZ] + right[1:-1, NZ:-NZ]
    return jnp.where(inside, center - total * (1.0 / 6.0), 0.0)


def total_over_devices(row):
    size = lax.axis_size("gx") * lax.axis_size("gy")
    copies = jnp.broadcast_to(row[None], (size,) + row.shape)
    return jnp.sum(lax.all_to_all(copies, ("gx", "gy"), 0, 0), axis=0)


def times_h(poly):
    top = 1.0 + 6.0 * radius_sq - 1.0
    out = list(poly) + [0.0]
    for power, entry in enumerate(poly):
        out[power + 1] = out[power + 1] + top * entry
    return out


def dot_poly(p, q, moments):
    total = 0.0
    for i, left in enumerate(p):
        for j, right in enumerate(q):
            total = total + left * right * moments[i + j]
    return total


def combination(moments):
    upper = 1.0 + 12.0 * radius_sq
    growth = (upper - 1.0) ** 2 / (4.0 * upper) * 1.001
    zero, one = jnp.zeros_like(moments[0]), jnp.ones_like(moments[0])
    solved, residual, direction = [zero], [one], [one]
    norm_now = moments[0]
    for iteration in range(ITERS):
        image = times_h(direction)
        step = norm_now / dot_poly(direction, image, moments)
        step = jnp.clip(step, 1.0 / upper, 1.0)
        solved = [
            (solved[k] if k < len(solved) else 0.0) + step * direction[k]
            for k in range(len(direction))
        ]
        if iteration == ITERS - 1:
            break
        residual = [
            (residual[k] if k < len(residual) else 0.0) - step * image[k] for k in range(len(image))
        ]
        norm_next = dot_poly(residual, residual, moments)
        ratio = jnp.clip(norm_next / norm_now, 0.0, growth)
        direction = [
            residual[k] + (ratio * direction[k] if k < len(direction) else 0.0)
            for k in range(len(residual))
        ]
        norm_now = jnp.maximum(norm_next, 0.0)
    return solved


def solve_filter(sensitivity):
    layers, columns = sensitivity.shape
    wide = padded_2(sensitivity, (("gx", 0),), ITERS, True)
    wide = padded_2(wide, (("gy", 1),), ITERS * NZ, False)
    place = lax.axis_index("gy")
    vectors = [wide]
    for power in range(ITERS):
        margin = (ITERS - power) * NZ
        column = jnp.arange(columns + 2 * margin)
        depth_index = column % NZ
        inner = column[NZ:-NZ] - margin + place * columns
        inside = (inner >= 0) & (inner < columns * lax.axis_size("gy"))
        vectors.append(laplace(vectors[-1], depth_index, inside))
    cores = []
    for power, field in enumerate(vectors):
        margin = ITERS - power
        cores.append(field[margin : margin + layers, margin * NZ : margin * NZ + columns])
    pairs = [(0, 0), (0, 1), (1, 1), (1, 2), (2, 2), (2, 3)]
    local = jnp.stack([jnp.sum(cores[i] * cores[j]) for i, j in pairs])
    row = jnp.pad(local, (0, 128 - len(pairs)))[None]
    moments = total_over_devices(row)[0]
    weights = combination([moments[k] for k in range(len(pairs))])
    return sum(weight * core for weight, core in zip(weights, cores))


def shards(forward, adjoint, design, node_type):
    populations, layers, columns = adjoint.shape
    read = pull_bordered(gather_faces(adjoint), layers, columns)
    adjoint_new, sensitivity = adjoint_cell(read, forward, design, node_type)
    filtered = solve_filter(sensitivity)
    return (adjoint_new, filtered)


def solution(mesh):
    placed = (P(None, "gx", "gy"), P(None, "gx", "gy"), P("gx", "gy"), P("gx", "gy"))
    return jax.shard_map(
        shards,
        mesh=mesh,
        in_specs=placed,
        out_specs=(P(None, "gx", "gy"), P("gx", "gy")),
        check_vma=False,
    )
```

```python
import jax
import jax.numpy as jnp
from jax import lax
from jax.experimental import pallas as pl
from jax.experimental.pallas import tpu as pltpu
from jax.sharding import PartitionSpec as P

NZ = 16
ITERS = 3
PAIRS = (
    (1, 0, 0),
    (0, 1, 0),
    (0, 0, 1),
    (1, 1, 0),
    (1, -1, 0),
    (1, 0, 1),
    (1, 0, -1),
    (0, 1, 1),
    (0, 1, -1),
)
WEIGHTS = (1.0 / 18.0,) * 3 + (1.0 / 36.0,) * 6
REST_WEIGHT = 1.0 / 3.0
X_PAIRS = (0, 3, 4, 5, 6)
Y_PAIRS = (1, 3, 4, 7, 8)
relax_rate = 1.25
radius_sq = 4.0
ROWS = 8
READS = 80
EDGE = 160


def iota(shape, axis):
    return lax.broadcasted_iota(jnp.int32, shape, axis)


def roll(value, shift, axis):
    shift = shift % value.shape[axis]
    return value if shift == 0 else pltpu.roll(value, shift, axis)


def signed_sum(terms):
    total = None
    for sign, value in terms:
        if total is None:
            total = value if sign > 0 else -value
        else:
            total = total + value if sign > 0 else total - value
    return total


def dot_velocity(velocity, vector):
    return signed_sum([(c, v) for c, v in zip(velocity, vector) if c != 0])


def momentum_of(differences):
    return [
        signed_sum([(PAIRS[k][axis], differences[k]) for k in range(9) if PAIRS[k][axis] != 0])
        for axis in range(3)
    ]


def member_of(k, sign):
    return 2 * k + 1 if sign > 0 else 2 * k + 2


def row_tile(ref, member, tile, step, above=None, below=None):
    start = tile * ROWS
    layers = ref.shape[1]
    if step == 0:
        return ref[member, start : start + ROWS, :]
    if 0 <= start + step and start + step + ROWS <= layers:
        return ref[member, start + step : start + step + ROWS, :]
    value = ref[member, start : start + ROWS, :]
    row = iota(value.shape, 0)
    if step > 0:
        return jnp.where(row < ROWS - 1, roll(value, ROWS - 1, 0), 0.0 if above is None else above)
    return jnp.where(row > 0, roll(value, 1, 0), 0.0 if below is None else below)


def slide(value, step_y, step_z):
    columns = value.shape[1]
    if step_y == 0 and step_z == 0:
        return value
    moved = roll(value, -(step_y * NZ + step_z), 1)
    column = iota(value.shape, 1)
    keep = None
    if step_y != 0:
        keep = column < columns - NZ if step_y > 0 else column >= NZ
    if step_z != 0:
        depth = column & (NZ - 1)
        inner = depth < NZ - 1 if step_z > 0 else depth > 0
        keep = inner if keep is None else keep & inner
    return jnp.where(keep, moved, 0.0)


def leaves_depth(shape, step_z):
    depth = iota(shape, 1) & (NZ - 1)
    return depth == NZ - 1 if step_z > 0 else depth == 0


def block_at(lane, start):
    return (lane >= start) & (lane < start + NZ)


def pack_edge(gains, populations, high):
    origin = 0 if not high else 128 - NZ
    shape = (ROWS, 128)
    lane = iota(shape, 1)
    halves = [jnp.zeros(shape, jnp.float32), jnp.zeros(shape, jnp.float32)]
    for place, value in enumerate(list(gains) + list(populations)):
        columns = value.shape[1]
        part = value[:, :128] if not high else value[:, columns - 128 :]
        half, start = divmod(place * NZ, 128)
        halves[half] = jnp.where(block_at(lane, start), roll(part, start - origin, 1), halves[half])
    return jnp.concatenate(halves, axis=1)


def collide_kernel(forward, adjoint, node_type, partial, edges, out_s, out_z):
    layers, columns = partial.shape
    tiles = layers // ROWS
    shape = (ROWS, columns)
    row = iota(shape, 0)
    packs = {}
    for tile in range(tiles):
        rows = slice(tile * ROWS, tile * ROWS + ROWS)
        differences = [forward[2 * k + 1, rows, :] - forward[2 * k + 2, rows, :] for k in range(9)]
        momentum = momentum_of(differences)
        fluid = node_type[rows, :] != 1
        gains = []
        total = None
        for k in range(9):
            gain = (relax_rate - 1.0) * differences[k]
            gain = gain - (6.0 * relax_rate * WEIGHTS[k]) * dot_velocity(PAIRS[k], momentum)
            gain = jnp.where(fluid, gain, 0.0)
            gains.append(gain)
            reads = []
            for sign in (1, -1):
                step = [sign * c for c in PAIRS[k]]
                read = row_tile(adjoint, member_of(k, sign), tile, step[0])
                read = slide(read, step[1], step[2])
                if step[2] != 0:
                    bounce = adjoint[member_of(k, -sign), rows, :]
                    read = jnp.where(leaves_depth(shape, step[2]), bounce, read)
                reads.append(read)
            term = (reads[0] - reads[1]) * gain
            total = term if total is None else total + term
        partial[rows, :] = total
        packed = []
        for high in (False, True):
            way = -1 if high else 1
            populations = [
                adjoint[member_of(k, way * PAIRS[k][1]), rows, :] for k in Y_PAIRS
            ]
            packed.append(pack_edge([gains[k] for k in Y_PAIRS], populations, high))
        edge = jnp.concatenate(packed, axis=1)
        edges[rows, :] = edge
        if tile == 0:
            top = total
            faces = jnp.zeros(shape, jnp.float32)
            for place, k in enumerate(X_PAIRS):
                top = jnp.where(row == 3 + place, gains[k][0:1, :], top)
                faces = jnp.where(row == place, adjoint[member_of(k, 1), 0:1, :], faces)
            packs["down"] = (top, edge, faces)
        if tile == tiles - 1:
            top = total
            faces = jnp.zeros(shape, jnp.float32)
            for place, k in enumerate(X_PAIRS):
                top = jnp.where(row == place, gains[k][ROWS - 1 :, :], top)
                last = adjoint[member_of(k, -1), layers - 1 : layers, :]
                faces = jnp.where(row == place, last, faces)
            packs["up"] = (top, edge, faces)
    even = (lax.axis_index("gx") & 1) == 0
    for part in range(3):
        rows = slice(part * ROWS, part * ROWS + ROWS)
        out_s[rows, :] = jnp.where(even, packs["up"][part], packs["down"][part])
        out_z[rows, :] = jnp.where(even, packs["down"][part], packs["up"][part])


def face_reads(faces, sign):
    row = iota(faces.shape, 0)
    result = faces
    for place, k in enumerate(X_PAIRS):
        step_y, step_z = sign * PAIRS[k][1], sign * PAIRS[k][2]
        if step_y or step_z:
            result = jnp.where(row == place, slide(faces, step_y, step_z), result)
    return result


def outgoing(edge, way):
    lane = iota(edge.shape, 1)
    result = edge
    for place, k in enumerate(Y_PAIRS):
        sign = way * PAIRS[k][1]
        step_x, step_z = sign * PAIRS[k][0], sign * PAIRS[k][2]
        start = READS + place * NZ
        if step_x:
            result = jnp.where(block_at(lane, start), roll(edge, -step_x, 0), result)
        if step_z:
            moved = jnp.where(leaves_depth(edge.shape, step_z), 0.0, roll(edge, -step_z, 1))
            result = jnp.where(block_at(lane, start), moved, result)
    return result


def faces_kernel(partial, edges, own_s, own_z, got_s, got_z, wide, out_s, out_z):
    layers, columns = partial.shape
    even = (lax.axis_index("gx") & 1) == 0

    def pick(first, second, part):
        rows = slice(part * ROWS, part * ROWS + ROWS)
        return jnp.where(even, first[rows, :], second[rows, :])

    up = [pick(own_s, own_z, part) for part in range(3)]
    down = [pick(own_z, own_s, part) for part in range(3)]
    above = [pick(got_s, got_z, part) for part in range(3)]
    below = [pick(got_z, got_s, part) for part in range(3)]
    row = iota((ROWS, columns), 0)

    def completion(reads, gains):
        return jnp.sum(reads * gains, axis=0, keepdims=True)

    own_last = completion(face_reads(above[2], 1), up[0])
    own_first = completion(face_reads(below[2], -1), roll(down[0], -3, 0))
    far_first = completion(face_reads(up[2], -1), roll(above[0], -3, 0))
    far_last = completion(face_reads(down[2], 1), below[0])
    last = ROWS - 1
    wide[:ROWS, :] = below[0] + jnp.where(row == last, far_last, 0.0)
    wide[ROWS : 2 * ROWS, :] = partial[:ROWS, :] - jnp.where(row == 0, own_first, 0.0)
    wide[2 * ROWS : layers, :] = partial[ROWS : layers - ROWS, :]
    wide[layers : layers + ROWS, :] = partial[layers - ROWS :, :] + jnp.where(
        row == last, own_last, 0.0
    )
    wide[layers + ROWS :, :] = above[0] - jnp.where(row == 0, far_first, 0.0)

    edge = jnp.concatenate([below[1], edges[...], above[1]], axis=0)
    half = edge.shape[1] // 2
    low = outgoing(edge[:, :half], 1)
    high = outgoing(edge[:, half:], -1)
    low_field = roll(wide[:, :128], EDGE - 128, 1)
    high_field = roll(wide[:, columns - 128 :], EDGE - 128 - (128 - 3 * NZ), 1)
    lane = iota(low_field.shape, 1)
    held = (lane >= EDGE - 128) & (lane < EDGE - 128 + 3 * NZ)
    to_left = [low[:, :128], jnp.where(held, low_field, low[:, 128:])]
    to_right = [high[:, :128], jnp.where(held, high_field, high[:, 128:])]
    even_y = (lax.axis_index("gy") & 1) == 0
    for part in range(2):
        lanes = slice(part * 128, part * 128 + 128)
        out_s[:, lanes] = jnp.where(even_y, to_right[part], to_left[part])
        out_z[:, lanes] = jnp.where(even_y, to_left[part], to_right[part])


def fold(reads, gains, way):
    moved = roll(reads, -READS, 1)[:, :128]
    gains = gains[:, :128]
    lane = iota(gains.shape, 1)
    product = moved * gains
    for place, k in enumerate(Y_PAIRS):
        if way * PAIRS[k][1] < 0:
            product = jnp.where(block_at(lane, place * NZ), -product, product)
    total = product
    for place in range(1, len(Y_PAIRS)):
        total = total + roll(product, -place * NZ, 1)
    return jnp.where(lane < NZ, total, 0.0)


def laplace(field, depth, inside):
    rows, lanes = field.shape
    total = roll(field, 1, 0) + roll(field, -1, 0)
    total = total + (roll(field, NZ, 1) + roll(field, -NZ, 1))
    total = total + jnp.where(depth > 0, roll(field, 1, 1), 0.0)
    total = total + jnp.where(depth < NZ - 1, roll(field, -1, 1), 0.0)
    result = field - total * (1.0 / 6.0)
    return result if inside is None else jnp.where(inside, result, 0.0)


def tree_sum(parts):
    while len(parts) > 1:
        half = (len(parts) + 1) // 2
        parts = [
            parts[i] + parts[i + half] if i + half < len(parts) else parts[i] for i in range(half)
        ]
    return parts[0]


def sum_all(value):
    rows, lanes = value.shape
    parts = [
        value[r : r + ROWS, c : c + 128] for r in range(0, rows, ROWS) for c in range(0, lanes, 128)
    ]
    folded = tree_sum(parts)
    return jnp.sum(jnp.sum(folded, axis=0, keepdims=True), axis=1, keepdims=True)


def krylov_kernel(wide, own_s, own_z, got_s, got_z, basis, shares):
    rows, columns = wide.shape
    place = lax.axis_index("gy")
    last_place = lax.axis_size("gy") - 1
    even = (place & 1) == 0

    def pick(first, second):
        return jnp.where(even, first[...], second[...])

    to_right = pick(own_s, own_z)
    to_left = pick(own_z, own_s)
    right = pick(got_s, got_z)
    left = pick(got_z, got_s)
    lane = iota((rows, 128), 1)
    field = wide[...]
    low_end = field[:, :128] + fold(left, to_left, -1)
    high_end = field[:, columns - 128 :] + roll(fold(right, to_right, 1), 128 - NZ, 1)
    right_halo = jnp.where(lane < 3 * NZ, roll(right[:, 128:], 128 - EDGE, 1), 0.0)
    right_halo = right_halo + fold(to_right, right, -1)
    left_halo = jnp.where(
        lane >= 128 - 3 * NZ, roll(left[:, 128:], 128 - 3 * NZ - (EDGE - 128), 1), 0.0
    )
    left_halo = left_halo + roll(fold(to_left, left, 1), 128 - NZ, 1)
    field = jnp.concatenate(
        [left_halo, low_end, field[:, 128 : columns - 128], high_end, right_halo], axis=1
    )
    column = iota(field.shape, 1)
    depth = column & (NZ - 1)
    inside = ((column >= 128) | (place > 0)) & ((column < 128 + columns) | (place < last_place))
    first = laplace(field, depth, inside)
    second = laplace(first, depth, inside)
    third = laplace(second, depth, None)
    cores = [v[ROWS : rows - ROWS, 128 : 128 + columns] for v in (field, first, second, third)]
    for power in range(ITERS):
        basis[power] = cores[power]
    row = jnp.zeros((1, 128), jnp.float32)
    lane = iota((1, 128), 1)
    for power in range(2 * ITERS):
        value = sum_all(cores[power // 2] * cores[(power + 1) // 2])
        row = jnp.where(lane == power, value, row)
    shares[...] = jnp.broadcast_to(row, shares.shape)


def times_h(poly):
    out = list(poly) + [0.0]
    for power, entry in enumerate(poly):
        out[power + 1] = out[power + 1] + (6.0 * radius_sq) * entry
    return out


def dot_poly(p, q, moments):
    total = 0.0
    for power in range(len(p) + len(q) - 1):
        terms = [p[i] * q[power - i] for i in range(len(p)) if 0 <= power - i < len(q)]
        total = total + tree_sum(terms) * moments[power]
    return total


def entry_of(poly, power):
    return poly[power] if power < len(poly) else 0.0


def combination(moments):
    upper = 1.0 + 12.0 * radius_sq
    growth = (upper - 1.0) ** 2 / (4.0 * upper) * 1.001
    one = jnp.ones_like(moments[0])
    solved, residual, direction = [], [one], [one]
    norm_now = moments[0]
    for iteration in range(ITERS):
        image = times_h(direction)
        step = norm_now / dot_poly(direction, image, moments)
        step = jnp.clip(step, 1.0 / upper, 1.0)
        solved = [entry_of(solved, k) + step * direction[k] for k in range(len(direction))]
        if iteration < ITERS - 1:
            residual = [entry_of(residual, k) - step * image[k] for k in range(len(image))]
            norm_next = jnp.maximum(dot_poly(residual, residual, moments), 0.0)
            ratio = jnp.clip(norm_next / norm_now, 0.0, growth)
            direction = [
                residual[k] + ratio * entry_of(direction, k) for k in range(len(residual))
            ]
            norm_now = norm_next
    return solved


def combine_kernel(shares, basis, filtered):
    count = shares.shape[0]
    total = tree_sum([shares[r : r + ROWS, :] for r in range(0, count, ROWS)])
    total = jnp.sum(total, axis=0, keepdims=True)
    lane = iota(total.shape, 1)
    moments = [
        jnp.sum(jnp.where(lane == power, total, 0.0), axis=1, keepdims=True)
        for power in range(2 * ITERS)
    ]
    weights = combination(moments)
    result = basis[0] * weights[0]
    for power in range(1, ITERS):
        result = result + basis[power] * weights[power]
    filtered[...] = result


def adjoint_kernel(
    forward, adjoint, design, node_type, got_s, got_z, side_s, side_z, adjoint_new
):
    layers, columns = design.shape
    tiles = layers // ROWS
    shape = (ROWS, columns)
    even = (lax.axis_index("gx") & 1) == 0
    even_y = (lax.axis_index("gy") & 1) == 0
    faces = slice(2 * ROWS, 3 * ROWS)
    above = jnp.where(even, got_s[faces, :], got_z[faces, :])
    below = jnp.where(even, got_z[faces, :], got_s[faces, :])
    column = iota(shape, 1)
    for tile in range(tiles):
        rows = slice(tile * ROWS, tile * ROWS + ROWS)
        wide_rows = slice(tile * ROWS + ROWS, tile * ROWS + 2 * ROWS)
        right = jnp.where(even_y, side_s[wide_rows, :], side_z[wide_rows, :])
        left = jnp.where(even_y, side_z[wide_rows, :], side_s[wide_rows, :])
        density = forward[0, rows, :]
        differences = []
        for k in range(9):
            one, other = forward[2 * k + 1, rows, :], forward[2 * k + 2, rows, :]
            density = density + (one + other)
            differences.append(one - other)
        inverse = 1.0 / density
        velocity = [part * inverse for part in momentum_of(differences)]
        speed_sq = velocity[0] * velocity[0] + velocity[1] * velocity[1]
        speed_sq = speed_sq + velocity[2] * velocity[2]
        kind = node_type[rows, :]
        wall = kind == 1
        source = jnp.where(kind == 2, 1.0, jnp.where(kind == 3, -1.0, 0.0))
        blend = 1.0 - 2.0 * design[rows, :]
        rest = adjoint[0, rows, :]
        zeroth = REST_WEIGHT * rest
        quadratic = None
        vector = [None, None, None]
        kept = []
        for k in range(9):
            reads = []
            for sign in (1, -1):
                step = [sign * c for c in PAIRS[k]]
                member = member_of(k, sign)
                place = X_PAIRS.index(k) if k in X_PAIRS else 0
                read = row_tile(
                    adjoint,
                    member,
                    tile,
                    step[0],
                    above[place : place + 1, :],
                    below[place : place + 1, :],
                )
                if step[1] or step[2]:
                    read = roll(read, -(step[1] * NZ + step[2]), 1)
                if step[1]:
                    start = READS + Y_PAIRS.index(k) * NZ
                    side = right if step[1] > 0 else left
                    target = columns - NZ if step[1] > 0 else 0
                    part = side[:, start // 128 * 128 : start // 128 * 128 + 128]
                    part = roll(part, target - start, 1)
                    border = column >= columns - NZ if step[1] > 0 else column < NZ
                    spread = jnp.concatenate([part] * (columns // 128), axis=1)
                    read = jnp.where(border, spread, read)
                if step[2]:
                    bounce = adjoint[member_of(k, -sign), rows, :]
                    read = jnp.where(leaves_depth(shape, step[2]), bounce, read)
                reads.append(read)
            both = reads[0] + reads[1]
            odd = blend * (reads[0] - reads[1])
            projected = dot_velocity(PAIRS[k], velocity)
            even_part = WEIGHTS[k] * both
            zeroth = zeroth + even_part
            moved = even_part * projected
            square = moved * projected
            quadratic = square if quadratic is None else quadratic + square
            pull = (3.0 * WEIGHTS[k]) * odd + 9.0 * moved
            for axis in range(3):
                if PAIRS[k][axis]:
                    vector[axis] = (
                        signed_sum([(PAIRS[k][axis], pull)])
                        if vector[axis] is None
                        else signed_sum([(1, vector[axis]), (PAIRS[k][axis], pull)])
                    )
            kept.append((reads[0], reads[1], both, odd))
        scaled = relax_rate * zeroth
        base = scaled * (1.0 + 1.5 * speed_sq) - (4.5 * relax_rate) * quadratic + source
        vector = [
            relax_rate * part - (3.0 * scaled) * speed for part, speed in zip(vector, velocity)
        ]
        keep = relax_rate - 1.0
        adjoint_new[0, rows, :] = jnp.where(wall, rest, base - keep * rest)
        for k in range(9):
            one, other, both, odd = kept[k]
            level = base - (0.5 * keep) * both
            slope = dot_velocity(PAIRS[k], vector) - (0.5 * keep) * odd
            adjoint_new[2 * k + 1, rows, :] = jnp.where(wall, other, level + slope)
            adjoint_new[2 * k + 2, rows, :] = jnp.where(wall, one, level - slope)


def run(kernel, outputs, *operands, flops=1_000_000):
    sizes = [jax.ShapeDtypeStruct(shape, jnp.float32) for shape in outputs]
    moved = 4 * sum(a.size for a in operands) + 4 * sum(s.size for s in sizes)
    result = pl.pallas_call(
        kernel,
        out_shape=sizes,
        in_specs=[pl.BlockSpec(memory_space=pltpu.VMEM) for _ in operands],
        out_specs=[pl.BlockSpec(memory_space=pltpu.VMEM) for _ in outputs],
        compiler_params=pltpu.CompilerParams(vmem_limit_bytes=32 * 1024 * 1024),
        cost_estimate=pl.CostEstimate(flops=flops, bytes_accessed=moved, transcendentals=0),
    )(*operands)
    return result


def swap(first, second, axis, closed):
    count = lax.axis_size(axis)
    near = [(i, i ^ 1) for i in range(count)]
    starts = range(1, count if closed else count - 1, 2)
    far = [(i, (i + 1) % count) for i in starts]
    far = far + [(b, a) for a, b in far]
    return lax.ppermute(first, axis, near), lax.ppermute(second, axis, far)


def shards(forward, adjoint, design, node_type):
    members, layers, columns = adjoint.shape
    sites = layers * columns
    devices = lax.axis_size("gx") * lax.axis_size("gy")
    plane = (layers, columns)
    face = (3 * ROWS, columns)
    side = (layers + 2 * ROWS, 256)
    partial, edges, own_s, own_z = run(
        collide_kernel, [plane, (layers, 512), face, face], forward, adjoint, node_type,
        flops=150 * sites,
    )
    got_s, got_z = swap(own_s, own_z, "gx", True)
    wide, out_s, out_z = run(
        faces_kernel,
        [(layers + 2 * ROWS, columns), side, side],
        partial, edges, own_s, own_z, got_s, got_z,
    )
    side_s, side_z = swap(out_s, out_z, "gy", False)
    basis, shares = run(
        krylov_kernel, [(ITERS,) + plane, (devices, 128)], wide, out_s, out_z, side_s, side_z,
        flops=60 * sites,
    )
    spread = lax.all_to_all(shares.reshape(devices, 1, 128), ("gx", "gy"), 0, 0)
    (adjoint_new,) = run(
        adjoint_kernel,
        [adjoint.shape],
        forward, adjoint, design, node_type, got_s, got_z, side_s, side_z,
        flops=400 * sites,
    )
    (filtered,) = run(combine_kernel, [plane], spread.reshape(devices, 128), basis)
    return (adjoint_new, filtered)


def solution(mesh):
    placed = (P(None, "gx", "gy"), P(None, "gx", "gy"), P("gx", "gy"), P("gx", "gy"))
    return jax.shard_map(
        shards,
        mesh=mesh,
        in_specs=placed,
        out_specs=(P(None, "gx", "gy"), P("gx", "gy")),
        check_vma=False,
    )
```

```python
import jax
import jax.numpy as jnp
from jax import lax
from jax.experimental import pallas as pl
from jax.experimental.pallas import tpu as pltpu
from jax.sharding import PartitionSpec as P

NZ = 16
ITERS = 3
PAIRS = (
    (1, 0, 0),
    (0, 1, 0),
    (0, 0, 1),
    (1, 1, 0),
    (1, -1, 0),
    (1, 0, 1),
    (1, 0, -1),
    (0, 1, 1),
    (0, 1, -1),
)
WEIGHTS = (1.0 / 18.0,) * 3 + (1.0 / 36.0,) * 6
REST_WEIGHT = 1.0 / 3.0
X_PAIRS = (0, 3, 4, 5, 6)
Y_PAIRS = (1, 3, 4, 7, 8)
relax_rate = 1.25
radius_sq = 4.0
ROWS = 8
READS = 80
EDGE = 160


def iota(shape, axis):
    return lax.broadcasted_iota(jnp.int32, shape, axis)


def roll(value, shift, axis):
    shift = shift % value.shape[axis]
    return value if shift == 0 else pltpu.roll(value, shift, axis)


def signed_sum(terms):
    total = None
    for sign, value in terms:
        if total is None:
            total = value if sign > 0 else -value
        else:
            total = total + value if sign > 0 else total - value
    return total


def dot_velocity(velocity, vector):
    return signed_sum([(c, v) for c, v in zip(velocity, vector) if c != 0])


def momentum_of(differences):
    return [
        signed_sum([(PAIRS[k][axis], differences[k]) for k in range(9) if PAIRS[k][axis] != 0])
        for axis in range(3)
    ]


def member_of(k, sign):
    return 2 * k + 1 if sign > 0 else 2 * k + 2


def row_tile(ref, member, tile, step, above=None, below=None):
    start = tile * ROWS
    layers = ref.shape[1]
    if step == 0:
        return ref[member, start : start + ROWS, :]
    if 0 <= start + step and start + step + ROWS <= layers:
        return ref[member, start + step : start + step + ROWS, :]
    value = ref[member, start : start + ROWS, :]
    row = iota(value.shape, 0)
    if step > 0:
        return jnp.where(row < ROWS - 1, roll(value, ROWS - 1, 0), 0.0 if above is None else above)
    return jnp.where(row > 0, roll(value, 1, 0), 0.0 if below is None else below)


def slide(value, step_y, step_z):
    columns = value.shape[1]
    if step_y == 0 and step_z == 0:
        return value
    moved = roll(value, -(step_y * NZ + step_z), 1)
    column = iota(value.shape, 1)
    keep = None
    if step_y != 0:
        keep = column < columns - NZ if step_y > 0 else column >= NZ
    if step_z != 0:
        depth = column & (NZ - 1)
        inner = depth < NZ - 1 if step_z > 0 else depth > 0
        keep = inner if keep is None else keep & inner
    return jnp.where(keep, moved, 0.0)


def leaves_depth(shape, step_z):
    depth = iota(shape, 1) & (NZ - 1)
    return depth == NZ - 1 if step_z > 0 else depth == 0


def block_at(lane, start):
    return (lane >= start) & (lane < start + NZ)


def pack_edge(gains, populations, high):
    origin = 0 if not high else 128 - NZ
    shape = (ROWS, 128)
    lane = iota(shape, 1)
    halves = [jnp.zeros(shape, jnp.float32), jnp.zeros(shape, jnp.float32)]
    for place, value in enumerate(list(gains) + list(populations)):
        columns = value.shape[1]
        part = value[:, :128] if not high else value[:, columns - 128 :]
        half, start = divmod(place * NZ, 128)
        halves[half] = jnp.where(block_at(lane, start), roll(part, start - origin, 1), halves[half])
    return jnp.concatenate(halves, axis=1)


def gains_of(forward, kinds):
    differences = [forward(2 * k + 1) - forward(2 * k + 2) for k in range(9)]
    momentum = momentum_of(differences)
    fluid = kinds != 1
    gains = []
    for k in range(9):
        gain = (relax_rate - 1.0) * differences[k]
        gain = gain - (6.0 * relax_rate * WEIGHTS[k]) * dot_velocity(PAIRS[k], momentum)
        gains.append(jnp.where(fluid, gain, 0.0))
    return gains


def inner_sensitivity(gains, rows_of):
    total = None
    for k in range(9):
        reads = []
        for sign in (1, -1):
            step = [sign * c for c in PAIRS[k]]
            read = slide(rows_of(member_of(k, sign), step[0]), step[1], step[2])
            if step[2] != 0:
                bounce = rows_of(member_of(k, -sign), 0)
                read = jnp.where(leaves_depth(read.shape, step[2]), bounce, read)
            reads.append(read)
        term = (reads[0] - reads[1]) * gains[k]
        total = term if total is None else total + term
    return total


def pack_edges(gains, adjoint):
    packed = []
    for high in (False, True):
        way = -1 if high else 1
        populations = [adjoint(member_of(k, way * PAIRS[k][1])) for k in Y_PAIRS]
        packed.append(pack_edge([gains[k] for k in Y_PAIRS], populations, high))
    return jnp.concatenate(packed, axis=1)


def border_kernel(forward, adjoint, node_type, out_s, out_z, moving, carried, kinds, sems):
    layers, columns = node_type.shape
    copies = []
    for place, start in enumerate((0, layers - ROWS)):
        rows = pl.ds(start, ROWS)
        copies.append(pltpu.make_async_copy(node_type.at[rows, :], kinds.at[place], sems.at[place]))
    for source, target in ((forward, moving), (adjoint, carried)):
        for place, start in enumerate((0, layers - ROWS)):
            part = source.at[:, pl.ds(start, ROWS), :]
            copies.append(pltpu.make_async_copy(part, target.at[place], sems.at[len(copies)]))
    for copy in copies:
        copy.start()
    row = iota((ROWS, columns), 0)
    for place in range(2):
        copies[place].wait()
    gains = []
    for place in range(2):
        copies[2 + place].wait()
        gains.append(gains_of(lambda member: moving[place, member], kinds[place]))
    packs = []
    for place in range(2):
        copies[4 + place].wait()

        def rows_of(member, step):
            value = carried[place, member]
            if step == 0:
                return value
            if step > 0:
                return jnp.where(row < ROWS - 1, roll(value, ROWS - 1, 0), 0.0)
            return jnp.where(row > 0, roll(value, 1, 0), 0.0)

        top = inner_sensitivity(gains[place], rows_of)
        edge = pack_edges(gains[place], lambda member: carried[place, member])
        faces = jnp.zeros((ROWS, columns), jnp.float32)
        last = place * (ROWS - 1)
        base = 3 * (1 - place)
        for index, k in enumerate(X_PAIRS):
            member = member_of(k, 1 - 2 * place)
            top = jnp.where(row == base + index, gains[place][k][last : last + 1, :], top)
            faces = jnp.where(row == index, carried[place, member, last : last + 1, :], faces)
        packs.append((top, edge, faces))
    even = (lax.axis_index("gx") & 1) == 0
    for part in range(3):
        rows = slice(part * ROWS, part * ROWS + ROWS)
        out_s[rows, :] = jnp.where(even, packs[1][part], packs[0][part])
        out_z[rows, :] = jnp.where(even, packs[0][part], packs[1][part])


def fetch_tiles(sources, targets, sems):
    tiles = sources[-1].shape[-2] // ROWS
    groups = []
    for tile in range(tiles):
        rows = pl.ds(tile * ROWS, ROWS)
        group = []
        for index, (source, target) in enumerate(zip(sources, targets)):
            at = (slice(None), rows) if len(source.shape) == 3 else (rows,)
            group.append(
                pltpu.make_async_copy(source.at[at], target.at[at], sems.at[tile, index])
            )
        for copy in group:
            copy.start()
        groups.append(group)
    return groups


def take(groups, tile):
    for ready in ((0, 1) if tile == 0 else (tile + 1,)):
        if ready < len(groups):
            for copy in groups[ready]:
                copy.wait()


def collide_kernel(forward, adjoint, node_type, partial, edges, moving, carried, kinds, sems):
    layers, columns = partial.shape
    groups = fetch_tiles((forward, adjoint, node_type), (moving, carried, kinds), sems)
    for tile in range(layers // ROWS):
        rows = slice(tile * ROWS, tile * ROWS + ROWS)
        take(groups, tile)
        gains = gains_of(lambda member: moving[member, rows, :], kinds[rows, :])
        partial[rows, :] = inner_sensitivity(
            gains, lambda member, step: row_tile(carried, member, tile, step)
        )
        edges[rows, :] = pack_edges(gains, lambda member: carried[member, rows, :])


def face_reads(faces, sign):
    row = iota(faces.shape, 0)
    result = faces
    for place, k in enumerate(X_PAIRS):
        step_y, step_z = sign * PAIRS[k][1], sign * PAIRS[k][2]
        if step_y or step_z:
            result = jnp.where(row == place, slide(faces, step_y, step_z), result)
    return result


def outgoing(edge, way):
    lane = iota(edge.shape, 1)
    result = edge
    for place, k in enumerate(Y_PAIRS):
        sign = way * PAIRS[k][1]
        step_x, step_z = sign * PAIRS[k][0], sign * PAIRS[k][2]
        start = READS + place * NZ
        if step_x:
            result = jnp.where(block_at(lane, start), roll(edge, -step_x, 0), result)
        if step_z:
            moved = jnp.where(leaves_depth(edge.shape, step_z), 0.0, roll(edge, -step_z, 1))
            result = jnp.where(block_at(lane, start), moved, result)
    return result


def faces_kernel(partial, edges, own_s, own_z, got_s, got_z, wide, out_s, out_z):
    layers, columns = partial.shape
    even = (lax.axis_index("gx") & 1) == 0

    def pick(first, second, part):
        rows = slice(part * ROWS, part * ROWS + ROWS)
        return jnp.where(even, first[rows, :], second[rows, :])

    up = [pick(own_s, own_z, part) for part in range(3)]
    down = [pick(own_z, own_s, part) for part in range(3)]
    above = [pick(got_s, got_z, part) for part in range(3)]
    below = [pick(got_z, got_s, part) for part in range(3)]
    row = iota((ROWS, columns), 0)

    def completion(reads, gains):
        return jnp.sum(reads * gains, axis=0, keepdims=True)

    own_last = completion(face_reads(above[2], 1), up[0])
    own_first = completion(face_reads(below[2], -1), roll(down[0], -3, 0))
    far_first = completion(face_reads(up[2], -1), roll(above[0], -3, 0))
    far_last = completion(face_reads(down[2], 1), below[0])
    last = ROWS - 1
    wide[:ROWS, :] = below[0] + jnp.where(row == last, far_last, 0.0)
    wide[ROWS : 2 * ROWS, :] = partial[:ROWS, :] - jnp.where(row == 0, own_first, 0.0)
    wide[2 * ROWS : layers, :] = partial[ROWS : layers - ROWS, :]
    wide[layers : layers + ROWS, :] = partial[layers - ROWS :, :] + jnp.where(
        row == last, own_last, 0.0
    )
    wide[layers + ROWS :, :] = above[0] - jnp.where(row == 0, far_first, 0.0)

    edge = jnp.concatenate([below[1], edges[...], above[1]], axis=0)
    half = edge.shape[1] // 2
    low = outgoing(edge[:, :half], 1)
    high = outgoing(edge[:, half:], -1)
    low_field = roll(wide[:, :128], EDGE - 128, 1)
    high_field = roll(wide[:, columns - 128 :], EDGE - 128 - (128 - 3 * NZ), 1)
    lane = iota(low_field.shape, 1)
    held = (lane >= EDGE - 128) & (lane < EDGE - 128 + 3 * NZ)
    to_left = [low[:, :128], jnp.where(held, low_field, low[:, 128:])]
    to_right = [high[:, :128], jnp.where(held, high_field, high[:, 128:])]
    even_y = (lax.axis_index("gy") & 1) == 0
    for part in range(2):
        lanes = slice(part * 128, part * 128 + 128)
        out_s[:, lanes] = jnp.where(even_y, to_right[part], to_left[part])
        out_z[:, lanes] = jnp.where(even_y, to_left[part], to_right[part])


def fold(reads, gains, way):
    moved = roll(reads, -READS, 1)[:, :128]
    gains = gains[:, :128]
    lane = iota(gains.shape, 1)
    product = moved * gains
    for place, k in enumerate(Y_PAIRS):
        if way * PAIRS[k][1] < 0:
            product = jnp.where(block_at(lane, place * NZ), -product, product)
    total = product
    for place in range(1, len(Y_PAIRS)):
        total = total + roll(product, -place * NZ, 1)
    return jnp.where(lane < NZ, total, 0.0)


def laplace(field, depth, inside):
    rows, lanes = field.shape
    total = roll(field, 1, 0) + roll(field, -1, 0)
    total = total + (roll(field, NZ, 1) + roll(field, -NZ, 1))
    total = total + jnp.where(depth > 0, roll(field, 1, 1), 0.0)
    total = total + jnp.where(depth < NZ - 1, roll(field, -1, 1), 0.0)
    result = field - total * (1.0 / 6.0)
    return result if inside is None else jnp.where(inside, result, 0.0)


def tree_sum(parts):
    while len(parts) > 1:
        half = (len(parts) + 1) // 2
        parts = [
            parts[i] + parts[i + half] if i + half < len(parts) else parts[i] for i in range(half)
        ]
    return parts[0]


def sum_all(value):
    rows, lanes = value.shape
    parts = [
        value[r : r + ROWS, c : c + 128] for r in range(0, rows, ROWS) for c in range(0, lanes, 128)
    ]
    folded = tree_sum(parts)
    return jnp.sum(jnp.sum(folded, axis=0, keepdims=True), axis=1, keepdims=True)


def krylov_kernel(wide, own_s, own_z, got_s, got_z, basis, shares):
    rows, columns = wide.shape
    place = lax.axis_index("gy")
    last_place = lax.axis_size("gy") - 1
    even = (place & 1) == 0

    def pick(first, second):
        return jnp.where(even, first[...], second[...])

    to_right = pick(own_s, own_z)
    to_left = pick(own_z, own_s)
    right = pick(got_s, got_z)
    left = pick(got_z, got_s)
    lane = iota((rows, 128), 1)
    field = wide[...]
    low_end = field[:, :128] + fold(left, to_left, -1)
    high_end = field[:, columns - 128 :] + roll(fold(right, to_right, 1), 128 - NZ, 1)
    right_halo = jnp.where(lane < 3 * NZ, roll(right[:, 128:], 128 - EDGE, 1), 0.0)
    right_halo = right_halo + fold(to_right, right, -1)
    left_halo = jnp.where(
        lane >= 128 - 3 * NZ, roll(left[:, 128:], 128 - 3 * NZ - (EDGE - 128), 1), 0.0
    )
    left_halo = left_halo + roll(fold(to_left, left, 1), 128 - NZ, 1)
    field = jnp.concatenate(
        [left_halo, low_end, field[:, 128 : columns - 128], high_end, right_halo], axis=1
    )
    column = iota(field.shape, 1)
    depth = column & (NZ - 1)
    inside = ((column >= 128) | (place > 0)) & ((column < 128 + columns) | (place < last_place))
    first = laplace(field, depth, inside)
    second = laplace(first, depth, inside)
    third = laplace(second, depth, None)
    cores = [v[ROWS : rows - ROWS, 128 : 128 + columns] for v in (field, first, second, third)]
    for power in range(ITERS):
        basis[power] = cores[power]
    row = jnp.zeros((1, 128), jnp.float32)
    lane = iota((1, 128), 1)
    for power in range(2 * ITERS):
        value = sum_all(cores[power // 2] * cores[(power + 1) // 2])
        row = jnp.where(lane == power, value, row)
    shares[...] = jnp.broadcast_to(row, shares.shape)


def times_h(poly):
    out = list(poly) + [0.0]
    for power, entry in enumerate(poly):
        out[power + 1] = out[power + 1] + (6.0 * radius_sq) * entry
    return out


def dot_poly(p, q, moments):
    total = 0.0
    for power in range(len(p) + len(q) - 1):
        terms = [p[i] * q[power - i] for i in range(len(p)) if 0 <= power - i < len(q)]
        total = total + tree_sum(terms) * moments[power]
    return total


def entry_of(poly, power):
    return poly[power] if power < len(poly) else 0.0


def combination(moments):
    upper = 1.0 + 12.0 * radius_sq
    growth = (upper - 1.0) ** 2 / (4.0 * upper) * 1.001
    one = jnp.ones_like(moments[0])
    solved, residual, direction = [], [one], [one]
    norm_now = moments[0]
    for iteration in range(ITERS):
        image = times_h(direction)
        step = norm_now / dot_poly(direction, image, moments)
        step = jnp.clip(step, 1.0 / upper, 1.0)
        solved = [entry_of(solved, k) + step * direction[k] for k in range(len(direction))]
        if iteration < ITERS - 1:
            residual = [entry_of(residual, k) - step * image[k] for k in range(len(image))]
            norm_next = jnp.maximum(dot_poly(residual, residual, moments), 0.0)
            ratio = jnp.clip(norm_next / norm_now, 0.0, growth)
            direction = [
                residual[k] + ratio * entry_of(direction, k) for k in range(len(residual))
            ]
            norm_now = norm_next
    return solved


def combine_kernel(shares, basis, filtered):
    count = shares.shape[0]
    total = tree_sum([shares[r : r + ROWS, :] for r in range(0, count, ROWS)])
    total = jnp.sum(total, axis=0, keepdims=True)
    lane = iota(total.shape, 1)
    moments = [
        jnp.sum(jnp.where(lane == power, total, 0.0), axis=1, keepdims=True)
        for power in range(2 * ITERS)
    ]
    weights = combination(moments)
    result = basis[0] * weights[0]
    for power in range(1, ITERS):
        result = result + basis[power] * weights[power]
    filtered[...] = result


def adjoint_kernel(
    forward_far,
    adjoint_far,
    design_far,
    node_far,
    got_s,
    got_z,
    side_s,
    side_z,
    result,
    forward,
    adjoint,
    design,
    node_type,
    adjoint_new,
    sems,
    out_sems,
):
    layers, columns = design.shape
    groups = fetch_tiles(
        (forward_far, adjoint_far, design_far, node_far),
        (forward, adjoint, design, node_type),
        sems,
    )
    sent = []
    tiles = layers // ROWS
    shape = (ROWS, columns)
    even = (lax.axis_index("gx") & 1) == 0
    even_y = (lax.axis_index("gy") & 1) == 0
    faces = slice(2 * ROWS, 3 * ROWS)
    above = jnp.where(even, got_s[faces, :], got_z[faces, :])
    below = jnp.where(even, got_z[faces, :], got_s[faces, :])
    column = iota(shape, 1)
    for tile in range(tiles):
        rows = slice(tile * ROWS, tile * ROWS + ROWS)
        wide_rows = slice(tile * ROWS + ROWS, tile * ROWS + 2 * ROWS)
        right = jnp.where(even_y, side_s[wide_rows, :], side_z[wide_rows, :])
        left = jnp.where(even_y, side_z[wide_rows, :], side_s[wide_rows, :])
        take(groups, tile)
        density = forward[0, rows, :]
        differences = []
        for k in range(9):
            one, other = forward[2 * k + 1, rows, :], forward[2 * k + 2, rows, :]
            density = density + (one + other)
            differences.append(one - other)
        inverse = 1.0 / density
        velocity = [part * inverse for part in momentum_of(differences)]
        speed_sq = velocity[0] * velocity[0] + velocity[1] * velocity[1]
        speed_sq = speed_sq + velocity[2] * velocity[2]
        kind = node_type[rows, :]
        wall = kind == 1
        source = jnp.where(kind == 2, 1.0, jnp.where(kind == 3, -1.0, 0.0))
        blend = 1.0 - 2.0 * design[rows, :]
        rest = adjoint[0, rows, :]
        zeroth = REST_WEIGHT * rest
        quadratic = None
        vector = [None, None, None]
        kept = []
        for k in range(9):
            reads = []
            for sign in (1, -1):
                step = [sign * c for c in PAIRS[k]]
                member = member_of(k, sign)
                place = X_PAIRS.index(k) if k in X_PAIRS else 0
                read = row_tile(
                    adjoint,
                    member,
                    tile,
                    step[0],
                    above[place : place + 1, :],
                    below[place : place + 1, :],
                )
                if step[1] or step[2]:
                    read = roll(read, -(step[1] * NZ + step[2]), 1)
                if step[1]:
                    start = READS + Y_PAIRS.index(k) * NZ
                    side = right if step[1] > 0 else left
                    target = columns - NZ if step[1] > 0 else 0
                    part = side[:, start // 128 * 128 : start // 128 * 128 + 128]
                    part = roll(part, target - start, 1)
                    border = column >= columns - NZ if step[1] > 0 else column < NZ
                    spread = jnp.concatenate([part] * (columns // 128), axis=1)
                    read = jnp.where(border, spread, read)
                if step[2]:
                    bounce = adjoint[member_of(k, -sign), rows, :]
                    read = jnp.where(leaves_depth(shape, step[2]), bounce, read)
                reads.append(read)
            both = reads[0] + reads[1]
            odd = blend * (reads[0] - reads[1])
            projected = dot_velocity(PAIRS[k], velocity)
            even_part = WEIGHTS[k] * both
            zeroth = zeroth + even_part
            moved = even_part * projected
            square = moved * projected
            quadratic = square if quadratic is None else quadratic + square
            pull = (3.0 * WEIGHTS[k]) * odd + 9.0 * moved
            for axis in range(3):
                if PAIRS[k][axis]:
                    vector[axis] = (
                        signed_sum([(PAIRS[k][axis], pull)])
                        if vector[axis] is None
                        else signed_sum([(1, vector[axis]), (PAIRS[k][axis], pull)])
                    )
            kept.append((reads[0], reads[1], both, odd))
        scaled = relax_rate * zeroth
        base = scaled * (1.0 + 1.5 * speed_sq) - (4.5 * relax_rate) * quadratic + source
        vector = [
            relax_rate * part - (3.0 * scaled) * speed for part, speed in zip(vector, velocity)
        ]
        keep = relax_rate - 1.0
        adjoint_new[0, rows, :] = jnp.where(wall, rest, base - keep * rest)
        for k in range(9):
            one, other, both, odd = kept[k]
            level = base - (0.5 * keep) * both
            slope = dot_velocity(PAIRS[k], vector) - (0.5 * keep) * odd
            adjoint_new[2 * k + 1, rows, :] = jnp.where(wall, other, level + slope)
            adjoint_new[2 * k + 2, rows, :] = jnp.where(wall, one, level - slope)
        part = pl.ds(tile * ROWS, ROWS)
        sent.append(
            pltpu.make_async_copy(
                adjoint_new.at[:, part, :], result.at[:, part, :], out_sems.at[tile]
            )
        )
        sent[-1].start()
    for copy in sent:
        copy.wait()


def run(kernel, outputs, *operands, flops, far=0, far_out=False, scratch=(), vmem=32):
    sizes = [jax.ShapeDtypeStruct(shape, jnp.float32) for shape in outputs]
    moved = 4 * sum(a.size for a in operands) + 4 * sum(s.size for s in sizes)
    operands = [
        pltpu.with_memory_space_constraint(a, pltpu.HBM) if i < far else a
        for i, a in enumerate(operands)
    ]
    near = pl.BlockSpec(memory_space=pltpu.VMEM)
    away = pl.BlockSpec(memory_space=pl.ANY)
    return pl.pallas_call(
        kernel,
        out_shape=sizes,
        in_specs=[away if i < far else near for i in range(len(operands))],
        out_specs=[away if far_out else near for _ in outputs],
        scratch_shapes=list(scratch),
        compiler_params=pltpu.CompilerParams(vmem_limit_bytes=vmem * 1024 * 1024),
        cost_estimate=pl.CostEstimate(flops=flops, bytes_accessed=moved, transcendentals=0),
    )(*operands)


def swap(first, second, axis, closed):
    count = lax.axis_size(axis)
    near = [(i, i ^ 1) for i in range(count)]
    starts = range(1, count if closed else count - 1, 2)
    far = [(i, (i + 1) % count) for i in starts]
    far = far + [(b, a) for a, b in far]
    return lax.ppermute(first, axis, near), lax.ppermute(second, axis, far)


def shards(forward, adjoint, design, node_type):
    members, layers, columns = adjoint.shape
    sites = layers * columns
    devices = lax.axis_size("gx") * lax.axis_size("gy")
    plane = (layers, columns)
    face = (3 * ROWS, columns)
    side = (layers + 2 * ROWS, 256)
    tiles = layers // ROWS
    field = pltpu.VMEM((members,) + plane, jnp.float32)
    ends = pltpu.VMEM((2, members, ROWS, columns), jnp.float32)
    own_s, own_z = run(
        border_kernel,
        [face, face],
        forward,
        adjoint,
        node_type,
        far=3,
        scratch=[
            ends,
            ends,
            pltpu.VMEM((2, ROWS, columns), jnp.int32),
            pltpu.SemaphoreType.DMA((6,)),
        ],
        flops=80 * sites,
    )
    got_s, got_z = swap(own_s, own_z, "gx", True)
    partial, edges = run(
        collide_kernel,
        [plane, (layers, 512)],
        forward,
        adjoint,
        node_type,
        far=3,
        scratch=[
            field,
            field,
            pltpu.VMEM(plane, jnp.int32),
            pltpu.SemaphoreType.DMA((tiles, 3)),
        ],
        flops=150 * sites,
    )
    wide, out_s, out_z = run(
        faces_kernel,
        [(layers + 2 * ROWS, columns), side, side],
        partial,
        edges,
        own_s,
        own_z,
        got_s,
        got_z,
        flops=10 * sites,
    )
    side_s, side_z = swap(out_s, out_z, "gy", False)
    basis, shares = run(
        krylov_kernel,
        [(ITERS,) + plane, (ROWS, 128)],
        wide,
        out_s,
        out_z,
        side_s,
        side_z,
        flops=60 * sites,
    )
    copies = jnp.broadcast_to(shares[None, :1], (devices, 1, 128))
    spread = lax.all_to_all(copies, ("gx", "gy"), 0, 0)
    (adjoint_new,) = run(
        adjoint_kernel,
        [adjoint.shape],
        forward,
        adjoint,
        design,
        node_type,
        got_s,
        got_z,
        side_s,
        side_z,
        far=4,
        far_out=True,
        scratch=[
            field,
            field,
            pltpu.VMEM(plane, jnp.float32),
            pltpu.VMEM(plane, jnp.int32),
            field,
            pltpu.SemaphoreType.DMA((tiles, 4)),
            pltpu.SemaphoreType.DMA((tiles,)),
        ],
        flops=400 * sites,
    )
    (filtered,) = run(
        combine_kernel, [plane], spread.reshape(devices, 128), basis, flops=10 * sites
    )
    return (adjoint_new, filtered)


def solution(mesh):
    placed = (P(None, "gx", "gy"), P(None, "gx", "gy"), P("gx", "gy"), P("gx", "gy"))
    return jax.shard_map(
        shards,
        mesh=mesh,
        in_specs=placed,
        out_specs=(P(None, "gx", "gy"), P("gx", "gy")),
        check_vma=False,
    )
```

```python
import functools

import jax
import jax.numpy as jnp
from jax import lax
from jax.experimental import pallas as pl
from jax.experimental.pallas import tpu as pltpu
from jax.sharding import PartitionSpec as P

NZ = 16
ITERS = 3
PAIRS = (
    (1, 0, 0),
    (0, 1, 0),
    (0, 0, 1),
    (1, 1, 0),
    (1, -1, 0),
    (1, 0, 1),
    (1, 0, -1),
    (0, 1, 1),
    (0, 1, -1),
)
WEIGHTS = (1.0 / 18.0,) * 3 + (1.0 / 36.0,) * 6
REST_WEIGHT = 1.0 / 3.0
X_PAIRS = (0, 3, 4, 5, 6)
Y_PAIRS = (1, 3, 4, 7, 8)
relax_rate = 1.25
radius_sq = 4.0
ROWS = 8
READS = 80
EDGE = 160


def iota(shape, axis):
    return lax.broadcasted_iota(jnp.int32, shape, axis)


def roll(value, shift, axis):
    shift = shift % value.shape[axis]
    return value if shift == 0 else pltpu.roll(value, shift, axis)


def signed_sum(terms):
    total = None
    for sign, value in terms:
        if total is None:
            total = value if sign > 0 else -value
        else:
            total = total + value if sign > 0 else total - value
    return total


def dot_velocity(velocity, vector):
    return signed_sum([(c, v) for c, v in zip(velocity, vector) if c != 0])


def momentum_of(differences):
    return [
        signed_sum([(PAIRS[k][axis], differences[k]) for k in range(9) if PAIRS[k][axis] != 0])
        for axis in range(3)
    ]


def member_of(k, sign):
    return 2 * k + 1 if sign > 0 else 2 * k + 2


def row_tile(ref, member, tile, step, above=None, below=None):
    start = tile * ROWS
    layers = ref.shape[1]
    if step == 0:
        return ref[member, start : start + ROWS, :]
    if 0 <= start + step and start + step + ROWS <= layers:
        return ref[member, start + step : start + step + ROWS, :]
    value = ref[member, start : start + ROWS, :]
    row = iota(value.shape, 0)
    if step > 0:
        return jnp.where(row < ROWS - 1, roll(value, ROWS - 1, 0), 0.0 if above is None else above)
    return jnp.where(row > 0, roll(value, 1, 0), 0.0 if below is None else below)


def slide(value, step_y, step_z):
    columns = value.shape[1]
    if step_y == 0 and step_z == 0:
        return value
    moved = roll(value, -(step_y * NZ + step_z), 1)
    column = iota(value.shape, 1)
    keep = None
    if step_y != 0:
        keep = column < columns - NZ if step_y > 0 else column >= NZ
    if step_z != 0:
        depth = column & (NZ - 1)
        inner = depth < NZ - 1 if step_z > 0 else depth > 0
        keep = inner if keep is None else keep & inner
    return jnp.where(keep, moved, 0.0)


def leaves_depth(shape, step_z):
    depth = iota(shape, 1) & (NZ - 1)
    return depth == NZ - 1 if step_z > 0 else depth == 0


def block_at(lane, start):
    return (lane >= start) & (lane < start + NZ)


def pack_edge(gains, populations, high):
    origin = 0 if not high else 128 - NZ
    shape = (ROWS, 128)
    lane = iota(shape, 1)
    halves = [jnp.zeros(shape, jnp.float32), jnp.zeros(shape, jnp.float32)]
    for place, value in enumerate(list(gains) + list(populations)):
        columns = value.shape[1]
        part = value[:, :128] if not high else value[:, columns - 128 :]
        half, start = divmod(place * NZ, 128)
        halves[half] = jnp.where(block_at(lane, start), roll(part, start - origin, 1), halves[half])
    return jnp.concatenate(halves, axis=1)


def gains_of(forward, kinds):
    differences = [forward(2 * k + 1) - forward(2 * k + 2) for k in range(9)]
    momentum = momentum_of(differences)
    fluid = kinds != 1
    gains = []
    for k in range(9):
        gain = (relax_rate - 1.0) * differences[k]
        gain = gain - (6.0 * relax_rate * WEIGHTS[k]) * dot_velocity(PAIRS[k], momentum)
        gains.append(jnp.where(fluid, gain, 0.0))
    return gains


def inner_sensitivity(gains, rows_of):
    total = None
    for k in range(9):
        reads = []
        for sign in (1, -1):
            step = [sign * c for c in PAIRS[k]]
            read = slide(rows_of(member_of(k, sign), step[0]), step[1], step[2])
            if step[2] != 0:
                bounce = rows_of(member_of(k, -sign), 0)
                read = jnp.where(leaves_depth(read.shape, step[2]), bounce, read)
            reads.append(read)
        term = (reads[0] - reads[1]) * gains[k]
        total = term if total is None else total + term
    return total


def pack_edges(gains, adjoint):
    packed = []
    for high in (False, True):
        way = -1 if high else 1
        populations = [adjoint(member_of(k, way * PAIRS[k][1])) for k in Y_PAIRS]
        packed.append(pack_edge([gains[k] for k in Y_PAIRS], populations, high))
    return jnp.concatenate(packed, axis=1)


def border_kernel(near, forward, adjoint, node_type, out, moving, carried, kinds, sems):
    layers, columns = node_type.shape
    odd = lax.axis_index("gx") & 1
    up = 1 - odd if near else odd
    rows = pl.ds(pl.multiple_of(up * (layers - ROWS), ROWS), ROWS)
    half = forward.shape[0] // 2
    copies = [pltpu.make_async_copy(node_type.at[rows, :], kinds, sems.at[0])]
    for source, target in ((forward, moving), (adjoint, carried)):
        for members in (pl.ds(0, half), pl.ds(half, forward.shape[0] - half)):
            copies.append(
                pltpu.make_async_copy(
                    source.at[members, rows, :], target.at[members], sems.at[len(copies)]
                )
            )
    for copy in copies:
        copy.start()
    for copy in copies[:3]:
        copy.wait()
    gains = gains_of(lambda member: moving[member], kinds[...])
    for copy in copies[3:]:
        copy.wait()
    row = iota((ROWS, columns), 0)

    def rows_of(member, step):
        value = carried[member]
        if step == 0:
            return value
        if step > 0:
            return jnp.where(row < ROWS - 1, roll(value, ROWS - 1, 0), 0.0)
        return jnp.where(row > 0, roll(value, 1, 0), 0.0)

    def border(value):
        return jnp.where(up == 1, value[ROWS - 1 :, :], value[:1, :])

    top = inner_sensitivity(gains, rows_of)
    faces = jnp.zeros((ROWS, columns), jnp.float32)
    base = 3 * (1 - up)
    for index, k in enumerate(X_PAIRS):
        top = jnp.where(row == base + index, border(gains[k]), top)
        outward = jnp.where(
            up == 1, carried[2 * k + 2, ROWS - 1 :, :], carried[2 * k + 1, :1, :]
        )
        faces = jnp.where(row == index, outward, faces)
    out[:ROWS, :] = top
    out[ROWS : 2 * ROWS, :] = pack_edges(gains, lambda member: carried[member])
    out[2 * ROWS :, :] = faces


def fetch_tiles(sources, targets, sems):
    tiles = sources[-1].shape[-2] // ROWS
    groups = []
    for tile in range(tiles):
        rows = pl.ds(tile * ROWS, ROWS)
        group = []
        for index, (source, target) in enumerate(zip(sources, targets)):
            at = (slice(None), rows) if len(source.shape) == 3 else (rows,)
            group.append(
                pltpu.make_async_copy(source.at[at], target.at[at], sems.at[tile, index])
            )
        for copy in group:
            copy.start()
        groups.append(group)
    return groups


def take(groups, tile):
    for ready in ((0, 1) if tile == 0 else (tile + 1,)):
        if ready < len(groups):
            for copy in groups[ready]:
                copy.wait()


def collide_kernel(forward, adjoint, node_type, partial, edges, moving, carried, kinds, sems):
    layers, columns = partial.shape
    groups = fetch_tiles((forward, adjoint, node_type), (moving, carried, kinds), sems)
    for tile in range(layers // ROWS):
        rows = slice(tile * ROWS, tile * ROWS + ROWS)
        take(groups, tile)
        gains = gains_of(lambda member: moving[member, rows, :], kinds[rows, :])
        partial[rows, :] = inner_sensitivity(
            gains, lambda member, step: row_tile(carried, member, tile, step)
        )
        edges[rows, :] = pack_edges(gains, lambda member: carried[member, rows, :])


def face_reads(faces, sign):
    row = iota(faces.shape, 0)
    result = faces
    for place, k in enumerate(X_PAIRS):
        step_y, step_z = sign * PAIRS[k][1], sign * PAIRS[k][2]
        if step_y or step_z:
            result = jnp.where(row == place, slide(faces, step_y, step_z), result)
    return result


def outgoing(edge, way):
    lane = iota(edge.shape, 1)
    result = edge
    for place, k in enumerate(Y_PAIRS):
        sign = way * PAIRS[k][1]
        step_x, step_z = sign * PAIRS[k][0], sign * PAIRS[k][2]
        start = READS + place * NZ
        if step_x:
            result = jnp.where(block_at(lane, start), roll(edge, -step_x, 0), result)
        if step_z:
            moved = jnp.where(leaves_depth(edge.shape, step_z), 0.0, roll(edge, -step_z, 1))
            result = jnp.where(block_at(lane, start), moved, result)
    return result


def faces_kernel(partial, edges, own_s, own_z, got_s, got_z, wide, out_s, out_z):
    layers, columns = partial.shape
    even = (lax.axis_index("gx") & 1) == 0

    def pick(first, second, part):
        rows = slice(part * ROWS, part * ROWS + ROWS)
        return jnp.where(even, first[rows, :], second[rows, :])

    up = [pick(own_s, own_z, part) for part in range(3)]
    down = [pick(own_z, own_s, part) for part in range(3)]
    above = [pick(got_s, got_z, part) for part in range(3)]
    below = [pick(got_z, got_s, part) for part in range(3)]
    row = iota((ROWS, columns), 0)

    def completion(reads, gains):
        return jnp.sum(reads * gains, axis=0, keepdims=True)

    own_last = completion(face_reads(above[2], 1), up[0])
    own_first = completion(face_reads(below[2], -1), roll(down[0], -3, 0))
    far_first = completion(face_reads(up[2], -1), roll(above[0], -3, 0))
    far_last = completion(face_reads(down[2], 1), below[0])
    last = ROWS - 1
    wide[:ROWS, :] = partial[:ROWS, :] - jnp.where(row == 0, own_first, 0.0)
    wide[ROWS : layers - ROWS, :] = partial[ROWS : layers - ROWS, :]
    wide[layers - ROWS : layers, :] = partial[layers - ROWS :, :] + jnp.where(
        row == last, own_last, 0.0
    )
    halo = jnp.where(row < ROWS // 2, above[0], below[0])
    halo = halo - jnp.where(row == 0, far_first, 0.0) + jnp.where(row == last, far_last, 0.0)
    wide[layers:, :] = halo

    halo = jnp.where(row < ROWS // 2, above[1], below[1])
    edge = jnp.concatenate([edges[...], halo], axis=0)
    half = edge.shape[1] // 2
    low = outgoing(edge[:, :half], 1)
    high = outgoing(edge[:, half:], -1)
    low_field = roll(wide[:, :128], EDGE - 128, 1)
    high_field = roll(wide[:, columns - 128 :], EDGE - 128 - (128 - 3 * NZ), 1)
    lane = iota(low_field.shape, 1)
    held = (lane >= EDGE - 128) & (lane < EDGE - 128 + 3 * NZ)
    to_left = [low[:, :128], jnp.where(held, low_field, low[:, 128:])]
    to_right = [high[:, :128], jnp.where(held, high_field, high[:, 128:])]
    even_y = (lax.axis_index("gy") & 1) == 0
    for part in range(2):
        lanes = slice(part * 128, part * 128 + 128)
        out_s[:, lanes] = jnp.where(even_y, to_right[part], to_left[part])
        out_z[:, lanes] = jnp.where(even_y, to_left[part], to_right[part])


def hand_on_kernel(first, second, out):
    out[...] = first[...]


def fold(reads, gains, way):
    moved = roll(reads, -READS, 1)[:, :128]
    gains = gains[:, :128]
    lane = iota(gains.shape, 1)
    product = moved * gains
    for place, k in enumerate(Y_PAIRS):
        if way * PAIRS[k][1] < 0:
            product = jnp.where(block_at(lane, place * NZ), -product, product)
    total = product
    for place in range(1, len(Y_PAIRS)):
        total = total + roll(product, -place * NZ, 1)
    return jnp.where(lane < NZ, total, 0.0)


def laplace(field, depth, inside):
    rows, lanes = field.shape
    total = roll(field, 1, 0) + roll(field, -1, 0)
    total = total + (roll(field, NZ, 1) + roll(field, -NZ, 1))
    total = total + jnp.where(depth > 0, roll(field, 1, 1), 0.0)
    total = total + jnp.where(depth < NZ - 1, roll(field, -1, 1), 0.0)
    result = field - total * (1.0 / 6.0)
    return result if inside is None else jnp.where(inside, result, 0.0)


def tree_sum(parts):
    while len(parts) > 1:
        half = (len(parts) + 1) // 2
        parts = [
            parts[i] + parts[i + half] if i + half < len(parts) else parts[i] for i in range(half)
        ]
    return parts[0]


def sum_all(value):
    rows, lanes = value.shape
    parts = [
        value[r : r + ROWS, c : c + 128] for r in range(0, rows, ROWS) for c in range(0, lanes, 128)
    ]
    folded = tree_sum(parts)
    return jnp.sum(jnp.sum(folded, axis=0, keepdims=True), axis=1, keepdims=True)


def krylov_kernel(wide, own_s, own_z, got_s, got_z, basis, shares):
    rows, columns = wide.shape
    place = lax.axis_index("gy")
    last_place = lax.axis_size("gy") - 1
    even = (place & 1) == 0

    def pick(first, second):
        return jnp.where(even, first[...], second[...])

    to_right = pick(own_s, own_z)
    to_left = pick(own_z, own_s)
    right = pick(got_s, got_z)
    left = pick(got_z, got_s)
    lane = iota((rows, 128), 1)
    field = wide[...]
    low_end = field[:, :128] + fold(left, to_left, -1)
    high_end = field[:, columns - 128 :] + roll(fold(right, to_right, 1), 128 - NZ, 1)
    right_halo = jnp.where(lane < 3 * NZ, roll(right[:, 128:], 128 - EDGE, 1), 0.0)
    left_halo = jnp.where(
        lane >= 128 - 3 * NZ, roll(left[:, 128:], 128 - 3 * NZ - (EDGE - 128), 1), 0.0
    )
    halo = right_halo + fold(to_right, right, -1)
    halo = halo + (left_halo + roll(fold(to_left, left, 1), 128 - NZ, 1))
    field = jnp.concatenate([low_end, field[:, 128 : columns - 128], high_end, halo], axis=1)
    column = iota(field.shape, 1)
    depth = column & (NZ - 1)
    on_right = (column < columns + 64) & (place < last_place)
    on_left = (column >= columns + 64) & (place > 0)
    inside = (column < columns) | on_right | on_left
    first = laplace(field, depth, inside)
    second = laplace(first, depth, inside)
    third = laplace(second, depth, None)
    cores = [v[: basis.shape[1], :columns] for v in (field, first, second, third)]
    for power in range(ITERS):
        basis[power] = cores[power]
    row = jnp.zeros((1, 128), jnp.float32)
    lane = iota((1, 128), 1)
    for power in range(2 * ITERS):
        value = sum_all(cores[power // 2] * cores[(power + 1) // 2])
        row = jnp.where(lane == power, value, row)
    shares[...] = jnp.broadcast_to(row, shares.shape)


def times_h(poly):
    out = list(poly) + [0.0]
    for power, entry in enumerate(poly):
        out[power + 1] = out[power + 1] + (6.0 * radius_sq) * entry
    return out


def dot_poly(p, q, moments):
    total = 0.0
    for power in range(len(p) + len(q) - 1):
        terms = [p[i] * q[power - i] for i in range(len(p)) if 0 <= power - i < len(q)]
        total = total + tree_sum(terms) * moments[power]
    return total


def entry_of(poly, power):
    return poly[power] if power < len(poly) else 0.0


def combination(moments):
    upper = 1.0 + 12.0 * radius_sq
    growth = (upper - 1.0) ** 2 / (4.0 * upper) * 1.001
    one = jnp.ones_like(moments[0])
    solved, residual, direction = [], [one], [one]
    norm_now = moments[0]
    for iteration in range(ITERS):
        image = times_h(direction)
        step = norm_now / dot_poly(direction, image, moments)
        step = jnp.clip(step, 1.0 / upper, 1.0)
        solved = [entry_of(solved, k) + step * direction[k] for k in range(len(direction))]
        if iteration < ITERS - 1:
            residual = [entry_of(residual, k) - step * image[k] for k in range(len(image))]
            norm_next = jnp.maximum(dot_poly(residual, residual, moments), 0.0)
            ratio = jnp.clip(norm_next / norm_now, 0.0, growth)
            direction = [
                residual[k] + ratio * entry_of(direction, k) for k in range(len(residual))
            ]
            norm_now = norm_next
    return solved


def combine_kernel(shares, basis, filtered):
    count = shares.shape[0]
    total = tree_sum([shares[r : r + ROWS, :] for r in range(0, count, ROWS)])
    total = jnp.sum(total, axis=0, keepdims=True)
    lane = iota(total.shape, 1)
    moments = [
        jnp.sum(jnp.where(lane == power, total, 0.0), axis=1, keepdims=True)
        for power in range(2 * ITERS)
    ]
    weights = combination(moments)
    result = basis[0] * weights[0]
    for power in range(1, ITERS):
        result = result + basis[power] * weights[power]
    filtered[...] = result


def adjoint_kernel(
    forward_far,
    adjoint_far,
    design_far,
    node_far,
    got_s,
    got_z,
    side_s,
    side_z,
    result,
    forward,
    adjoint,
    design,
    node_type,
    adjoint_new,
    sems,
    out_sems,
):
    layers, columns = design.shape
    groups = fetch_tiles(
        (forward_far, adjoint_far, design_far, node_far),
        (forward, adjoint, design, node_type),
        sems,
    )
    sent = []
    tiles = layers // ROWS
    shape = (ROWS, columns)
    even = (lax.axis_index("gx") & 1) == 0
    even_y = (lax.axis_index("gy") & 1) == 0
    faces = slice(2 * ROWS, 3 * ROWS)
    above = jnp.where(even, got_s[faces, :], got_z[faces, :])
    below = jnp.where(even, got_z[faces, :], got_s[faces, :])
    column = iota(shape, 1)
    for tile in range(tiles):
        rows = slice(tile * ROWS, tile * ROWS + ROWS)
        right = jnp.where(even_y, side_s[rows, :], side_z[rows, :])
        left = jnp.where(even_y, side_z[rows, :], side_s[rows, :])
        take(groups, tile)
        density = forward[0, rows, :]
        differences = []
        for k in range(9):
            one, other = forward[2 * k + 1, rows, :], forward[2 * k + 2, rows, :]
            density = density + (one + other)
            differences.append(one - other)
        inverse = 1.0 / density
        velocity = [part * inverse for part in momentum_of(differences)]
        speed_sq = velocity[0] * velocity[0] + velocity[1] * velocity[1]
        speed_sq = speed_sq + velocity[2] * velocity[2]
        kind = node_type[rows, :]
        wall = kind == 1
        source = jnp.where(kind == 2, 1.0, jnp.where(kind == 3, -1.0, 0.0))
        blend = 1.0 - 2.0 * design[rows, :]
        rest = adjoint[0, rows, :]
        zeroth = REST_WEIGHT * rest
        quadratic = None
        vector = [None, None, None]
        kept = []
        for k in range(9):
            reads = []
            for sign in (1, -1):
                step = [sign * c for c in PAIRS[k]]
                member = member_of(k, sign)
                place = X_PAIRS.index(k) if k in X_PAIRS else 0
                read = row_tile(
                    adjoint,
                    member,
                    tile,
                    step[0],
                    above[place : place + 1, :],
                    below[place : place + 1, :],
                )
                if step[1] or step[2]:
                    read = roll(read, -(step[1] * NZ + step[2]), 1)
                if step[1]:
                    start = READS + Y_PAIRS.index(k) * NZ
                    side = right if step[1] > 0 else left
                    target = columns - NZ if step[1] > 0 else 0
                    part = side[:, start // 128 * 128 : start // 128 * 128 + 128]
                    part = roll(part, target - start, 1)
                    border = column >= columns - NZ if step[1] > 0 else column < NZ
                    spread = jnp.concatenate([part] * (columns // 128), axis=1)
                    read = jnp.where(border, spread, read)
                if step[2]:
                    bounce = adjoint[member_of(k, -sign), rows, :]
                    read = jnp.where(leaves_depth(shape, step[2]), bounce, read)
                reads.append(read)
            both = reads[0] + reads[1]
            odd = blend * (reads[0] - reads[1])
            projected = dot_velocity(PAIRS[k], velocity)
            even_part = WEIGHTS[k] * both
            zeroth = zeroth + even_part
            moved = even_part * projected
            square = moved * projected
            quadratic = square if quadratic is None else quadratic + square
            pull = (3.0 * WEIGHTS[k]) * odd + 9.0 * moved
            for axis in range(3):
                if PAIRS[k][axis]:
                    vector[axis] = (
                        signed_sum([(PAIRS[k][axis], pull)])
                        if vector[axis] is None
                        else signed_sum([(1, vector[axis]), (PAIRS[k][axis], pull)])
                    )
            kept.append((reads[0], reads[1], both, odd))
        scaled = relax_rate * zeroth
        base = scaled * (1.0 + 1.5 * speed_sq) - (4.5 * relax_rate) * quadratic + source
        vector = [
            relax_rate * part - (3.0 * scaled) * speed for part, speed in zip(vector, velocity)
        ]
        keep = relax_rate - 1.0
        adjoint_new[0, rows, :] = jnp.where(wall, rest, base - keep * rest)
        for k in range(9):
            one, other, both, odd = kept[k]
            level = base - (0.5 * keep) * both
            slope = dot_velocity(PAIRS[k], vector) - (0.5 * keep) * odd
            adjoint_new[2 * k + 1, rows, :] = jnp.where(wall, other, level + slope)
            adjoint_new[2 * k + 2, rows, :] = jnp.where(wall, one, level - slope)
        part = pl.ds(tile * ROWS, ROWS)
        sent.append(
            pltpu.make_async_copy(
                adjoint_new.at[:, part, :], result.at[:, part, :], out_sems.at[tile]
            )
        )
        sent[-1].start()
    for copy in sent:
        copy.wait()


def run(kernel, outputs, *operands, flops, far=0, far_out=False, scratch=(), vmem=32):
    sizes = [jax.ShapeDtypeStruct(shape, jnp.float32) for shape in outputs]
    moved = 4 * sum(a.size for a in operands) + 4 * sum(s.size for s in sizes)
    operands = [
        pltpu.with_memory_space_constraint(a, pltpu.HBM) if i < far else a
        for i, a in enumerate(operands)
    ]
    near = pl.BlockSpec(memory_space=pltpu.VMEM)
    away = pl.BlockSpec(memory_space=pl.ANY)
    return pl.pallas_call(
        kernel,
        out_shape=sizes,
        in_specs=[away if i < far else near for i in range(len(operands))],
        out_specs=[away if far_out else near for _ in outputs],
        scratch_shapes=list(scratch),
        compiler_params=pltpu.CompilerParams(vmem_limit_bytes=vmem * 1024 * 1024),
        cost_estimate=pl.CostEstimate(flops=flops, bytes_accessed=moved, transcendentals=0),
    )(*operands)


def swap(first, second, axis, closed):
    count = lax.axis_size(axis)
    starts = range(1, count if closed else count - 1, 2)
    far = [(i, (i + 1) % count) for i in starts]
    far = far + [(b, a) for a, b in far]
    near = [(i, i ^ 1) for i in range(count)]
    return lax.ppermute(first, axis, far), lax.ppermute(second, axis, near)


def shards(forward, adjoint, design, node_type):
    members, layers, columns = adjoint.shape
    sites = layers * columns
    devices = lax.axis_size("gx") * lax.axis_size("gy")
    plane = (layers, columns)
    face = (3 * ROWS, columns)
    side = (layers + ROWS, 256)
    tiles = layers // ROWS
    field = pltpu.VMEM((members,) + plane, jnp.float32)
    end = pltpu.VMEM((members, ROWS, columns), jnp.float32)

    def border(near):
        (message,) = run(
            functools.partial(border_kernel, near),
            [face],
            forward,
            adjoint,
            node_type,
            far=3,
            scratch=[
                end,
                end,
                pltpu.VMEM((ROWS, columns), jnp.int32),
                pltpu.SemaphoreType.DMA((5,)),
            ],
            flops=40 * sites,
        )
        return message

    own_z = border(False)
    own_s = border(True)
    got_z, got_s = swap(own_z, own_s, "gx", True)
    got_z = lax.optimization_barrier(got_z)
    partial, edges = run(
        collide_kernel,
        [plane, (layers, 512)],
        forward,
        adjoint,
        node_type,
        far=3,
        scratch=[
            field,
            field,
            pltpu.VMEM(plane, jnp.int32),
            pltpu.SemaphoreType.DMA((tiles, 3)),
        ],
        flops=150 * sites,
    )
    wide, out_s, out_z = run(
        faces_kernel,
        [(layers + ROWS, columns), side, side],
        partial,
        edges,
        own_s,
        own_z,
        got_s,
        got_z,
        flops=10 * sites,
    )
    side_z, side_s = swap(out_z, out_s, "gy", False)
    side_z = lax.optimization_barrier(side_z)
    basis, shares = run(
        krylov_kernel,
        [(ITERS,) + plane, (ROWS, 128)],
        wide,
        out_s,
        out_z,
        side_s,
        side_z,
        flops=60 * sites,
    )
    copies = jnp.broadcast_to(shares[None, :1], (devices, 1, 128))
    spread = lax.all_to_all(copies, ("gx", "gy"), 0, 0)
    (adjoint_new,) = run(
        adjoint_kernel,
        [adjoint.shape],
        forward,
        adjoint,
        design,
        node_type,
        got_s,
        got_z,
        side_s,
        side_z,
        far=4,
        far_out=True,
        scratch=[
            field,
            field,
            pltpu.VMEM(plane, jnp.float32),
            pltpu.VMEM(plane, jnp.int32),
            field,
            pltpu.SemaphoreType.DMA((tiles, 4)),
            pltpu.SemaphoreType.DMA((tiles,)),
        ],
        flops=400 * sites,
    )
    (filtered,) = run(
        combine_kernel, [plane], spread.reshape(devices, 128), basis, flops=10 * sites
    )
    return (adjoint_new, filtered)


def solution(mesh):
    placed = (P(None, "gx", "gy"), P(None, "gx", "gy"), P("gx", "gy"), P("gx", "gy"))
    return jax.shard_map(
        shards,
        mesh=mesh,
        in_specs=placed,
        out_specs=(P(None, "gx", "gy"), P("gx", "gy")),
        check_vma=False,
    )
```

```python
import functools

import jax
import jax.numpy as jnp
from jax import lax
from jax.experimental import pallas as pl
from jax.experimental.pallas import tpu as pltpu
from jax.sharding import PartitionSpec as P

NZ = 16
ITERS = 3
PAIRS = (
    (1, 0, 0),
    (0, 1, 0),
    (0, 0, 1),
    (1, 1, 0),
    (1, -1, 0),
    (1, 0, 1),
    (1, 0, -1),
    (0, 1, 1),
    (0, 1, -1),
)
WEIGHTS = (1.0 / 18.0,) * 3 + (1.0 / 36.0,) * 6
REST_WEIGHT = 1.0 / 3.0
X_PAIRS = (0, 3, 4, 5, 6)
Y_PAIRS = (1, 3, 4, 7, 8)
relax_rate = 1.25
radius_sq = 4.0
ROWS = 8
READS = 128
EDGE = 208
SPARE = 80


def iota(shape, axis):
    return lax.broadcasted_iota(jnp.int32, shape, axis)


def roll(value, shift, axis):
    shift = shift % value.shape[axis]
    return value if shift == 0 else pltpu.roll(value, shift, axis)


def signed_sum(terms):
    total = None
    for sign, value in terms:
        if total is None:
            total = value if sign > 0 else -value
        else:
            total = total + value if sign > 0 else total - value
    return total


def dot_velocity(velocity, vector):
    return signed_sum([(c, v) for c, v in zip(velocity, vector) if c != 0])


def momentum_of(differences):
    return [
        signed_sum([(PAIRS[k][axis], differences[k]) for k in range(9) if PAIRS[k][axis] != 0])
        for axis in range(3)
    ]


def member_of(k, sign):
    return 2 * k + 1 if sign > 0 else 2 * k + 2


def row_tile(ref, member, tile, step, above=None, below=None):
    start = tile * ROWS
    layers = ref.shape[1]
    if step == 0:
        return ref[member, start : start + ROWS, :]
    if 0 <= start + step and start + step + ROWS <= layers:
        return ref[member, start + step : start + step + ROWS, :]
    value = ref[member, start : start + ROWS, :]
    row = iota(value.shape, 0)
    if step > 0:
        return jnp.where(row < ROWS - 1, roll(value, ROWS - 1, 0), 0.0 if above is None else above)
    return jnp.where(row > 0, roll(value, 1, 0), 0.0 if below is None else below)


def slide(value, step_y, step_z):
    columns = value.shape[1]
    if step_y == 0 and step_z == 0:
        return value
    moved = roll(value, -(step_y * NZ + step_z), 1)
    column = iota(value.shape, 1)
    keep = None
    if step_y != 0:
        keep = column < columns - NZ if step_y > 0 else column >= NZ
    if step_z != 0:
        depth = column & (NZ - 1)
        inner = depth < NZ - 1 if step_z > 0 else depth > 0
        keep = inner if keep is None else keep & inner
    return jnp.where(keep, moved, 0.0)


def leaves_depth(shape, step_z):
    depth = iota(shape, 1) & (NZ - 1)
    return depth == NZ - 1 if step_z > 0 else depth == 0


def block_at(lane, start):
    return (lane >= start) & (lane < start + NZ)


def pack_edge(gains, populations, high):
    origin = 0 if not high else 128 - NZ
    shape = (ROWS, 128)
    lane = iota(shape, 1)
    halves = [jnp.zeros(shape, jnp.float32), jnp.zeros(shape, jnp.float32)]
    for half, values in enumerate((gains, populations)):
        for place, value in enumerate(values):
            columns = value.shape[1]
            part = value[:, :128] if not high else value[:, columns - 128 :]
            moved = roll(part, place * NZ - origin, 1)
            halves[half] = jnp.where(block_at(lane, place * NZ), moved, halves[half])
    return jnp.concatenate(halves, axis=1)


def gains_of(forward, kinds):
    differences = [forward(2 * k + 1) - forward(2 * k + 2) for k in range(9)]
    momentum = momentum_of(differences)
    fluid = kinds != 1
    gains = []
    for k in range(9):
        gain = (relax_rate - 1.0) * differences[k]
        gain = gain - (6.0 * relax_rate * WEIGHTS[k]) * dot_velocity(PAIRS[k], momentum)
        gains.append(jnp.where(fluid, gain, 0.0))
    return gains


def inner_sensitivity(gains, rows_of):
    total = None
    for k in range(9):
        reads = []
        for sign in (1, -1):
            step = [sign * c for c in PAIRS[k]]
            read = slide(rows_of(member_of(k, sign), step[0]), step[1], step[2])
            if step[2] != 0:
                bounce = rows_of(member_of(k, -sign), 0)
                read = jnp.where(leaves_depth(read.shape, step[2]), bounce, read)
            reads.append(read)
        term = (reads[0] - reads[1]) * gains[k]
        total = term if total is None else total + term
    return total


def pack_edges(gains, adjoint):
    packed = []
    for high in (False, True):
        way = -1 if high else 1
        populations = [adjoint(member_of(k, way * PAIRS[k][1])) for k in Y_PAIRS]
        packed.append(pack_edge([gains[k] for k in Y_PAIRS], populations, high))
    return jnp.concatenate(packed, axis=1)


def fourth(up, high):
    place = 1 if up == high else 2
    return READS + place * NZ


def stow(edge, up):
    half = edge.shape[1] // 2
    lane = iota((ROWS, half), 1)
    sides = []
    for high in (False, True):
        part = edge[:, half : 2 * half] if high else edge[:, :half]
        below = roll(roll(part, 1, 0), SPARE - fourth(True, high), 1)
        above = roll(roll(part, -1, 0), SPARE - fourth(False, high), 1)
        sides.append(jnp.where(block_at(lane, SPARE), jnp.where(up, below, above), part))
    return jnp.concatenate(sides, axis=1)


def unstow(halo):
    half = halo.shape[1] // 2
    lane = iota((ROWS, half), 1)
    row = iota((ROWS, half), 0)
    sides = []
    for high in (False, True):
        part = halo[:, half : 2 * half] if high else halo[:, :half]
        result = part
        for up, at, step in ((False, 3, 1), (True, 4, -1)):
            start = fourth(up, high)
            moved = roll(roll(part, step, 0), start - SPARE, 1)
            result = jnp.where((row == at) & block_at(lane, start), moved, result)
        sides.append(result)
    return jnp.concatenate(sides, axis=1)


def border_kernel(near, forward, adjoint, node_type, out, moving, carried, kinds, sems):
    layers, columns = node_type.shape
    odd = lax.axis_index("gx") & 1
    up = 1 - odd if near else odd
    rows = pl.ds(pl.multiple_of(up * (layers - ROWS), ROWS), ROWS)
    cuts = (1, 10, 19)
    copies = [pltpu.make_async_copy(node_type.at[rows, :], kinds, sems.at[0])]
    for source, target in ((forward, moving), (adjoint, carried)):
        for low, high in zip(cuts, cuts[1:]):
            members = pl.ds(low, high - low)
            copies.append(
                pltpu.make_async_copy(
                    source.at[members, rows, :], target.at[members], sems.at[len(copies)]
                )
            )
    for copy in copies:
        copy.start()
    for copy in copies[:3]:
        copy.wait()
    gains = gains_of(lambda member: moving[member], kinds[...])
    for copy in copies[3:]:
        copy.wait()
    row = iota((ROWS, columns), 0)

    def rows_of(member, step):
        value = carried[member]
        if step == 0:
            return value
        if step > 0:
            return jnp.where(row < ROWS - 1, roll(value, ROWS - 1, 0), 0.0)
        return jnp.where(row > 0, roll(value, 1, 0), 0.0)

    def border(value):
        return jnp.where(up == 1, value[ROWS - 1 :, :], value[:1, :])

    top = inner_sensitivity(gains, rows_of)
    edge = stow(pack_edges(gains, lambda member: carried[member]), up == 1)
    base = 3 * (1 - up)
    for index, k in enumerate(X_PAIRS):
        top = jnp.where(row == base + index, border(gains[k]), top)
        outward = jnp.where(
            up == 1, carried[2 * k + 2, ROWS - 1 :, :], carried[2 * k + 1, :1, :]
        )
        edge = jnp.where(row == base + index, outward, edge)
    out[:ROWS, :] = top
    out[ROWS:, :] = edge


def fetch_tiles(sources, targets, sems):
    tiles = sources[-1].shape[-2] // ROWS
    groups = []
    for tile in range(tiles):
        rows = pl.ds(tile * ROWS, ROWS)
        group = []
        for index, (source, target) in enumerate(zip(sources, targets)):
            at = (slice(None), rows) if len(source.shape) == 3 else (rows,)
            group.append(
                pltpu.make_async_copy(source.at[at], target.at[at], sems.at[tile, index])
            )
        for copy in group:
            copy.start()
        groups.append(group)
    return groups


def take(groups, tile):
    for ready in ((0, 1) if tile == 0 else (tile + 1,)):
        if ready < len(groups):
            for copy in groups[ready]:
                copy.wait()


def collide_kernel(forward, adjoint, node_type, partial, edges, moving, carried, kinds, sems):
    layers, columns = partial.shape
    groups = fetch_tiles((forward, adjoint, node_type), (moving, carried, kinds), sems)
    for tile in range(layers // ROWS):
        rows = slice(tile * ROWS, tile * ROWS + ROWS)
        take(groups, tile)
        gains = gains_of(lambda member: moving[member, rows, :], kinds[rows, :])
        partial[rows, :] = inner_sensitivity(
            gains, lambda member, step: row_tile(carried, member, tile, step)
        )
        edges[rows, :] = pack_edges(gains, lambda member: carried[member, rows, :])


def face_reads(faces, sign):
    row = iota(faces.shape, 0)
    result = faces
    for place, k in enumerate(X_PAIRS):
        step_y, step_z = sign * PAIRS[k][1], sign * PAIRS[k][2]
        if step_y or step_z:
            result = jnp.where(row == place, slide(faces, step_y, step_z), result)
    return result


def outgoing(edge, way):
    lane = iota(edge.shape, 1)
    result = edge
    for place, k in enumerate(Y_PAIRS):
        sign = way * PAIRS[k][1]
        step_x, step_z = sign * PAIRS[k][0], sign * PAIRS[k][2]
        start = READS + place * NZ
        if step_x:
            result = jnp.where(block_at(lane, start), roll(edge, -step_x, 0), result)
        if step_z:
            moved = jnp.where(leaves_depth(edge.shape, step_z), 0.0, roll(edge, -step_z, 1))
            result = jnp.where(block_at(lane, start), moved, result)
    return result


def faces_kernel(partial, edges, own_s, own_z, got_s, got_z, wide, out_s, out_z):
    layers, columns = partial.shape
    even = (lax.axis_index("gx") & 1) == 0

    def pick(first, second, part):
        rows = slice(part * ROWS, part * ROWS + ROWS)
        return jnp.where(even, first[rows, :], second[rows, :])

    up = [pick(own_s, own_z, part) for part in range(2)]
    down = [pick(own_z, own_s, part) for part in range(2)]
    above = [pick(got_s, got_z, part) for part in range(2)]
    below = [pick(got_z, got_s, part) for part in range(2)]
    row = iota((ROWS, columns), 0)

    def completion(reads, gains):
        product = jnp.where(row < len(X_PAIRS), reads * gains, 0.0)
        return jnp.sum(product, axis=0, keepdims=True)

    own_last = completion(face_reads(roll(above[1], -3, 0), 1), up[0])
    own_first = completion(face_reads(below[1], -1), roll(down[0], -3, 0))
    far_first = completion(face_reads(up[1], -1), roll(above[0], -3, 0))
    far_last = completion(face_reads(roll(down[1], -3, 0), 1), below[0])
    last = ROWS - 1
    wide[:ROWS, :] = partial[:ROWS, :] - jnp.where(row == 0, own_first, 0.0)
    wide[ROWS : layers - ROWS, :] = partial[ROWS : layers - ROWS, :]
    wide[layers - ROWS : layers, :] = partial[layers - ROWS :, :] + jnp.where(
        row == last, own_last, 0.0
    )
    halo = jnp.where(row < ROWS // 2, above[0], below[0])
    halo = halo - jnp.where(row == 0, far_first, 0.0) + jnp.where(row == last, far_last, 0.0)
    wide[layers:, :] = halo

    halo = unstow(jnp.where(row < ROWS // 2, above[1], below[1]))
    edge = jnp.concatenate([edges[...], halo], axis=0)
    half = edge.shape[1] // 2
    low = outgoing(edge[:, :half], 1)
    high = outgoing(edge[:, half:], -1)
    low_field = roll(wide[:, :128], EDGE - 128, 1)
    high_field = roll(wide[:, columns - 128 :], EDGE - 128 - (128 - 3 * NZ), 1)
    lane = iota(low_field.shape, 1)
    held = (lane >= EDGE - 128) & (lane < EDGE - 128 + 3 * NZ)
    to_left = [low[:, :128], jnp.where(held, low_field, low[:, 128:])]
    to_right = [high[:, :128], jnp.where(held, high_field, high[:, 128:])]
    even_y = (lax.axis_index("gy") & 1) == 0
    for part in range(2):
        lanes = slice(part * 128, part * 128 + 128)
        out_s[:, lanes] = jnp.where(even_y, to_right[part], to_left[part])
        out_z[:, lanes] = jnp.where(even_y, to_left[part], to_right[part])


def hand_on_kernel(first, second, out):
    out[...] = first[...]


def signed_products(reads, gains, way):
    product = reads[:, READS:] * gains[:, :128]
    lane = iota(product.shape, 1)
    for place, k in enumerate(Y_PAIRS):
        if way * PAIRS[k][1] < 0:
            product = jnp.where(block_at(lane, place * NZ), -product, product)
    return product


def fold(first, second):
    lane = iota(first.shape, 1)
    total = jnp.where(lane < 64, first, roll(second, 64, 1))
    total = total + roll(total, -NZ, 1)
    total = total + roll(total, -2 * NZ, 1)
    total = total + jnp.where(lane < 64, roll(first, 64, 1), second)
    low = jnp.where(lane < NZ, total, 0.0)
    return low, jnp.where(lane >= 128 - NZ, roll(total, 64 - NZ, 1), 0.0)


def laplace(field, depth, inside):
    rows, lanes = field.shape
    total = roll(field, 1, 0) + roll(field, -1, 0)
    total = total + (roll(field, NZ, 1) + roll(field, -NZ, 1))
    total = total + jnp.where(depth > 0, roll(field, 1, 1), 0.0)
    total = total + jnp.where(depth < NZ - 1, roll(field, -1, 1), 0.0)
    return jnp.where(inside, field - total * (1.0 / 6.0), 0.0)


def tree_sum(parts):
    while len(parts) > 1:
        half = (len(parts) + 1) // 2
        parts = [
            parts[i] + parts[i + half] if i + half < len(parts) else parts[i] for i in range(half)
        ]
    return parts[0]


def sum_all(value):
    rows, lanes = value.shape
    parts = [
        value[r : r + ROWS, c : c + 128] for r in range(0, rows, ROWS) for c in range(0, lanes, 128)
    ]
    folded = tree_sum(parts)
    return jnp.sum(jnp.sum(folded, axis=0, keepdims=True), axis=1, keepdims=True)


def krylov_kernel(wide, own_s, own_z, got_s, got_z, basis, shares):
    rows, columns = wide.shape
    place = lax.axis_index("gy")
    last_place = lax.axis_size("gy") - 1
    even = (place & 1) == 0

    def pick(first, second):
        return jnp.where(even, first[...], second[...])

    to_right = pick(own_s, own_z)
    to_left = pick(own_z, own_s)
    right = pick(got_s, got_z)
    left = pick(got_z, got_s)
    lane = iota((rows, 128), 1)
    field = wide[...]
    low, high = fold(signed_products(left, to_left, -1), signed_products(right, to_right, 1))
    low_end = field[:, :128] + low
    high_end = field[:, columns - 128 :] + high
    right_halo = jnp.where(lane < 3 * NZ, roll(right[:, 128:], 128 - EDGE, 1), 0.0)
    left_halo = jnp.where(
        lane >= 128 - 3 * NZ, roll(left[:, 128:], 128 - 3 * NZ - (EDGE - 128), 1), 0.0
    )
    low, high = fold(signed_products(to_right, right, -1), signed_products(to_left, left, 1))
    halo = (right_halo + low) + (left_halo + high)
    field = jnp.concatenate([low_end, field[:, 128 : columns - 128], high_end, halo], axis=1)
    column = iota(field.shape, 1)
    depth = column & (NZ - 1)
    on_right = (column < columns + 64) & (place < last_place)
    on_left = (column >= columns + 64) & (place > 0)
    inside = (column < columns) | on_right | on_left
    first = laplace(field, depth, inside)
    second = laplace(first, depth, inside)
    ahead = roll(second, -1, 0) + roll(second, -NZ, 1)
    ahead = ahead + jnp.where(depth < NZ - 1, roll(second, -1, 1), 0.0)
    third = second - ahead * (1.0 / 3.0)
    cores = [v[: basis.shape[1], :columns] for v in (field, first, second, third)]
    for power in range(ITERS):
        basis[power] = cores[power]
    row = jnp.zeros((1, 128), jnp.float32)
    lane = iota((1, 128), 1)
    for power in range(2 * ITERS):
        value = sum_all(cores[power // 2] * cores[(power + 1) // 2])
        row = jnp.where(lane == power, value, row)
    shares[...] = jnp.broadcast_to(row, shares.shape)


def times_h(poly):
    out = list(poly) + [0.0]
    for power, entry in enumerate(poly):
        out[power + 1] = out[power + 1] + (6.0 * radius_sq) * entry
    return out


def dot_poly(p, q, moments):
    total = 0.0
    for power in range(len(p) + len(q) - 1):
        terms = [p[i] * q[power - i] for i in range(len(p)) if 0 <= power - i < len(q)]
        total = total + tree_sum(terms) * moments[power]
    return total


def entry_of(poly, power):
    return poly[power] if power < len(poly) else 0.0


def combination(moments):
    upper = 1.0 + 12.0 * radius_sq
    growth = (upper - 1.0) ** 2 / (4.0 * upper) * 1.001
    one = jnp.ones_like(moments[0])
    solved, residual, direction = [], [one], [one]
    norm_now = moments[0]
    for iteration in range(ITERS):
        image = times_h(direction)
        step = norm_now / dot_poly(direction, image, moments)
        step = jnp.clip(step, 1.0 / upper, 1.0)
        solved = [entry_of(solved, k) + step * direction[k] for k in range(len(direction))]
        if iteration < ITERS - 1:
            residual = [entry_of(residual, k) - step * image[k] for k in range(len(image))]
            norm_next = jnp.maximum(dot_poly(residual, residual, moments), 0.0)
            ratio = jnp.clip(norm_next / norm_now, 0.0, growth)
            direction = [
                residual[k] + ratio * entry_of(direction, k) for k in range(len(residual))
            ]
            norm_now = norm_next
    return solved


def combine_kernel(shares, basis, filtered):
    count = shares.shape[0]
    total = tree_sum([shares[r : r + ROWS, :] for r in range(0, count, ROWS)])
    total = jnp.sum(total, axis=0, keepdims=True)
    lane = iota(total.shape, 1)
    moments = [
        jnp.sum(jnp.where(lane == power, total, 0.0), axis=1, keepdims=True)
        for power in range(2 * ITERS)
    ]
    weights = combination(moments)
    result = basis[0] * weights[0]
    for power in range(1, ITERS):
        result = result + basis[power] * weights[power]
    filtered[...] = result


def adjoint_kernel(
    forward_far,
    adjoint_far,
    design_far,
    node_far,
    got_s,
    got_z,
    side_s,
    side_z,
    result,
    forward,
    adjoint,
    design,
    node_type,
    adjoint_new,
    sems,
    out_sems,
):
    layers, columns = design.shape
    groups = fetch_tiles(
        (forward_far, adjoint_far, design_far, node_far),
        (forward, adjoint, design, node_type),
        sems,
    )
    sent = []
    tiles = layers // ROWS
    shape = (ROWS, columns)
    even = (lax.axis_index("gx") & 1) == 0
    even_y = (lax.axis_index("gy") & 1) == 0
    faces = slice(ROWS, 2 * ROWS)
    above = jnp.where(even, got_s[faces, :], got_z[faces, :])
    below = jnp.where(even, got_z[faces, :], got_s[faces, :])
    column = iota(shape, 1)
    for tile in range(tiles):
        rows = slice(tile * ROWS, tile * ROWS + ROWS)
        right = jnp.where(even_y, side_s[rows, :], side_z[rows, :])
        left = jnp.where(even_y, side_z[rows, :], side_s[rows, :])
        take(groups, tile)
        density = forward[0, rows, :]
        differences = []
        for k in range(9):
            one, other = forward[2 * k + 1, rows, :], forward[2 * k + 2, rows, :]
            density = density + (one + other)
            differences.append(one - other)
        inverse = 1.0 / density
        velocity = [part * inverse for part in momentum_of(differences)]
        speed_sq = velocity[0] * velocity[0] + velocity[1] * velocity[1]
        speed_sq = speed_sq + velocity[2] * velocity[2]
        kind = node_type[rows, :]
        wall = kind == 1
        source = jnp.where(kind == 2, 1.0, jnp.where(kind == 3, -1.0, 0.0))
        blend = 1.0 - 2.0 * design[rows, :]
        rest = adjoint[0, rows, :]
        zeroth = REST_WEIGHT * rest
        quadratic = None
        vector = [None, None, None]
        kept = []
        for k in range(9):
            reads = []
            for sign in (1, -1):
                step = [sign * c for c in PAIRS[k]]
                member = member_of(k, sign)
                place = X_PAIRS.index(k) if k in X_PAIRS else 0
                read = row_tile(
                    adjoint,
                    member,
                    tile,
                    step[0],
                    above[3 + place : 4 + place, :],
                    below[place : place + 1, :],
                )
                if step[1] or step[2]:
                    read = roll(read, -(step[1] * NZ + step[2]), 1)
                if step[1]:
                    start = READS + Y_PAIRS.index(k) * NZ
                    side = right if step[1] > 0 else left
                    target = columns - NZ if step[1] > 0 else 0
                    part = side[:, start // 128 * 128 : start // 128 * 128 + 128]
                    part = roll(part, target - start, 1)
                    border = column >= columns - NZ if step[1] > 0 else column < NZ
                    spread = jnp.concatenate([part] * (columns // 128), axis=1)
                    read = jnp.where(border, spread, read)
                if step[2]:
                    bounce = adjoint[member_of(k, -sign), rows, :]
                    read = jnp.where(leaves_depth(shape, step[2]), bounce, read)
                reads.append(read)
            both = reads[0] + reads[1]
            odd = blend * (reads[0] - reads[1])
            projected = dot_velocity(PAIRS[k], velocity)
            even_part = WEIGHTS[k] * both
            zeroth = zeroth + even_part
            moved = even_part * projected
            square = moved * projected
            quadratic = square if quadratic is None else quadratic + square
            pull = (3.0 * WEIGHTS[k]) * odd + 9.0 * moved
            for axis in range(3):
                if PAIRS[k][axis]:
                    vector[axis] = (
                        signed_sum([(PAIRS[k][axis], pull)])
                        if vector[axis] is None
                        else signed_sum([(1, vector[axis]), (PAIRS[k][axis], pull)])
                    )
            kept.append((reads[0], reads[1], both, odd))
        scaled = relax_rate * zeroth
        base = scaled * (1.0 + 1.5 * speed_sq) - (4.5 * relax_rate) * quadratic + source
        vector = [
            relax_rate * part - (3.0 * scaled) * speed for part, speed in zip(vector, velocity)
        ]
        keep = relax_rate - 1.0
        adjoint_new[0, rows, :] = jnp.where(wall, rest, base - keep * rest)
        for k in range(9):
            one, other, both, odd = kept[k]
            level = base - (0.5 * keep) * both
            slope = dot_velocity(PAIRS[k], vector) - (0.5 * keep) * odd
            adjoint_new[2 * k + 1, rows, :] = jnp.where(wall, other, level + slope)
            adjoint_new[2 * k + 2, rows, :] = jnp.where(wall, one, level - slope)
        part = pl.ds(tile * ROWS, ROWS)
        sent.append(
            pltpu.make_async_copy(
                adjoint_new.at[:, part, :], result.at[:, part, :], out_sems.at[tile]
            )
        )
        sent[-1].start()
    for copy in sent:
        copy.wait()


def run(kernel, outputs, *operands, flops, far=0, far_out=False, scratch=(), vmem=32):
    sizes = [jax.ShapeDtypeStruct(shape, jnp.float32) for shape in outputs]
    moved = 4 * sum(a.size for a in operands) + 4 * sum(s.size for s in sizes)
    operands = [
        pltpu.with_memory_space_constraint(a, pltpu.HBM) if i < far else a
        for i, a in enumerate(operands)
    ]
    near = pl.BlockSpec(memory_space=pltpu.VMEM)
    away = pl.BlockSpec(memory_space=pl.ANY)
    return pl.pallas_call(
        kernel,
        out_shape=sizes,
        in_specs=[away if i < far else near for i in range(len(operands))],
        out_specs=[away if far_out else near for _ in outputs],
        scratch_shapes=list(scratch),
        compiler_params=pltpu.CompilerParams(vmem_limit_bytes=vmem * 1024 * 1024),
        cost_estimate=pl.CostEstimate(flops=flops, bytes_accessed=moved, transcendentals=0),
    )(*operands)


def swap(first, second, axis, closed):
    count = lax.axis_size(axis)
    starts = range(1, count if closed else count - 1, 2)
    far = [(i, (i + 1) % count) for i in starts]
    far = far + [(b, a) for a, b in far]
    near = [(i, i ^ 1) for i in range(count)]
    return lax.ppermute(first, axis, far), lax.ppermute(second, axis, near)


def shards(forward, adjoint, design, node_type):
    members, layers, columns = adjoint.shape
    sites = layers * columns
    devices = lax.axis_size("gx") * lax.axis_size("gy")
    plane = (layers, columns)
    face = (2 * ROWS, columns)
    side = (layers + ROWS, 256)
    tiles = layers // ROWS
    field = pltpu.VMEM((members,) + plane, jnp.float32)
    end = pltpu.VMEM((members, ROWS, columns), jnp.float32)

    def border(near):
        (message,) = run(
            functools.partial(border_kernel, near),
            [face],
            forward,
            adjoint,
            node_type,
            far=3,
            scratch=[
                end,
                end,
                pltpu.VMEM((ROWS, columns), jnp.int32),
                pltpu.SemaphoreType.DMA((5,)),
            ],
            flops=40 * sites,
        )
        return message

    own_z = border(False)
    own_s = border(True)
    got_z, got_s = swap(own_z, own_s, "gx", True)
    got_z = lax.optimization_barrier(got_z)
    partial, edges = run(
        collide_kernel,
        [plane, (layers, 512)],
        forward,
        adjoint,
        node_type,
        far=3,
        scratch=[
            field,
            field,
            pltpu.VMEM(plane, jnp.int32),
            pltpu.SemaphoreType.DMA((tiles, 3)),
        ],
        flops=150 * sites,
    )
    wide, out_s, out_z = run(
        faces_kernel,
        [(layers + ROWS, columns), side, side],
        partial,
        edges,
        own_s,
        own_z,
        got_s,
        got_z,
        flops=10 * sites,
    )
    side_z, side_s = swap(out_z, out_s, "gy", False)
    side_z = lax.optimization_barrier(side_z)
    basis, shares = run(
        krylov_kernel,
        [(ITERS,) + plane, (devices, 128)],
        wide,
        out_s,
        out_z,
        side_s,
        side_z,
        flops=60 * sites,
    )
    spread = lax.all_to_all(shares.reshape(devices, 1, 128), ("gx", "gy"), 0, 0)
    (adjoint_new,) = run(
        adjoint_kernel,
        [adjoint.shape],
        forward,
        adjoint,
        design,
        node_type,
        got_s,
        got_z,
        side_s,
        side_z,
        far=4,
        far_out=True,
        scratch=[
            field,
            field,
            pltpu.VMEM(plane, jnp.float32),
            pltpu.VMEM(plane, jnp.int32),
            field,
            pltpu.SemaphoreType.DMA((tiles, 4)),
            pltpu.SemaphoreType.DMA((tiles,)),
        ],
        flops=400 * sites,
    )
    (filtered,) = run(
        combine_kernel, [plane], spread.reshape(devices, 128), basis, flops=10 * sites
    )
    return (adjoint_new, filtered)


def solution(mesh):
    placed = (P(None, "gx", "gy"), P(None, "gx", "gy"), P("gx", "gy"), P("gx", "gy"))
    return jax.shard_map(
        shards,
        mesh=mesh,
        in_specs=placed,
        out_specs=(P(None, "gx", "gy"), P("gx", "gy")),
        check_vma=False,
    )
```

```python
import functools

import jax
import jax.numpy as jnp
from jax import lax
from jax.experimental import pallas as pl
from jax.experimental.pallas import tpu as pltpu
from jax.sharding import PartitionSpec as P

NZ = 16
ITERS = 3
PAIRS = (
    (1, 0, 0),
    (0, 1, 0),
    (0, 0, 1),
    (1, 1, 0),
    (1, -1, 0),
    (1, 0, 1),
    (1, 0, -1),
    (0, 1, 1),
    (0, 1, -1),
)
WEIGHTS = (1.0 / 18.0,) * 3 + (1.0 / 36.0,) * 6
REST_WEIGHT = 1.0 / 3.0
X_PAIRS = (0, 3, 4, 5, 6)
Y_PAIRS = (1, 3, 4, 7, 8)
relax_rate = 1.25
radius_sq = 4.0
ROWS = 8
READS = 128
EDGE = 208
SPARE = 80


def iota(shape, axis):
    return lax.broadcasted_iota(jnp.int32, shape, axis)


def roll(value, shift, axis):
    shift = shift % value.shape[axis]
    return value if shift == 0 else pltpu.roll(value, shift, axis)


def signed_sum(terms):
    total = None
    for sign, value in terms:
        if total is None:
            total = value if sign > 0 else -value
        else:
            total = total + value if sign > 0 else total - value
    return total


def dot_velocity(velocity, vector):
    return signed_sum([(c, v) for c, v in zip(velocity, vector) if c != 0])


def momentum_of(differences):
    return [
        signed_sum([(PAIRS[k][axis], differences[k]) for k in range(9) if PAIRS[k][axis] != 0])
        for axis in range(3)
    ]


def member_of(k, sign):
    return 2 * k + 1 if sign > 0 else 2 * k + 2


def row_tile(ref, member, tile, step, above=None, below=None):
    start = tile * ROWS
    layers = ref.shape[1]
    if step == 0:
        return ref[member, start : start + ROWS, :]
    if 0 <= start + step and start + step + ROWS <= layers:
        return ref[member, start + step : start + step + ROWS, :]
    value = ref[member, start : start + ROWS, :]
    row = iota(value.shape, 0)
    if step > 0:
        return jnp.where(row < ROWS - 1, roll(value, ROWS - 1, 0), 0.0 if above is None else above)
    return jnp.where(row > 0, roll(value, 1, 0), 0.0 if below is None else below)


def slide(value, step_y, step_z):
    columns = value.shape[1]
    if step_y == 0 and step_z == 0:
        return value
    moved = roll(value, -(step_y * NZ + step_z), 1)
    column = iota(value.shape, 1)
    keep = None
    if step_y != 0:
        keep = column < columns - NZ if step_y > 0 else column >= NZ
    if step_z != 0:
        depth = column & (NZ - 1)
        inner = depth < NZ - 1 if step_z > 0 else depth > 0
        keep = inner if keep is None else keep & inner
    return jnp.where(keep, moved, 0.0)


def leaves_depth(shape, step_z):
    depth = iota(shape, 1) & (NZ - 1)
    return depth == NZ - 1 if step_z > 0 else depth == 0


def block_at(lane, start):
    return (lane >= start) & (lane < start + NZ)


def pack_edge(gains, populations, high):
    origin = 0 if not high else 128 - NZ
    shape = (ROWS, 128)
    lane = iota(shape, 1)
    halves = [jnp.zeros(shape, jnp.float32), jnp.zeros(shape, jnp.float32)]
    for half, values in enumerate((gains, populations)):
        for place, value in enumerate(values):
            columns = value.shape[1]
            part = value[:, :128] if not high else value[:, columns - 128 :]
            moved = roll(part, place * NZ - origin, 1)
            halves[half] = jnp.where(block_at(lane, place * NZ), moved, halves[half])
    return jnp.concatenate(halves, axis=1)


def gains_of(forward, kinds):
    differences = [forward(2 * k + 1) - forward(2 * k + 2) for k in range(9)]
    momentum = momentum_of(differences)
    fluid = kinds != 1
    gains = []
    for k in range(9):
        gain = (relax_rate - 1.0) * differences[k]
        gain = gain - (6.0 * relax_rate * WEIGHTS[k]) * dot_velocity(PAIRS[k], momentum)
        gains.append(jnp.where(fluid, gain, 0.0))
    return gains


def inner_sensitivity(gains, rows_of):
    total = None
    for k in range(9):
        reads = []
        for sign in (1, -1):
            step = [sign * c for c in PAIRS[k]]
            read = slide(rows_of(member_of(k, sign), step[0]), step[1], step[2])
            if step[2] != 0:
                bounce = rows_of(member_of(k, -sign), 0)
                read = jnp.where(leaves_depth(read.shape, step[2]), bounce, read)
            reads.append(read)
        term = (reads[0] - reads[1]) * gains[k]
        total = term if total is None else total + term
    return total


def pack_edges(gains, adjoint):
    packed = []
    for high in (False, True):
        way = -1 if high else 1
        populations = [adjoint(member_of(k, way * PAIRS[k][1])) for k in Y_PAIRS]
        packed.append(pack_edge([gains[k] for k in Y_PAIRS], populations, high))
    return jnp.concatenate(packed, axis=1)


def fourth(up, high):
    place = 1 if up == high else 2
    return READS + place * NZ


def stow(edge, up):
    half = edge.shape[1] // 2
    lane = iota((ROWS, half), 1)
    sides = []
    for high in (False, True):
        part = edge[:, half : 2 * half] if high else edge[:, :half]
        below = roll(roll(part, 1, 0), SPARE - fourth(True, high), 1)
        above = roll(roll(part, -1, 0), SPARE - fourth(False, high), 1)
        sides.append(jnp.where(block_at(lane, SPARE), jnp.where(up, below, above), part))
    return jnp.concatenate(sides, axis=1)


def unstow(halo):
    half = halo.shape[1] // 2
    lane = iota((ROWS, half), 1)
    row = iota((ROWS, half), 0)
    sides = []
    for high in (False, True):
        part = halo[:, half : 2 * half] if high else halo[:, :half]
        result = part
        for up, at, step in ((False, 3, 1), (True, 4, -1)):
            start = fourth(up, high)
            moved = roll(roll(part, step, 0), start - SPARE, 1)
            result = jnp.where((row == at) & block_at(lane, start), moved, result)
        sides.append(result)
    return jnp.concatenate(sides, axis=1)


def border_kernel(near, forward, adjoint, node_type, out, moving, carried, kinds, sems):
    layers, columns = node_type.shape
    odd = lax.axis_index("gx") & 1
    up = 1 - odd if near else odd
    half = ROWS // 2
    rows = pl.ds(pl.multiple_of(up * (layers - half), half), half)
    held = pl.ds(pl.multiple_of(up * half, half), half)
    cuts = (1, 7, 13, 19)
    copies = [pltpu.make_async_copy(node_type.at[rows, :], kinds.at[held, :], sems.at[0])]
    for source, target in ((forward, moving), (adjoint, carried)):
        for low, high in zip(cuts, cuts[1:]):
            members = pl.ds(low, high - low)
            copies.append(
                pltpu.make_async_copy(
                    source.at[members, rows, :], target.at[members, held, :], sems.at[len(copies)]
                )
            )
    for copy in copies:
        copy.start()
    for copy in copies[:4]:
        copy.wait()
    gains = gains_of(lambda member: moving[member], kinds[...])
    for copy in copies[4:]:
        copy.wait()
    row = iota((ROWS, columns), 0)

    def rows_of(member, step):
        value = carried[member]
        if step == 0:
            return value
        if step > 0:
            return jnp.where(row < ROWS - 1, roll(value, ROWS - 1, 0), 0.0)
        return jnp.where(row > 0, roll(value, 1, 0), 0.0)

    def border(value):
        return jnp.where(up == 1, value[ROWS - 1 :, :], value[:1, :])

    top = inner_sensitivity(gains, rows_of)
    edge = stow(pack_edges(gains, lambda member: carried[member]), up == 1)
    base = 3 * (1 - up)
    for index, k in enumerate(X_PAIRS):
        top = jnp.where(row == base + index, border(gains[k]), top)
        outward = jnp.where(
            up == 1, carried[2 * k + 2, ROWS - 1 :, :], carried[2 * k + 1, :1, :]
        )
        edge = jnp.where(row == base + index, outward, edge)
    out[:ROWS, :] = top
    out[ROWS:, :] = edge


def fetch_tiles(sources, targets, sems):
    tiles = sources[-1].shape[-2] // ROWS
    groups = []
    for tile in range(tiles):
        rows = pl.ds(tile * ROWS, ROWS)
        group = []
        for index, (source, target) in enumerate(zip(sources, targets)):
            at = (slice(None), rows) if len(source.shape) == 3 else (rows,)
            group.append(
                pltpu.make_async_copy(source.at[at], target.at[at], sems.at[tile, index])
            )
        for copy in group:
            copy.start()
        groups.append(group)
    return groups


def take(groups, tile):
    for ready in ((0, 1) if tile == 0 else (tile + 1,)):
        if ready < len(groups):
            for copy in groups[ready]:
                copy.wait()


def collide_kernel(forward, adjoint, node_type, partial, edges, moving, carried, kinds, sems):
    layers, columns = partial.shape
    groups = fetch_tiles((forward, adjoint, node_type), (moving, carried, kinds), sems)
    for tile in range(layers // ROWS):
        rows = slice(tile * ROWS, tile * ROWS + ROWS)
        take(groups, tile)
        gains = gains_of(lambda member: moving[member, rows, :], kinds[rows, :])
        partial[rows, :] = inner_sensitivity(
            gains, lambda member, step: row_tile(carried, member, tile, step)
        )
        edges[rows, :] = pack_edges(gains, lambda member: carried[member, rows, :])


def face_reads(faces, sign):
    row = iota(faces.shape, 0)
    result = faces
    for place, k in enumerate(X_PAIRS):
        step_y, step_z = sign * PAIRS[k][1], sign * PAIRS[k][2]
        if step_y or step_z:
            result = jnp.where(row == place, slide(faces, step_y, step_z), result)
    return result


def outgoing(edge, way):
    lane = iota(edge.shape, 1)
    result = edge
    for place, k in enumerate(Y_PAIRS):
        sign = way * PAIRS[k][1]
        step_x, step_z = sign * PAIRS[k][0], sign * PAIRS[k][2]
        start = READS + place * NZ
        if step_x:
            result = jnp.where(block_at(lane, start), roll(edge, -step_x, 0), result)
        if step_z:
            moved = jnp.where(leaves_depth(edge.shape, step_z), 0.0, roll(edge, -step_z, 1))
            result = jnp.where(block_at(lane, start), moved, result)
    return result


def faces_kernel(partial, edges, own_s, own_z, got_s, got_z, wide, out_s, out_z):
    layers, columns = partial.shape
    even = (lax.axis_index("gx") & 1) == 0

    def pick(first, second, part):
        rows = slice(part * ROWS, part * ROWS + ROWS)
        return jnp.where(even, first[rows, :], second[rows, :])

    up = [pick(own_s, own_z, part) for part in range(2)]
    down = [pick(own_z, own_s, part) for part in range(2)]
    above = [pick(got_s, got_z, part) for part in range(2)]
    below = [pick(got_z, got_s, part) for part in range(2)]
    row = iota((ROWS, columns), 0)

    def completion(reads, gains):
        product = jnp.where(row < len(X_PAIRS), reads * gains, 0.0)
        return jnp.sum(product, axis=0, keepdims=True)

    own_last = completion(face_reads(roll(above[1], -3, 0), 1), up[0])
    own_first = completion(face_reads(below[1], -1), roll(down[0], -3, 0))
    far_first = completion(face_reads(up[1], -1), roll(above[0], -3, 0))
    far_last = completion(face_reads(roll(down[1], -3, 0), 1), below[0])
    last = ROWS - 1
    wide[:ROWS, :] = partial[:ROWS, :] - jnp.where(row == 0, own_first, 0.0)
    wide[ROWS : layers - ROWS, :] = partial[ROWS : layers - ROWS, :]
    wide[layers - ROWS : layers, :] = partial[layers - ROWS :, :] + jnp.where(
        row == last, own_last, 0.0
    )
    halo = jnp.where(row < ROWS // 2, above[0], below[0])
    halo = halo - jnp.where(row == 0, far_first, 0.0) + jnp.where(row == last, far_last, 0.0)
    wide[layers:, :] = halo

    halo = unstow(jnp.where(row < ROWS // 2, above[1], below[1]))
    edge = jnp.concatenate([edges[...], halo], axis=0)
    half = edge.shape[1] // 2
    low = outgoing(edge[:, :half], 1)
    high = outgoing(edge[:, half:], -1)
    low_field = roll(wide[:, :128], EDGE - 128, 1)
    high_field = roll(wide[:, columns - 128 :], EDGE - 128 - (128 - 3 * NZ), 1)
    lane = iota(low_field.shape, 1)
    held = (lane >= EDGE - 128) & (lane < EDGE - 128 + 3 * NZ)
    to_left = [low[:, :128], jnp.where(held, low_field, low[:, 128:])]
    to_right = [high[:, :128], jnp.where(held, high_field, high[:, 128:])]
    even_y = (lax.axis_index("gy") & 1) == 0
    for part in range(2):
        lanes = slice(part * 128, part * 128 + 128)
        out_s[:, lanes] = jnp.where(even_y, to_right[part], to_left[part])
        out_z[:, lanes] = jnp.where(even_y, to_left[part], to_right[part])


def hand_on_kernel(first, second, out):
    out[...] = first[...]


def signed_products(reads, gains, way):
    product = reads[:, READS:] * gains[:, :128]
    lane = iota(product.shape, 1)
    for place, k in enumerate(Y_PAIRS):
        if way * PAIRS[k][1] < 0:
            product = jnp.where(block_at(lane, place * NZ), -product, product)
    return product


def fold(first, second):
    lane = iota(first.shape, 1)
    total = jnp.where(lane < 64, first, roll(second, 64, 1))
    total = total + roll(total, -NZ, 1)
    total = total + roll(total, -2 * NZ, 1)
    total = total + jnp.where(lane < 64, roll(first, 64, 1), second)
    low = jnp.where(lane < NZ, total, 0.0)
    return low, jnp.where(lane >= 128 - NZ, roll(total, 64 - NZ, 1), 0.0)


def laplace(field, depth, inside):
    rows, lanes = field.shape
    total = roll(field, 1, 0) + roll(field, -1, 0)
    total = total + (roll(field, NZ, 1) + roll(field, -NZ, 1))
    total = total + jnp.where(depth > 0, roll(field, 1, 1), 0.0)
    total = total + jnp.where(depth < NZ - 1, roll(field, -1, 1), 0.0)
    return jnp.where(inside, field - total * (1.0 / 6.0), 0.0)


def tree_sum(parts):
    while len(parts) > 1:
        half = (len(parts) + 1) // 2
        parts = [
            parts[i] + parts[i + half] if i + half < len(parts) else parts[i] for i in range(half)
        ]
    return parts[0]


def sum_all(value):
    rows, lanes = value.shape
    parts = [
        value[r : r + ROWS, c : c + 128] for r in range(0, rows, ROWS) for c in range(0, lanes, 128)
    ]
    folded = tree_sum(parts)
    return jnp.sum(jnp.sum(folded, axis=0, keepdims=True), axis=1, keepdims=True)


def krylov_kernel(wide, own_s, own_z, got_s, got_z, basis, shares):
    rows, columns = wide.shape
    place = lax.axis_index("gy")
    last_place = lax.axis_size("gy") - 1
    even = (place & 1) == 0

    def pick(first, second):
        return jnp.where(even, first[...], second[...])

    to_right = pick(own_s, own_z)
    to_left = pick(own_z, own_s)
    right = pick(got_s, got_z)
    left = pick(got_z, got_s)
    lane = iota((rows, 128), 1)
    field = wide[...]
    low, high = fold(signed_products(left, to_left, -1), signed_products(right, to_right, 1))
    low_end = field[:, :128] + low
    high_end = field[:, columns - 128 :] + high
    right_halo = jnp.where(lane < 3 * NZ, roll(right[:, 128:], 128 - EDGE, 1), 0.0)
    left_halo = jnp.where(
        lane >= 128 - 3 * NZ, roll(left[:, 128:], 128 - 3 * NZ - (EDGE - 128), 1), 0.0
    )
    low, high = fold(signed_products(to_right, right, -1), signed_products(to_left, left, 1))
    halo = (right_halo + low) + (left_halo + high)
    field = jnp.concatenate([low_end, field[:, 128 : columns - 128], high_end, halo], axis=1)
    column = iota(field.shape, 1)
    depth = column & (NZ - 1)
    on_right = (column < columns + 64) & (place < last_place)
    on_left = (column >= columns + 64) & (place > 0)
    inside = (column < columns) | on_right | on_left
    first = laplace(field, depth, inside)
    second = laplace(first, depth, inside)
    ahead = roll(second, -1, 0) + roll(second, -NZ, 1)
    ahead = ahead + jnp.where(depth < NZ - 1, roll(second, -1, 1), 0.0)
    third = second - ahead * (1.0 / 3.0)
    cores = [v[: basis.shape[1], :columns] for v in (field, first, second, third)]
    for power in range(ITERS):
        basis[power] = cores[power]
    row = jnp.zeros((1, 128), jnp.float32)
    lane = iota((1, 128), 1)
    for power in range(2 * ITERS):
        value = sum_all(cores[power // 2] * cores[(power + 1) // 2])
        row = jnp.where(lane == power, value, row)
    shares[...] = jnp.broadcast_to(row, shares.shape)


def times_h(poly):
    out = list(poly) + [0.0]
    for power, entry in enumerate(poly):
        out[power + 1] = out[power + 1] + (6.0 * radius_sq) * entry
    return out


def dot_poly(p, q, moments):
    total = 0.0
    for power in range(len(p) + len(q) - 1):
        terms = [p[i] * q[power - i] for i in range(len(p)) if 0 <= power - i < len(q)]
        total = total + tree_sum(terms) * moments[power]
    return total


def entry_of(poly, power):
    return poly[power] if power < len(poly) else 0.0


def combination(moments):
    upper = 1.0 + 12.0 * radius_sq
    growth = (upper - 1.0) ** 2 / (4.0 * upper) * 1.001
    one = jnp.ones_like(moments[0])
    solved, residual, direction = [], [one], [one]
    norm_now = moments[0]
    for iteration in range(ITERS):
        image = times_h(direction)
        step = norm_now / dot_poly(direction, image, moments)
        step = jnp.clip(step, 1.0 / upper, 1.0)
        solved = [entry_of(solved, k) + step * direction[k] for k in range(len(direction))]
        if iteration < ITERS - 1:
            residual = [entry_of(residual, k) - step * image[k] for k in range(len(image))]
            norm_next = jnp.maximum(dot_poly(residual, residual, moments), 0.0)
            ratio = jnp.clip(norm_next / norm_now, 0.0, growth)
            direction = [
                residual[k] + ratio * entry_of(direction, k) for k in range(len(residual))
            ]
            norm_now = norm_next
    return solved


def combine_kernel(shares, basis, filtered):
    count = shares.shape[0]
    total = tree_sum([shares[r : r + ROWS, :] for r in range(0, count, ROWS)])
    total = jnp.sum(total, axis=0, keepdims=True)
    lane = iota(total.shape, 1)
    moments = [
        jnp.sum(jnp.where(lane == power, total, 0.0), axis=1, keepdims=True)
        for power in range(2 * ITERS)
    ]
    weights = combination(moments)
    result = basis[0] * weights[0]
    for power in range(1, ITERS):
        result = result + basis[power] * weights[power]
    filtered[...] = result


def adjoint_kernel(
    forward_far,
    adjoint_far,
    design_far,
    node_far,
    got_s,
    got_z,
    side_s,
    side_z,
    result,
    forward,
    adjoint,
    design,
    node_type,
    adjoint_new,
    sems,
    out_sems,
):
    layers, columns = design.shape
    groups = fetch_tiles(
        (forward_far, adjoint_far, design_far, node_far),
        (forward, adjoint, design, node_type),
        sems,
    )
    sent = []
    tiles = layers // ROWS
    shape = (ROWS, columns)
    even = (lax.axis_index("gx") & 1) == 0
    even_y = (lax.axis_index("gy") & 1) == 0
    faces = slice(ROWS, 2 * ROWS)
    above = jnp.where(even, got_s[faces, :], got_z[faces, :])
    below = jnp.where(even, got_z[faces, :], got_s[faces, :])
    column = iota(shape, 1)
    for tile in range(tiles):
        rows = slice(tile * ROWS, tile * ROWS + ROWS)
        right = jnp.where(even_y, side_s[rows, :], side_z[rows, :])
        left = jnp.where(even_y, side_z[rows, :], side_s[rows, :])
        take(groups, tile)
        density = forward[0, rows, :]
        differences = []
        for k in range(9):
            one, other = forward[2 * k + 1, rows, :], forward[2 * k + 2, rows, :]
            density = density + (one + other)
            differences.append(one - other)
        inverse = 1.0 / density
        velocity = [part * inverse for part in momentum_of(differences)]
        speed_sq = velocity[0] * velocity[0] + velocity[1] * velocity[1]
        speed_sq = speed_sq + velocity[2] * velocity[2]
        kind = node_type[rows, :]
        wall = kind == 1
        source = jnp.where(kind == 2, 1.0, jnp.where(kind == 3, -1.0, 0.0))
        blend = 1.0 - 2.0 * design[rows, :]
        rest = adjoint[0, rows, :]
        zeroth = REST_WEIGHT * rest
        quadratic = None
        vector = [None, None, None]
        kept = []
        for k in range(9):
            reads = []
            for sign in (1, -1):
                step = [sign * c for c in PAIRS[k]]
                member = member_of(k, sign)
                place = X_PAIRS.index(k) if k in X_PAIRS else 0
                read = row_tile(
                    adjoint,
                    member,
                    tile,
                    step[0],
                    above[3 + place : 4 + place, :],
                    below[place : place + 1, :],
                )
                if step[1] or step[2]:
                    read = roll(read, -(step[1] * NZ + step[2]), 1)
                if step[1]:
                    start = READS + Y_PAIRS.index(k) * NZ
                    side = right if step[1] > 0 else left
                    target = columns - NZ if step[1] > 0 else 0
                    part = side[:, start // 128 * 128 : start // 128 * 128 + 128]
                    part = roll(part, target - start, 1)
                    border = column >= columns - NZ if step[1] > 0 else column < NZ
                    spread = jnp.concatenate([part] * (columns // 128), axis=1)
                    read = jnp.where(border, spread, read)
                if step[2]:
                    bounce = adjoint[member_of(k, -sign), rows, :]
                    read = jnp.where(leaves_depth(shape, step[2]), bounce, read)
                reads.append(read)
            both = reads[0] + reads[1]
            odd = blend * (reads[0] - reads[1])
            projected = dot_velocity(PAIRS[k], velocity)
            even_part = WEIGHTS[k] * both
            zeroth = zeroth + even_part
            moved = even_part * projected
            square = moved * projected
            quadratic = square if quadratic is None else quadratic + square
            pull = (3.0 * WEIGHTS[k]) * odd + 9.0 * moved
            for axis in range(3):
                if PAIRS[k][axis]:
                    vector[axis] = (
                        signed_sum([(PAIRS[k][axis], pull)])
                        if vector[axis] is None
                        else signed_sum([(1, vector[axis]), (PAIRS[k][axis], pull)])
                    )
            kept.append((reads[0], reads[1], both, odd))
        scaled = relax_rate * zeroth
        base = scaled * (1.0 + 1.5 * speed_sq) - (4.5 * relax_rate) * quadratic + source
        vector = [
            relax_rate * part - (3.0 * scaled) * speed for part, speed in zip(vector, velocity)
        ]
        keep = relax_rate - 1.0
        adjoint_new[0, rows, :] = jnp.where(wall, rest, base - keep * rest)
        for k in range(9):
            one, other, both, odd = kept[k]
            level = base - (0.5 * keep) * both
            slope = dot_velocity(PAIRS[k], vector) - (0.5 * keep) * odd
            adjoint_new[2 * k + 1, rows, :] = jnp.where(wall, other, level + slope)
            adjoint_new[2 * k + 2, rows, :] = jnp.where(wall, one, level - slope)
        part = pl.ds(tile * ROWS, ROWS)
        sent.append(
            pltpu.make_async_copy(
                adjoint_new.at[:, part, :], result.at[:, part, :], out_sems.at[tile]
            )
        )
        sent[-1].start()
    for copy in sent:
        copy.wait()


def run(kernel, outputs, *operands, flops, far=0, far_out=False, scratch=(), vmem=32):
    sizes = [jax.ShapeDtypeStruct(shape, jnp.float32) for shape in outputs]
    moved = 4 * sum(a.size for a in operands) + 4 * sum(s.size for s in sizes)
    operands = [
        pltpu.with_memory_space_constraint(a, pltpu.HBM) if i < far else a
        for i, a in enumerate(operands)
    ]
    near = pl.BlockSpec(memory_space=pltpu.VMEM)
    away = pl.BlockSpec(memory_space=pl.ANY)
    return pl.pallas_call(
        kernel,
        out_shape=sizes,
        in_specs=[away if i < far else near for i in range(len(operands))],
        out_specs=[away if far_out else near for _ in outputs],
        scratch_shapes=list(scratch),
        compiler_params=pltpu.CompilerParams(vmem_limit_bytes=vmem * 1024 * 1024),
        cost_estimate=pl.CostEstimate(flops=flops, bytes_accessed=moved, transcendentals=0),
    )(*operands)


def swap(first, second, axis, closed):
    count = lax.axis_size(axis)
    starts = range(1, count if closed else count - 1, 2)
    far = [(i, (i + 1) % count) for i in starts]
    far = far + [(b, a) for a, b in far]
    near = [(i, i ^ 1) for i in range(count)]
    return lax.ppermute(first, axis, far), lax.ppermute(second, axis, near)


def shards(forward, adjoint, design, node_type):
    members, layers, columns = adjoint.shape
    sites = layers * columns
    devices = lax.axis_size("gx") * lax.axis_size("gy")
    plane = (layers, columns)
    face = (2 * ROWS, columns)
    side = (layers + ROWS, 256)
    tiles = layers // ROWS
    field = pltpu.VMEM((members,) + plane, jnp.float32)
    end = pltpu.VMEM((members, ROWS, columns), jnp.float32)

    def border(near):
        (message,) = run(
            functools.partial(border_kernel, near),
            [face],
            forward,
            adjoint,
            node_type,
            far=3,
            scratch=[
                end,
                end,
                pltpu.VMEM((ROWS, columns), jnp.int32),
                pltpu.SemaphoreType.DMA((7,)),
            ],
            flops=40 * sites,
        )
        return message

    own_z = border(False)
    own_s = border(True)
    got_z, got_s = swap(own_z, own_s, "gx", True)
    got_z = lax.optimization_barrier(got_z)
    partial, edges = run(
        collide_kernel,
        [plane, (layers, 512)],
        forward,
        adjoint,
        node_type,
        far=3,
        scratch=[
            field,
            field,
            pltpu.VMEM(plane, jnp.int32),
            pltpu.SemaphoreType.DMA((tiles, 3)),
        ],
        flops=150 * sites,
    )
    wide, out_s, out_z = run(
        faces_kernel,
        [(layers + ROWS, columns), side, side],
        partial,
        edges,
        own_s,
        own_z,
        got_s,
        got_z,
        flops=10 * sites,
    )
    side_z, side_s = swap(out_z, out_s, "gy", False)
    side_z = lax.optimization_barrier(side_z)
    basis, shares = run(
        krylov_kernel,
        [(ITERS,) + plane, (devices, 128)],
        wide,
        out_s,
        out_z,
        side_s,
        side_z,
        flops=60 * sites,
    )
    spread = lax.all_to_all(shares.reshape(devices, 1, 128), ("gx", "gy"), 0, 0)
    (adjoint_new,) = run(
        adjoint_kernel,
        [adjoint.shape],
        forward,
        adjoint,
        design,
        node_type,
        got_s,
        got_z,
        side_s,
        side_z,
        far=4,
        far_out=True,
        scratch=[
            field,
            field,
            pltpu.VMEM(plane, jnp.float32),
            pltpu.VMEM(plane, jnp.int32),
            field,
            pltpu.SemaphoreType.DMA((tiles, 4)),
            pltpu.SemaphoreType.DMA((tiles,)),
        ],
        flops=400 * sites,
    )
    (filtered,) = run(
        combine_kernel, [plane], spread.reshape(devices, 128), basis, flops=10 * sites
    )
    return (adjoint_new, filtered)


def solution(mesh):
    placed = (P(None, "gx", "gy"), P(None, "gx", "gy"), P("gx", "gy"), P("gx", "gy"))
    return jax.shard_map(
        shards,
        mesh=mesh,
        in_specs=placed,
        out_specs=(P(None, "gx", "gy"), P("gx", "gy")),
        check_vma=False,
    )
```

```python
import functools

import jax
import jax.numpy as jnp
from jax import lax
from jax.experimental import pallas as pl
from jax.experimental.pallas import tpu as pltpu
from jax.sharding import PartitionSpec as P

NZ = 16
ITERS = 3
PAIRS = (
    (1, 0, 0),
    (0, 1, 0),
    (0, 0, 1),
    (1, 1, 0),
    (1, -1, 0),
    (1, 0, 1),
    (1, 0, -1),
    (0, 1, 1),
    (0, 1, -1),
)
WEIGHTS = (1.0 / 18.0,) * 3 + (1.0 / 36.0,) * 6
REST_WEIGHT = 1.0 / 3.0
X_PAIRS = (0, 3, 4, 5, 6)
Y_PAIRS = (1, 3, 4, 7, 8)
relax_rate = 1.25
radius_sq = 4.0
ROWS = 8
READS = 128
EDGE = 208
SPARE = 80
CENTRES = (0.0, 1.0, 2.0)


def iota(shape, axis):
    return lax.broadcasted_iota(jnp.int32, shape, axis)


def roll(value, shift, axis):
    shift = shift % value.shape[axis]
    return value if shift == 0 else pltpu.roll(value, shift, axis)


def signed_sum(terms):
    total = None
    for sign, value in terms:
        if total is None:
            total = value if sign > 0 else -value
        else:
            total = total + value if sign > 0 else total - value
    return total


def dot_velocity(velocity, vector):
    return signed_sum([(c, v) for c, v in zip(velocity, vector) if c != 0])


def momentum_of(differences):
    return [
        signed_sum([(PAIRS[k][axis], differences[k]) for k in range(9) if PAIRS[k][axis] != 0])
        for axis in range(3)
    ]


def member_of(k, sign):
    return 2 * k + 1 if sign > 0 else 2 * k + 2


def row_tile(ref, member, tile, step, above=None, below=None):
    start = tile * ROWS
    layers = ref.shape[1]
    if step == 0:
        return ref[member, start : start + ROWS, :]
    if 0 <= start + step and start + step + ROWS <= layers:
        return ref[member, start + step : start + step + ROWS, :]
    value = ref[member, start : start + ROWS, :]
    row = iota(value.shape, 0)
    if step > 0:
        return jnp.where(row < ROWS - 1, roll(value, ROWS - 1, 0), 0.0 if above is None else above)
    return jnp.where(row > 0, roll(value, 1, 0), 0.0 if below is None else below)


def slide(value, step_y, step_z):
    columns = value.shape[1]
    if step_y == 0 and step_z == 0:
        return value
    moved = roll(value, -(step_y * NZ + step_z), 1)
    column = iota(value.shape, 1)
    keep = None
    if step_y != 0:
        keep = column < columns - NZ if step_y > 0 else column >= NZ
    if step_z != 0:
        depth = column & (NZ - 1)
        inner = depth < NZ - 1 if step_z > 0 else depth > 0
        keep = inner if keep is None else keep & inner
    return jnp.where(keep, moved, 0.0)


def leaves_depth(shape, step_z):
    depth = iota(shape, 1) & (NZ - 1)
    return depth == NZ - 1 if step_z > 0 else depth == 0


def block_at(lane, start):
    return (lane >= start) & (lane < start + NZ)


def pack_edge(gains, populations, high):
    origin = 0 if not high else 128 - NZ
    shape = (ROWS, 128)
    lane = iota(shape, 1)
    halves = [jnp.zeros(shape, jnp.float32), jnp.zeros(shape, jnp.float32)]
    for half, values in enumerate((gains, populations)):
        for place, value in enumerate(values):
            columns = value.shape[1]
            part = value[:, :128] if not high else value[:, columns - 128 :]
            moved = roll(part, place * NZ - origin, 1)
            halves[half] = jnp.where(block_at(lane, place * NZ), moved, halves[half])
    return jnp.concatenate(halves, axis=1)


def gains_of(forward, kinds):
    differences = [forward(2 * k + 1) - forward(2 * k + 2) for k in range(9)]
    momentum = momentum_of(differences)
    fluid = kinds != 1
    gains = []
    for k in range(9):
        gain = (relax_rate - 1.0) * differences[k]
        gain = gain - (6.0 * relax_rate * WEIGHTS[k]) * dot_velocity(PAIRS[k], momentum)
        gains.append(jnp.where(fluid, gain, 0.0))
    return gains


def inner_sensitivity(gains, rows_of):
    total = None
    for k in range(9):
        reads = []
        for sign in (1, -1):
            step = [sign * c for c in PAIRS[k]]
            read = slide(rows_of(member_of(k, sign), step[0]), step[1], step[2])
            if step[2] != 0:
                bounce = rows_of(member_of(k, -sign), 0)
                read = jnp.where(leaves_depth(read.shape, step[2]), bounce, read)
            reads.append(read)
        term = (reads[0] - reads[1]) * gains[k]
        total = term if total is None else total + term
    return total


def pack_edges(gains, adjoint):
    packed = []
    for high in (False, True):
        way = -1 if high else 1
        populations = [adjoint(member_of(k, way * PAIRS[k][1])) for k in Y_PAIRS]
        packed.append(pack_edge([gains[k] for k in Y_PAIRS], populations, high))
    return jnp.concatenate(packed, axis=1)


def fourth(up, high):
    place = 1 if up == high else 2
    return READS + place * NZ


def stow(edge, up):
    half = edge.shape[1] // 2
    lane = iota((ROWS, half), 1)
    sides = []
    for high in (False, True):
        part = edge[:, half : 2 * half] if high else edge[:, :half]
        below = roll(roll(part, 1, 0), SPARE - fourth(True, high), 1)
        above = roll(roll(part, -1, 0), SPARE - fourth(False, high), 1)
        sides.append(jnp.where(block_at(lane, SPARE), jnp.where(up, below, above), part))
    return jnp.concatenate(sides, axis=1)


def unstow(halo):
    half = halo.shape[1] // 2
    lane = iota((ROWS, half), 1)
    row = iota((ROWS, half), 0)
    sides = []
    for high in (False, True):
        part = halo[:, half : 2 * half] if high else halo[:, :half]
        result = part
        for up, at, step in ((False, 3, 1), (True, 4, -1)):
            start = fourth(up, high)
            moved = roll(roll(part, step, 0), start - SPARE, 1)
            result = jnp.where((row == at) & block_at(lane, start), moved, result)
        sides.append(result)
    return jnp.concatenate(sides, axis=1)


def border_kernel(near, forward, adjoint, node_type, out, moving, carried, kinds, sems):
    layers, columns = node_type.shape
    odd = lax.axis_index("gx") & 1
    up = 1 - odd if near else odd
    half = ROWS // 2
    rows = pl.ds(pl.multiple_of(up * (layers - half), half), half)
    held = pl.ds(pl.multiple_of(up * half, half), half)
    cuts = (1, 7, 13, 19)
    copies = [pltpu.make_async_copy(node_type.at[rows, :], kinds.at[held, :], sems.at[0])]
    for source, target in ((forward, moving), (adjoint, carried)):
        for low, high in zip(cuts, cuts[1:]):
            members = pl.ds(low, high - low)
            copies.append(
                pltpu.make_async_copy(
                    source.at[members, rows, :], target.at[members, held, :], sems.at[len(copies)]
                )
            )
    for copy in copies:
        copy.start()
    for copy in copies[:4]:
        copy.wait()
    gains = gains_of(lambda member: moving[member], kinds[...])
    for copy in copies[4:]:
        copy.wait()
    row = iota((ROWS, columns), 0)

    def rows_of(member, step):
        value = carried[member]
        if step == 0:
            return value
        if step > 0:
            return jnp.where(row < ROWS - 1, roll(value, ROWS - 1, 0), 0.0)
        return jnp.where(row > 0, roll(value, 1, 0), 0.0)

    def border(value):
        return jnp.where(up == 1, value[ROWS - 1 :, :], value[:1, :])

    top = inner_sensitivity(gains, rows_of)
    edge = stow(pack_edges(gains, lambda member: carried[member]), up == 1)
    base = 3 * (1 - up)
    for index, k in enumerate(X_PAIRS):
        top = jnp.where(row == base + index, border(gains[k]), top)
        outward = jnp.where(
            up == 1, carried[2 * k + 2, ROWS - 1 :, :], carried[2 * k + 1, :1, :]
        )
        edge = jnp.where(row == base + index, outward, edge)
    out[:ROWS, :] = top
    out[ROWS:, :] = edge


def fetch_tiles(sources, targets, sems):
    tiles = sources[-1].shape[-2] // ROWS
    groups = []
    for tile in range(tiles):
        rows = pl.ds(tile * ROWS, ROWS)
        group = []
        for index, (source, target) in enumerate(zip(sources, targets)):
            at = (slice(None), rows) if len(source.shape) == 3 else (rows,)
            group.append(
                pltpu.make_async_copy(source.at[at], target.at[at], sems.at[tile, index])
            )
        for copy in group:
            copy.start()
        groups.append(group)
    return groups


def take(groups, tile):
    for ready in ((0, 1) if tile == 0 else (tile + 1,)):
        if ready < len(groups):
            for copy in groups[ready]:
                copy.wait()


def collide_kernel(forward, adjoint, node_type, partial, edges, moving, carried, kinds, sems):
    layers, columns = partial.shape
    groups = fetch_tiles((forward, adjoint, node_type), (moving, carried, kinds), sems)
    for tile in range(layers // ROWS):
        rows = slice(tile * ROWS, tile * ROWS + ROWS)
        take(groups, tile)
        gains = gains_of(lambda member: moving[member, rows, :], kinds[rows, :])
        partial[rows, :] = inner_sensitivity(
            gains, lambda member, step: row_tile(carried, member, tile, step)
        )
        edges[rows, :] = pack_edges(gains, lambda member: carried[member, rows, :])


def face_reads(faces, sign):
    row = iota(faces.shape, 0)
    result = faces
    for place, k in enumerate(X_PAIRS):
        step_y, step_z = sign * PAIRS[k][1], sign * PAIRS[k][2]
        if step_y or step_z:
            result = jnp.where(row == place, slide(faces, step_y, step_z), result)
    return result


def outgoing(edge, way):
    lane = iota(edge.shape, 1)
    result = edge
    for place, k in enumerate(Y_PAIRS):
        sign = way * PAIRS[k][1]
        step_x, step_z = sign * PAIRS[k][0], sign * PAIRS[k][2]
        start = READS + place * NZ
        if step_x:
            result = jnp.where(block_at(lane, start), roll(edge, -step_x, 0), result)
        if step_z:
            moved = jnp.where(leaves_depth(edge.shape, step_z), 0.0, roll(edge, -step_z, 1))
            result = jnp.where(block_at(lane, start), moved, result)
    return result


def faces_kernel(partial, edges, own_s, own_z, got_s, got_z, wide, out_s, out_z):
    layers, columns = partial.shape
    even = (lax.axis_index("gx") & 1) == 0

    def pick(first, second, part):
        rows = slice(part * ROWS, part * ROWS + ROWS)
        return jnp.where(even, first[rows, :], second[rows, :])

    up = [pick(own_s, own_z, part) for part in range(2)]
    down = [pick(own_z, own_s, part) for part in range(2)]
    above = [pick(got_s, got_z, part) for part in range(2)]
    below = [pick(got_z, got_s, part) for part in range(2)]
    row = iota((ROWS, columns), 0)

    def completion(reads, gains):
        product = jnp.where(row < len(X_PAIRS), reads * gains, 0.0)
        return jnp.sum(product, axis=0, keepdims=True)

    own_last = completion(face_reads(roll(above[1], -3, 0), 1), up[0])
    own_first = completion(face_reads(below[1], -1), roll(down[0], -3, 0))
    far_first = completion(face_reads(up[1], -1), roll(above[0], -3, 0))
    far_last = completion(face_reads(roll(down[1], -3, 0), 1), below[0])
    last = ROWS - 1
    wide[:ROWS, :] = partial[:ROWS, :] - jnp.where(row == 0, own_first, 0.0)
    wide[ROWS : layers - ROWS, :] = partial[ROWS : layers - ROWS, :]
    wide[layers - ROWS : layers, :] = partial[layers - ROWS :, :] + jnp.where(
        row == last, own_last, 0.0
    )
    halo = jnp.where(row < ROWS // 2, above[0], below[0])
    halo = halo - jnp.where(row == 0, far_first, 0.0) + jnp.where(row == last, far_last, 0.0)
    wide[layers:, :] = halo

    halo = unstow(jnp.where(row < ROWS // 2, above[1], below[1]))
    edge = jnp.concatenate([edges[...], halo], axis=0)
    half = edge.shape[1] // 2
    low = outgoing(edge[:, :half], 1)
    high = outgoing(edge[:, half:], -1)
    low_field = roll(wide[:, :128], EDGE - 128, 1)
    high_field = roll(wide[:, columns - 128 :], EDGE - 128 - (128 - 3 * NZ), 1)
    lane = iota(low_field.shape, 1)
    held = (lane >= EDGE - 128) & (lane < EDGE - 128 + 3 * NZ)
    to_left = [low[:, :128], jnp.where(held, low_field, low[:, 128:])]
    to_right = [high[:, :128], jnp.where(held, high_field, high[:, 128:])]
    even_y = (lax.axis_index("gy") & 1) == 0
    for part in range(2):
        lanes = slice(part * 128, part * 128 + 128)
        out_s[:, lanes] = jnp.where(even_y, to_right[part], to_left[part])
        out_z[:, lanes] = jnp.where(even_y, to_left[part], to_right[part])


def hand_on_kernel(first, second, out):
    out[...] = first[...]


def signed_products(reads, gains, way):
    product = reads[:, READS:] * gains[:, :128]
    lane = iota(product.shape, 1)
    for place, k in enumerate(Y_PAIRS):
        if way * PAIRS[k][1] < 0:
            product = jnp.where(block_at(lane, place * NZ), -product, product)
    return product


def fold(first, second):
    lane = iota(first.shape, 1)
    total = jnp.where(lane < 64, first, roll(second, 64, 1))
    total = total + roll(total, -NZ, 1)
    total = total + roll(total, -2 * NZ, 1)
    total = total + jnp.where(lane < 64, roll(first, 64, 1), second)
    low = jnp.where(lane < NZ, total, 0.0)
    return low, jnp.where(lane >= 128 - NZ, roll(total, 64 - NZ, 1), 0.0)


def laplace(field, depth, inside):
    rows, lanes = field.shape
    total = roll(field, 1, 0) + roll(field, -1, 0)
    total = total + (roll(field, NZ, 1) + roll(field, -NZ, 1))
    total = total + jnp.where(depth > 0, roll(field, 1, 1), 0.0)
    total = total + jnp.where(depth < NZ - 1, roll(field, -1, 1), 0.0)
    return jnp.where(inside, field - total * (1.0 / 6.0), 0.0)


def tree_sum(parts):
    while len(parts) > 1:
        half = (len(parts) + 1) // 2
        parts = [
            parts[i] + parts[i + half] if i + half < len(parts) else parts[i] for i in range(half)
        ]
    return parts[0]


def sum_all(value):
    rows, lanes = value.shape
    parts = [
        value[r : r + ROWS, c : c + 128] for r in range(0, rows, ROWS) for c in range(0, lanes, 128)
    ]
    folded = tree_sum(parts)
    return jnp.sum(jnp.sum(folded, axis=0, keepdims=True), axis=1, keepdims=True)


def krylov_kernel(wide, own_s, own_z, got_s, got_z, basis, shares):
    rows, columns = wide.shape
    place = lax.axis_index("gy")
    last_place = lax.axis_size("gy") - 1
    even = (place & 1) == 0

    def pick(first, second):
        return jnp.where(even, first[...], second[...])

    to_right = pick(own_s, own_z)
    to_left = pick(own_z, own_s)
    right = pick(got_s, got_z)
    left = pick(got_z, got_s)
    lane = iota((rows, 128), 1)
    field = wide[...]
    low, high = fold(signed_products(left, to_left, -1), signed_products(right, to_right, 1))
    low_end = field[:, :128] + low
    high_end = field[:, columns - 128 :] + high
    right_halo = jnp.where(lane < 3 * NZ, roll(right[:, 128:], 128 - EDGE, 1), 0.0)
    left_halo = jnp.where(
        lane >= 128 - 3 * NZ, roll(left[:, 128:], 128 - 3 * NZ - (EDGE - 128), 1), 0.0
    )
    low, high = fold(signed_products(to_right, right, -1), signed_products(to_left, left, 1))
    halo = (right_halo + low) + (left_halo + high)
    field = jnp.concatenate([low_end, field[:, 128 : columns - 128], high_end, halo], axis=1)
    column = iota(field.shape, 1)
    depth = column & (NZ - 1)
    on_right = (column < columns + 64) & (place < last_place)
    on_left = (column >= columns + 64) & (place > 0)
    inside = (column < columns) | on_right | on_left
    first = laplace(field, depth, inside)
    second = laplace(first, depth, inside)
    third = laplace(second, depth, inside)
    cores = [v[: basis.shape[1], :columns] for v in (field, first, second, third)]
    for power in range(ITERS):
        basis[power] = cores[power]
    row = jnp.zeros((1, 128), jnp.float32)
    lane = iota((1, 128), 1)
    for index, centre in enumerate(CENTRES):
        vectors = about(cores, centre)
        for power in range(2 * ITERS):
            value = sum_all(vectors[power // 2] * vectors[(power + 1) // 2])
            row = jnp.where(lane == index * 2 * ITERS + power, value, row)
    shares[...] = jnp.broadcast_to(row, shares.shape)


def about(vectors, centre):
    if isinstance(centre, float) and centre == 0.0:
        return list(vectors)
    result = [vectors[0]]
    level = list(vectors)
    while len(level) > 1:
        level = [level[k + 1] - centre * level[k] for k in range(len(level) - 1)]
        result.append(level[0])
    return result


def times_h(poly, centre):
    out = [entry * (1.0 + 6.0 * radius_sq * centre) for entry in poly] + [0.0]
    for power, entry in enumerate(poly):
        out[power + 1] = out[power + 1] + (6.0 * radius_sq) * entry
    return out


def dot_poly(p, q, moments):
    total = 0.0
    for power in range(len(p) + len(q) - 1):
        terms = [p[i] * q[power - i] for i in range(len(p)) if 0 <= power - i < len(q)]
        total = total + tree_sum(terms) * moments[power]
    return total


def entry_of(poly, power):
    return poly[power] if power < len(poly) else 0.0


def combination(moments, centre):
    upper = 1.0 + 12.0 * radius_sq
    growth = (upper - 1.0) ** 2 / (4.0 * upper) * 1.001
    one = jnp.ones_like(moments[0])
    solved, residual, direction = [], [one], [one]
    norm_now = moments[0]
    for iteration in range(ITERS):
        image = times_h(direction, centre)
        step = norm_now / dot_poly(direction, image, moments)
        step = jnp.clip(step, 1.0 / upper, 1.0)
        solved = [entry_of(solved, k) + step * direction[k] for k in range(len(direction))]
        if iteration < ITERS - 1:
            residual = [entry_of(residual, k) - step * image[k] for k in range(len(image))]
            norm_next = jnp.maximum(dot_poly(residual, residual, moments), 0.0)
            ratio = jnp.clip(norm_next / norm_now, 0.0, growth)
            direction = [
                residual[k] + ratio * entry_of(direction, k) for k in range(len(residual))
            ]
            norm_now = norm_next
    return solved


def combine_kernel(shares, basis, filtered):
    count = shares.shape[0]
    total = tree_sum([shares[r : r + ROWS, :] for r in range(0, count, ROWS)])
    total = jnp.sum(total, axis=0, keepdims=True)
    lane = iota(total.shape, 1)
    moments = [
        jnp.sum(jnp.where(lane == place, total, 0.0), axis=1, keepdims=True)
        for place in range(2 * ITERS * len(CENTRES))
    ]
    chosen = moments[: 2 * ITERS]
    centre = jnp.zeros_like(moments[0]) + CENTRES[0]
    for index in range(1, len(CENTRES)):
        border = 0.5 * (CENTRES[index - 1] + CENTRES[index])
        beyond = moments[1] > border * moments[0]
        centre = jnp.where(beyond, CENTRES[index], centre)
        for power in range(2 * ITERS):
            other = moments[index * 2 * ITERS + power]
            chosen[power] = jnp.where(beyond, other, chosen[power])
    weights = combination(chosen, centre)
    vectors = about([basis[power] for power in range(ITERS)], centre)
    result = vectors[0] * weights[0]
    for power in range(1, ITERS):
        result = result + vectors[power] * weights[power]
    filtered[...] = result


def adjoint_kernel(
    forward_far,
    adjoint_far,
    design_far,
    node_far,
    got_s,
    got_z,
    side_s,
    side_z,
    result,
    forward,
    adjoint,
    design,
    node_type,
    adjoint_new,
    sems,
    out_sems,
):
    layers, columns = design.shape
    groups = fetch_tiles(
        (forward_far, adjoint_far, design_far, node_far),
        (forward, adjoint, design, node_type),
        sems,
    )
    sent = []
    tiles = layers // ROWS
    shape = (ROWS, columns)
    even = (lax.axis_index("gx") & 1) == 0
    even_y = (lax.axis_index("gy") & 1) == 0
    faces = slice(ROWS, 2 * ROWS)
    above = jnp.where(even, got_s[faces, :], got_z[faces, :])
    below = jnp.where(even, got_z[faces, :], got_s[faces, :])
    column = iota(shape, 1)
    for tile in range(tiles):
        rows = slice(tile * ROWS, tile * ROWS + ROWS)
        right = jnp.where(even_y, side_s[rows, :], side_z[rows, :])
        left = jnp.where(even_y, side_z[rows, :], side_s[rows, :])
        take(groups, tile)
        density = forward[0, rows, :]
        differences = []
        for k in range(9):
            one, other = forward[2 * k + 1, rows, :], forward[2 * k + 2, rows, :]
            density = density + (one + other)
            differences.append(one - other)
        inverse = 1.0 / density
        velocity = [part * inverse for part in momentum_of(differences)]
        speed_sq = velocity[0] * velocity[0] + velocity[1] * velocity[1]
        speed_sq = speed_sq + velocity[2] * velocity[2]
        kind = node_type[rows, :]
        wall = kind == 1
        source = jnp.where(kind == 2, 1.0, jnp.where(kind == 3, -1.0, 0.0))
        blend = 1.0 - 2.0 * design[rows, :]
        rest = adjoint[0, rows, :]
        zeroth = REST_WEIGHT * rest
        quadratic = None
        vector = [None, None, None]
        kept = []
        for k in range(9):
            reads = []
            for sign in (1, -1):
                step = [sign * c for c in PAIRS[k]]
                member = member_of(k, sign)
                place = X_PAIRS.index(k) if k in X_PAIRS else 0
                read = row_tile(
                    adjoint,
                    member,
                    tile,
                    step[0],
                    above[3 + place : 4 + place, :],
                    below[place : place + 1, :],
                )
                if step[1] or step[2]:
                    read = roll(read, -(step[1] * NZ + step[2]), 1)
                if step[1]:
                    start = READS + Y_PAIRS.index(k) * NZ
                    side = right if step[1] > 0 else left
                    target = columns - NZ if step[1] > 0 else 0
                    part = side[:, start // 128 * 128 : start // 128 * 128 + 128]
                    part = roll(part, target - start, 1)
                    border = column >= columns - NZ if step[1] > 0 else column < NZ
                    spread = jnp.concatenate([part] * (columns // 128), axis=1)
                    read = jnp.where(border, spread, read)
                if step[2]:
                    bounce = adjoint[member_of(k, -sign), rows, :]
                    read = jnp.where(leaves_depth(shape, step[2]), bounce, read)
                reads.append(read)
            both = reads[0] + reads[1]
            odd = blend * (reads[0] - reads[1])
            projected = dot_velocity(PAIRS[k], velocity)
            even_part = WEIGHTS[k] * both
            zeroth = zeroth + even_part
            moved = even_part * projected
            square = moved * projected
            quadratic = square if quadratic is None else quadratic + square
            pull = (3.0 * WEIGHTS[k]) * odd + 9.0 * moved
            for axis in range(3):
                if PAIRS[k][axis]:
                    vector[axis] = (
                        signed_sum([(PAIRS[k][axis], pull)])
                        if vector[axis] is None
                        else signed_sum([(1, vector[axis]), (PAIRS[k][axis], pull)])
                    )
            kept.append((reads[0], reads[1], both, odd))
        scaled = relax_rate * zeroth
        base = scaled * (1.0 + 1.5 * speed_sq) - (4.5 * relax_rate) * quadratic + source
        vector = [
            relax_rate * part - (3.0 * scaled) * speed for part, speed in zip(vector, velocity)
        ]
        keep = relax_rate - 1.0
        adjoint_new[0, rows, :] = jnp.where(wall, rest, base - keep * rest)
        for k in range(9):
            one, other, both, odd = kept[k]
            level = base - (0.5 * keep) * both
            slope = dot_velocity(PAIRS[k], vector) - (0.5 * keep) * odd
            adjoint_new[2 * k + 1, rows, :] = jnp.where(wall, other, level + slope)
            adjoint_new[2 * k + 2, rows, :] = jnp.where(wall, one, level - slope)
        part = pl.ds(tile * ROWS, ROWS)
        sent.append(
            pltpu.make_async_copy(
                adjoint_new.at[:, part, :], result.at[:, part, :], out_sems.at[tile]
            )
        )
        sent[-1].start()
    for copy in sent:
        copy.wait()


def run(kernel, outputs, *operands, flops, far=0, far_out=False, scratch=(), vmem=32):
    sizes = [jax.ShapeDtypeStruct(shape, jnp.float32) for shape in outputs]
    moved = 4 * sum(a.size for a in operands) + 4 * sum(s.size for s in sizes)
    operands = [
        pltpu.with_memory_space_constraint(a, pltpu.HBM) if i < far else a
        for i, a in enumerate(operands)
    ]
    near = pl.BlockSpec(memory_space=pltpu.VMEM)
    away = pl.BlockSpec(memory_space=pl.ANY)
    return pl.pallas_call(
        kernel,
        out_shape=sizes,
        in_specs=[away if i < far else near for i in range(len(operands))],
        out_specs=[away if far_out else near for _ in outputs],
        scratch_shapes=list(scratch),
        compiler_params=pltpu.CompilerParams(vmem_limit_bytes=vmem * 1024 * 1024),
        cost_estimate=pl.CostEstimate(flops=flops, bytes_accessed=moved, transcendentals=0),
    )(*operands)


def swap(first, second, axis, closed):
    count = lax.axis_size(axis)
    starts = range(1, count if closed else count - 1, 2)
    far = [(i, (i + 1) % count) for i in starts]
    far = far + [(b, a) for a, b in far]
    near = [(i, i ^ 1) for i in range(count)]
    return lax.ppermute(first, axis, far), lax.ppermute(second, axis, near)


def shards(forward, adjoint, design, node_type):
    members, layers, columns = adjoint.shape
    sites = layers * columns
    devices = lax.axis_size("gx") * lax.axis_size("gy")
    plane = (layers, columns)
    face = (2 * ROWS, columns)
    side = (layers + ROWS, 256)
    tiles = layers // ROWS
    field = pltpu.VMEM((members,) + plane, jnp.float32)
    end = pltpu.VMEM((members, ROWS, columns), jnp.float32)

    def border(near):
        (message,) = run(
            functools.partial(border_kernel, near),
            [face],
            forward,
            adjoint,
            node_type,
            far=3,
            scratch=[
                end,
                end,
                pltpu.VMEM((ROWS, columns), jnp.int32),
                pltpu.SemaphoreType.DMA((7,)),
            ],
            flops=40 * sites,
        )
        return message

    own_z = border(False)
    own_s = border(True)
    got_z, got_s = swap(own_z, own_s, "gx", True)
    got_z = lax.optimization_barrier(got_z)
    partial, edges = run(
        collide_kernel,
        [plane, (layers, 512)],
        forward,
        adjoint,
        node_type,
        far=3,
        scratch=[
            field,
            field,
            pltpu.VMEM(plane, jnp.int32),
            pltpu.SemaphoreType.DMA((tiles, 3)),
        ],
        flops=150 * sites,
    )
    wide, out_s, out_z = run(
        faces_kernel,
        [(layers + ROWS, columns), side, side],
        partial,
        edges,
        own_s,
        own_z,
        got_s,
        got_z,
        flops=10 * sites,
    )
    side_z, side_s = swap(out_z, out_s, "gy", False)
    side_z = lax.optimization_barrier(side_z)
    basis, shares = run(
        krylov_kernel,
        [(ITERS,) + plane, (devices, 128)],
        wide,
        out_s,
        out_z,
        side_s,
        side_z,
        flops=60 * sites,
    )
    spread = lax.all_to_all(shares.reshape(devices, 1, 128), ("gx", "gy"), 0, 0)
    (adjoint_new,) = run(
        adjoint_kernel,
        [adjoint.shape],
        forward,
        adjoint,
        design,
        node_type,
        got_s,
        got_z,
        side_s,
        side_z,
        far=4,
        far_out=True,
        scratch=[
            field,
            field,
            pltpu.VMEM(plane, jnp.float32),
            pltpu.VMEM(plane, jnp.int32),
            field,
            pltpu.SemaphoreType.DMA((tiles, 4)),
            pltpu.SemaphoreType.DMA((tiles,)),
        ],
        flops=400 * sites,
    )
    (filtered,) = run(
        combine_kernel, [plane], spread.reshape(devices, 128), basis, flops=10 * sites
    )
    return (adjoint_new, filtered)


def solution(mesh):
    placed = (P(None, "gx", "gy"), P(None, "gx", "gy"), P("gx", "gy"), P("gx", "gy"))
    return jax.shard_map(
        shards,
        mesh=mesh,
        in_specs=placed,
        out_specs=(P(None, "gx", "gy"), P("gx", "gy")),
        check_vma=False,
    )
```

```python
import functools

import jax
import jax.numpy as jnp
from jax import lax
from jax.experimental import pallas as pl
from jax.experimental.pallas import tpu as pltpu
from jax.sharding import PartitionSpec as P

NZ = 16
ITERS = 3
PAIRS = (
    (1, 0, 0),
    (0, 1, 0),
    (0, 0, 1),
    (1, 1, 0),
    (1, -1, 0),
    (1, 0, 1),
    (1, 0, -1),
    (0, 1, 1),
    (0, 1, -1),
)
WEIGHTS = (1.0 / 18.0,) * 3 + (1.0 / 36.0,) * 6
REST_WEIGHT = 1.0 / 3.0
X_PAIRS = (0, 3, 4, 5, 6)
Y_PAIRS = (1, 3, 4, 7, 8)
relax_rate = 1.25
radius_sq = 4.0
ROWS = 8
READS = 128
EDGE = 208
SPARE = 80
CENTRES = (0.0, 1.0, 2.0)


def iota(shape, axis):
    return lax.broadcasted_iota(jnp.int32, shape, axis)


def roll(value, shift, axis):
    shift = shift % value.shape[axis]
    return value if shift == 0 else pltpu.roll(value, shift, axis)


def signed_sum(terms):
    total = None
    for sign, value in terms:
        if total is None:
            total = value if sign > 0 else -value
        else:
            total = total + value if sign > 0 else total - value
    return total


def dot_velocity(velocity, vector):
    return signed_sum([(c, v) for c, v in zip(velocity, vector) if c != 0])


def momentum_of(differences):
    return [
        signed_sum([(PAIRS[k][axis], differences[k]) for k in range(9) if PAIRS[k][axis] != 0])
        for axis in range(3)
    ]


def member_of(k, sign):
    return 2 * k + 1 if sign > 0 else 2 * k + 2


def row_tile(ref, member, tile, step, above=None, below=None):
    start = tile * ROWS
    layers = ref.shape[1]
    if step == 0:
        return ref[member, start : start + ROWS, :]
    if 0 <= start + step and start + step + ROWS <= layers:
        return ref[member, start + step : start + step + ROWS, :]
    value = ref[member, start : start + ROWS, :]
    row = iota(value.shape, 0)
    if step > 0:
        return jnp.where(row < ROWS - 1, roll(value, ROWS - 1, 0), 0.0 if above is None else above)
    return jnp.where(row > 0, roll(value, 1, 0), 0.0 if below is None else below)


def slide(value, step_y, step_z):
    columns = value.shape[1]
    if step_y == 0 and step_z == 0:
        return value
    moved = roll(value, -(step_y * NZ + step_z), 1)
    column = iota(value.shape, 1)
    keep = None
    if step_y != 0:
        keep = column < columns - NZ if step_y > 0 else column >= NZ
    if step_z != 0:
        depth = column & (NZ - 1)
        inner = depth < NZ - 1 if step_z > 0 else depth > 0
        keep = inner if keep is None else keep & inner
    return jnp.where(keep, moved, 0.0)


def leaves_depth(shape, step_z):
    depth = iota(shape, 1) & (NZ - 1)
    return depth == NZ - 1 if step_z > 0 else depth == 0


def block_at(lane, start):
    return (lane >= start) & (lane < start + NZ)


def pack_edge(gains, populations, high):
    origin = 0 if not high else 128 - NZ
    shape = (ROWS, 128)
    lane = iota(shape, 1)
    halves = [jnp.zeros(shape, jnp.float32), jnp.zeros(shape, jnp.float32)]
    for half, values in enumerate((gains, populations)):
        for place, value in enumerate(values):
            columns = value.shape[1]
            part = value[:, :128] if not high else value[:, columns - 128 :]
            moved = roll(part, place * NZ - origin, 1)
            halves[half] = jnp.where(block_at(lane, place * NZ), moved, halves[half])
    return jnp.concatenate(halves, axis=1)


def gains_of(forward, kinds):
    differences = [forward(2 * k + 1) - forward(2 * k + 2) for k in range(9)]
    momentum = momentum_of(differences)
    fluid = kinds != 1
    gains = []
    for k in range(9):
        gain = (relax_rate - 1.0) * differences[k]
        gain = gain - (6.0 * relax_rate * WEIGHTS[k]) * dot_velocity(PAIRS[k], momentum)
        gains.append(jnp.where(fluid, gain, 0.0))
    return gains


def inner_sensitivity(gains, rows_of):
    total = None
    for k in range(9):
        reads = []
        for sign in (1, -1):
            step = [sign * c for c in PAIRS[k]]
            read = slide(rows_of(member_of(k, sign), step[0]), step[1], step[2])
            if step[2] != 0:
                bounce = rows_of(member_of(k, -sign), 0)
                read = jnp.where(leaves_depth(read.shape, step[2]), bounce, read)
            reads.append(read)
        term = (reads[0] - reads[1]) * gains[k]
        total = term if total is None else total + term
    return total


def pack_edges(gains, adjoint):
    packed = []
    for high in (False, True):
        way = -1 if high else 1
        populations = [adjoint(member_of(k, way * PAIRS[k][1])) for k in Y_PAIRS]
        packed.append(pack_edge([gains[k] for k in Y_PAIRS], populations, high))
    return jnp.concatenate(packed, axis=1)


def fourth(up, high):
    place = 1 if up == high else 2
    return READS + place * NZ


def stow(edge, up):
    half = edge.shape[1] // 2
    lane = iota((ROWS, half), 1)
    sides = []
    for high in (False, True):
        part = edge[:, half : 2 * half] if high else edge[:, :half]
        below = roll(roll(part, 1, 0), SPARE - fourth(True, high), 1)
        above = roll(roll(part, -1, 0), SPARE - fourth(False, high), 1)
        sides.append(jnp.where(block_at(lane, SPARE), jnp.where(up, below, above), part))
    return jnp.concatenate(sides, axis=1)


def unstow(halo):
    half = halo.shape[1] // 2
    lane = iota((ROWS, half), 1)
    row = iota((ROWS, half), 0)
    sides = []
    for high in (False, True):
        part = halo[:, half : 2 * half] if high else halo[:, :half]
        result = part
        for up, at, step in ((False, 3, 1), (True, 4, -1)):
            start = fourth(up, high)
            moved = roll(roll(part, step, 0), start - SPARE, 1)
            result = jnp.where((row == at) & block_at(lane, start), moved, result)
        sides.append(result)
    return jnp.concatenate(sides, axis=1)


def border_kernel(near, forward, adjoint, node_type, out, moving, carried, kinds, sems):
    layers, columns = node_type.shape
    odd = lax.axis_index("gx") & 1
    up = 1 - odd if near else odd
    half = ROWS // 2
    rows = pl.ds(pl.multiple_of(up * (layers - half), half), half)
    held = pl.ds(pl.multiple_of(up * half, half), half)
    cuts = (1, 7, 13, 19)
    copies = [pltpu.make_async_copy(node_type.at[rows, :], kinds.at[held, :], sems.at[0])]
    for source, target in ((forward, moving), (adjoint, carried)):
        for low, high in zip(cuts, cuts[1:]):
            members = pl.ds(low, high - low)
            copies.append(
                pltpu.make_async_copy(
                    source.at[members, rows, :], target.at[members, held, :], sems.at[len(copies)]
                )
            )
    for copy in copies:
        copy.start()
    for copy in copies[:4]:
        copy.wait()
    gains = gains_of(lambda member: moving[member], kinds[...])
    for copy in copies[4:]:
        copy.wait()
    row = iota((ROWS, columns), 0)

    def rows_of(member, step):
        value = carried[member]
        if step == 0:
            return value
        if step > 0:
            return jnp.where(row < ROWS - 1, roll(value, ROWS - 1, 0), 0.0)
        return jnp.where(row > 0, roll(value, 1, 0), 0.0)

    def border(value):
        return jnp.where(up == 1, value[ROWS - 1 :, :], value[:1, :])

    top = inner_sensitivity(gains, rows_of)
    edge = stow(pack_edges(gains, lambda member: carried[member]), up == 1)
    base = 3 * (1 - up)
    for index, k in enumerate(X_PAIRS):
        top = jnp.where(row == base + index, border(gains[k]), top)
        outward = jnp.where(
            up == 1, carried[2 * k + 2, ROWS - 1 :, :], carried[2 * k + 1, :1, :]
        )
        edge = jnp.where(row == base + index, outward, edge)
    out[:ROWS, :] = top
    out[ROWS:, :] = edge


def fetch_tiles(sources, targets, sems):
    tiles = sources[-1].shape[-2] // ROWS
    groups = []
    for tile in range(tiles):
        rows = pl.ds(tile * ROWS, ROWS)
        group = []
        for index, (source, target) in enumerate(zip(sources, targets)):
            at = (slice(None), rows) if len(source.shape) == 3 else (rows,)
            group.append(
                pltpu.make_async_copy(source.at[at], target.at[at], sems.at[tile, index])
            )
        for copy in group:
            copy.start()
        groups.append(group)
    return groups


def take(groups, tile):
    for ready in ((0, 1) if tile == 0 else (tile + 1,)):
        if ready < len(groups):
            for copy in groups[ready]:
                copy.wait()


def collide_kernel(forward, adjoint, node_type, partial, edges, moving, carried, kinds, sems):
    layers, columns = partial.shape
    groups = fetch_tiles((forward, adjoint, node_type), (moving, carried, kinds), sems)
    for tile in range(layers // ROWS):
        rows = slice(tile * ROWS, tile * ROWS + ROWS)
        take(groups, tile)
        gains = gains_of(lambda member: moving[member, rows, :], kinds[rows, :])
        partial[rows, :] = inner_sensitivity(
            gains, lambda member, step: row_tile(carried, member, tile, step)
        )
        edges[rows, :] = pack_edges(gains, lambda member: carried[member, rows, :])


def face_reads(faces, sign):
    row = iota(faces.shape, 0)
    result = faces
    for place, k in enumerate(X_PAIRS):
        step_y, step_z = sign * PAIRS[k][1], sign * PAIRS[k][2]
        if step_y or step_z:
            result = jnp.where(row == place, slide(faces, step_y, step_z), result)
    return result


def outgoing(edge, way):
    lane = iota(edge.shape, 1)
    result = edge
    for place, k in enumerate(Y_PAIRS):
        sign = way * PAIRS[k][1]
        step_x, step_z = sign * PAIRS[k][0], sign * PAIRS[k][2]
        start = READS + place * NZ
        if step_x:
            result = jnp.where(block_at(lane, start), roll(edge, -step_x, 0), result)
        if step_z:
            moved = jnp.where(leaves_depth(edge.shape, step_z), 0.0, roll(edge, -step_z, 1))
            result = jnp.where(block_at(lane, start), moved, result)
    return result


def faces_kernel(near, partial, edges, own_s, own_z, got_s, got_z, out, wide):
    layers, columns = partial.shape
    even = (lax.axis_index("gx") & 1) == 0

    def pick(first, second, part):
        rows = slice(part * ROWS, part * ROWS + ROWS)
        return jnp.where(even, first[rows, :], second[rows, :])

    up = [pick(own_s, own_z, part) for part in range(2)]
    down = [pick(own_z, own_s, part) for part in range(2)]
    above = [pick(got_s, got_z, part) for part in range(2)]
    below = [pick(got_z, got_s, part) for part in range(2)]
    row = iota((ROWS, columns), 0)

    def completion(reads, gains):
        product = jnp.where(row < len(X_PAIRS), reads * gains, 0.0)
        return jnp.sum(product, axis=0, keepdims=True)

    own_last = completion(face_reads(roll(above[1], -3, 0), 1), up[0])
    own_first = completion(face_reads(below[1], -1), roll(down[0], -3, 0))
    far_first = completion(face_reads(up[1], -1), roll(above[0], -3, 0))
    far_last = completion(face_reads(roll(down[1], -3, 0), 1), below[0])
    last = ROWS - 1
    top = partial[:ROWS, :] - jnp.where(row == 0, own_first, 0.0)
    bottom = partial[layers - ROWS :, :] + jnp.where(row == last, own_last, 0.0)
    halo = jnp.where(row < ROWS // 2, above[0], below[0])
    halo = halo - jnp.where(row == 0, far_first, 0.0) + jnp.where(row == last, far_last, 0.0)
    for start in range(0, columns, 128):
        if near or start in (0, columns - 128):
            lanes = slice(start, start + 128)
            wide[:ROWS, lanes] = top[:, lanes]
            wide[ROWS : layers - ROWS, lanes] = partial[ROWS : layers - ROWS, lanes]
            wide[layers - ROWS : layers, lanes] = bottom[:, lanes]
            wide[layers:, lanes] = halo[:, lanes]

    halo = unstow(jnp.where(row < ROWS // 2, above[1], below[1]))
    edge = jnp.concatenate([edges[...], halo], axis=0)
    half = edge.shape[1] // 2
    low = outgoing(edge[:, :half], 1)
    high = outgoing(edge[:, half:], -1)
    low_field = roll(wide[:, :128], EDGE - 128, 1)
    high_field = roll(wide[:, columns - 128 :], EDGE - 128 - (128 - 3 * NZ), 1)
    lane = iota(low_field.shape, 1)
    held = (lane >= EDGE - 128) & (lane < EDGE - 128 + 3 * NZ)
    to_left = [low[:, :128], jnp.where(held, low_field, low[:, 128:])]
    to_right = [high[:, :128], jnp.where(held, high_field, high[:, 128:])]
    even_y = (lax.axis_index("gy") & 1) == 0
    for part in range(2):
        lanes = slice(part * 128, part * 128 + 128)
        out[:, lanes] = jnp.where(even_y == near, to_right[part], to_left[part])


def hand_on_kernel(first, second, out):
    out[...] = first[...]


def signed_products(reads, gains, way):
    product = reads[:, READS:] * gains[:, :128]
    lane = iota(product.shape, 1)
    for place, k in enumerate(Y_PAIRS):
        if way * PAIRS[k][1] < 0:
            product = jnp.where(block_at(lane, place * NZ), -product, product)
    return product


def fold(first, second):
    lane = iota(first.shape, 1)
    total = jnp.where(lane < 64, first, roll(second, 64, 1))
    total = total + roll(total, -NZ, 1)
    total = total + roll(total, -2 * NZ, 1)
    total = total + jnp.where(lane < 64, roll(first, 64, 1), second)
    low = jnp.where(lane < NZ, total, 0.0)
    return low, jnp.where(lane >= 128 - NZ, roll(total, 64 - NZ, 1), 0.0)


def laplace(field, depth):
    rows, lanes = field.shape
    total = roll(field, 1, 0) + roll(field, -1, 0)
    total = total + (roll(field, NZ, 1) + roll(field, -NZ, 1))
    total = total + jnp.where(depth > 0, roll(field, 1, 1), 0.0)
    total = total + jnp.where(depth < NZ - 1, roll(field, -1, 1), 0.0)
    return field - total * (1.0 / 6.0)


def tree_sum(parts):
    while len(parts) > 1:
        half = (len(parts) + 1) // 2
        parts = [
            parts[i] + parts[i + half] if i + half < len(parts) else parts[i] for i in range(half)
        ]
    return parts[0]


def sum_all(value):
    rows, lanes = value.shape
    parts = [
        value[r : r + ROWS, c : c + 128] for r in range(0, rows, ROWS) for c in range(0, lanes, 128)
    ]
    folded = tree_sum(parts)
    return jnp.sum(jnp.sum(folded, axis=0, keepdims=True), axis=1, keepdims=True)


def krylov_kernel(wide, own_s, own_z, got_s, got_z, basis, shares):
    rows, columns = wide.shape
    place = lax.axis_index("gy")
    last_place = lax.axis_size("gy") - 1
    even = (place & 1) == 0

    def pick(first, second):
        return jnp.where(even, first[...], second[...])

    to_right = pick(own_s, own_z)
    to_left = pick(own_z, own_s)
    right = pick(got_s, got_z)
    left = pick(got_z, got_s)
    lane = iota((rows, 128), 1)
    field = wide[...]
    low, high = fold(signed_products(left, to_left, -1), signed_products(right, to_right, 1))
    low_end = field[:, :128] + low
    high_end = field[:, columns - 128 :] + high
    right_halo = jnp.where(lane < 3 * NZ, roll(right[:, 128:], 128 - EDGE, 1), 0.0)
    left_halo = jnp.where(
        lane >= 128 - 3 * NZ, roll(left[:, 128:], 128 - 3 * NZ - (EDGE - 128), 1), 0.0
    )
    low, high = fold(signed_products(to_right, right, -1), signed_products(to_left, left, 1))
    halo = (right_halo + low) + (left_halo + high)
    field = jnp.concatenate([low_end, field[:, 128 : columns - 128], high_end, halo], axis=1)
    depth = iota(field.shape, 1) & (NZ - 1)
    inside = ((lane < 64) & (place < last_place)) | ((lane >= 64) & (place > 0))

    def within(value):
        halo = jnp.where(inside, value[:, columns:], 0.0)
        return jnp.concatenate([value[:, :columns], halo], axis=1)

    first = within(laplace(field, depth))
    second = within(laplace(first, depth))
    third = laplace(second, depth)
    cores = [v[: basis.shape[1], :columns] for v in (field, first, second, third)]
    for power in range(ITERS):
        basis[power] = cores[power]
    row = jnp.zeros((1, 128), jnp.float32)
    lane = iota((1, 128), 1)
    for index, centre in enumerate(CENTRES):
        vectors = about(cores, centre)
        for power in range(2 * ITERS):
            value = sum_all(vectors[power // 2] * vectors[(power + 1) // 2])
            row = jnp.where(lane == index * 2 * ITERS + power, value, row)
    shares[...] = jnp.broadcast_to(row, shares.shape)


def about(vectors, centre):
    if isinstance(centre, float) and centre == 0.0:
        return list(vectors)
    result = [vectors[0]]
    level = list(vectors)
    while len(level) > 1:
        level = [level[k + 1] - centre * level[k] for k in range(len(level) - 1)]
        result.append(level[0])
    return result


def times_h(poly, centre):
    out = [entry * (1.0 + 6.0 * radius_sq * centre) for entry in poly] + [0.0]
    for power, entry in enumerate(poly):
        out[power + 1] = out[power + 1] + (6.0 * radius_sq) * entry
    return out


def dot_poly(p, q, moments):
    total = 0.0
    for power in range(len(p) + len(q) - 1):
        terms = [p[i] * q[power - i] for i in range(len(p)) if 0 <= power - i < len(q)]
        total = total + tree_sum(terms) * moments[power]
    return total


def entry_of(poly, power):
    return poly[power] if power < len(poly) else 0.0


def combination(moments, centre):
    upper = 1.0 + 12.0 * radius_sq
    growth = (upper - 1.0) ** 2 / (4.0 * upper) * 1.001
    one = jnp.ones_like(moments[0])
    solved, residual, direction = [], [one], [one]
    norm_now = moments[0]
    for iteration in range(ITERS):
        image = times_h(direction, centre)
        step = norm_now / dot_poly(direction, image, moments)
        step = jnp.clip(step, 1.0 / upper, 1.0)
        solved = [entry_of(solved, k) + step * direction[k] for k in range(len(direction))]
        if iteration < ITERS - 1:
            residual = [entry_of(residual, k) - step * image[k] for k in range(len(image))]
            norm_next = jnp.maximum(dot_poly(residual, residual, moments), 0.0)
            ratio = jnp.clip(norm_next / norm_now, 0.0, growth)
            direction = [
                residual[k] + ratio * entry_of(direction, k) for k in range(len(residual))
            ]
            norm_now = norm_next
    return solved


def combine_kernel(shares, basis, filtered):
    count = shares.shape[0]
    total = tree_sum([shares[r : r + ROWS, :] for r in range(0, count, ROWS)])
    total = jnp.sum(total, axis=0, keepdims=True)
    lane = iota(total.shape, 1)
    moments = [
        jnp.sum(jnp.where(lane == place, total, 0.0), axis=1, keepdims=True)
        for place in range(2 * ITERS * len(CENTRES))
    ]
    chosen = moments[: 2 * ITERS]
    centre = jnp.zeros_like(moments[0]) + CENTRES[0]
    for index in range(1, len(CENTRES)):
        border = 0.5 * (CENTRES[index - 1] + CENTRES[index])
        beyond = moments[1] > border * moments[0]
        centre = jnp.where(beyond, CENTRES[index], centre)
        for power in range(2 * ITERS):
            other = moments[index * 2 * ITERS + power]
            chosen[power] = jnp.where(beyond, other, chosen[power])
    weights = combination(chosen, centre)
    vectors = about([basis[power] for power in range(ITERS)], centre)
    result = vectors[0] * weights[0]
    for power in range(1, ITERS):
        result = result + vectors[power] * weights[power]
    filtered[...] = result


def adjoint_kernel(
    forward_far,
    adjoint_far,
    design_far,
    node_far,
    got_s,
    got_z,
    side_s,
    side_z,
    result,
    forward,
    adjoint,
    design,
    node_type,
    adjoint_new,
    sems,
    out_sems,
):
    layers, columns = design.shape
    groups = fetch_tiles(
        (forward_far, adjoint_far, design_far, node_far),
        (forward, adjoint, design, node_type),
        sems,
    )
    sent = []
    tiles = layers // ROWS
    shape = (ROWS, columns)
    even = (lax.axis_index("gx") & 1) == 0
    even_y = (lax.axis_index("gy") & 1) == 0
    faces = slice(ROWS, 2 * ROWS)
    above = jnp.where(even, got_s[faces, :], got_z[faces, :])
    below = jnp.where(even, got_z[faces, :], got_s[faces, :])
    column = iota(shape, 1)
    for tile in range(tiles):
        rows = slice(tile * ROWS, tile * ROWS + ROWS)
        right = jnp.where(even_y, side_s[rows, :], side_z[rows, :])
        left = jnp.where(even_y, side_z[rows, :], side_s[rows, :])
        take(groups, tile)
        density = forward[0, rows, :]
        differences = []
        for k in range(9):
            one, other = forward[2 * k + 1, rows, :], forward[2 * k + 2, rows, :]
            density = density + (one + other)
            differences.append(one - other)
        inverse = 1.0 / density
        velocity = [part * inverse for part in momentum_of(differences)]
        speed_sq = velocity[0] * velocity[0] + velocity[1] * velocity[1]
        speed_sq = speed_sq + velocity[2] * velocity[2]
        kind = node_type[rows, :]
        wall = kind == 1
        source = jnp.where(kind == 2, 1.0, jnp.where(kind == 3, -1.0, 0.0))
        blend = 1.0 - 2.0 * design[rows, :]
        rest = adjoint[0, rows, :]
        zeroth = REST_WEIGHT * rest
        quadratic = None
        vector = [None, None, None]
        kept = []
        for k in range(9):
            reads = []
            for sign in (1, -1):
                step = [sign * c for c in PAIRS[k]]
                member = member_of(k, sign)
                place = X_PAIRS.index(k) if k in X_PAIRS else 0
                read = row_tile(
                    adjoint,
                    member,
                    tile,
                    step[0],
                    above[3 + place : 4 + place, :],
                    below[place : place + 1, :],
                )
                if step[1] or step[2]:
                    read = roll(read, -(step[1] * NZ + step[2]), 1)
                if step[1]:
                    start = READS + Y_PAIRS.index(k) * NZ
                    side = right if step[1] > 0 else left
                    target = columns - NZ if step[1] > 0 else 0
                    part = side[:, start // 128 * 128 : start // 128 * 128 + 128]
                    part = roll(part, target - start, 1)
                    border = column >= columns - NZ if step[1] > 0 else column < NZ
                    spread = jnp.concatenate([part] * (columns // 128), axis=1)
                    read = jnp.where(border, spread, read)
                if step[2]:
                    bounce = adjoint[member_of(k, -sign), rows, :]
                    read = jnp.where(leaves_depth(shape, step[2]), bounce, read)
                reads.append(read)
            both = reads[0] + reads[1]
            odd = blend * (reads[0] - reads[1])
            projected = dot_velocity(PAIRS[k], velocity)
            even_part = WEIGHTS[k] * both
            zeroth = zeroth + even_part
            moved = even_part * projected
            square = moved * projected
            quadratic = square if quadratic is None else quadratic + square
            pull = (3.0 * WEIGHTS[k]) * odd + 9.0 * moved
            for axis in range(3):
                if PAIRS[k][axis]:
                    vector[axis] = (
                        signed_sum([(PAIRS[k][axis], pull)])
                        if vector[axis] is None
                        else signed_sum([(1, vector[axis]), (PAIRS[k][axis], pull)])
                    )
            kept.append((reads[0], reads[1], both, odd))
        scaled = relax_rate * zeroth
        base = scaled * (1.0 + 1.5 * speed_sq) - (4.5 * relax_rate) * quadratic + source
        vector = [
            relax_rate * part - (3.0 * scaled) * speed for part, speed in zip(vector, velocity)
        ]
        keep = relax_rate - 1.0
        adjoint_new[0, rows, :] = jnp.where(wall, rest, base - keep * rest)
        for k in range(9):
            one, other, both, odd = kept[k]
            level = base - (0.5 * keep) * both
            slope = dot_velocity(PAIRS[k], vector) - (0.5 * keep) * odd
            adjoint_new[2 * k + 1, rows, :] = jnp.where(wall, other, level + slope)
            adjoint_new[2 * k + 2, rows, :] = jnp.where(wall, one, level - slope)
        part = pl.ds(tile * ROWS, ROWS)
        sent.append(
            pltpu.make_async_copy(
                adjoint_new.at[:, part, :], result.at[:, part, :], out_sems.at[tile]
            )
        )
        sent[-1].start()
    for copy in sent:
        copy.wait()


def run(kernel, outputs, *operands, flops, far=0, far_out=False, scratch=(), vmem=32):
    sizes = [jax.ShapeDtypeStruct(shape, jnp.float32) for shape in outputs]
    moved = 4 * sum(a.size for a in operands) + 4 * sum(s.size for s in sizes)
    operands = [
        pltpu.with_memory_space_constraint(a, pltpu.HBM) if i < far else a
        for i, a in enumerate(operands)
    ]
    near = pl.BlockSpec(memory_space=pltpu.VMEM)
    away = pl.BlockSpec(memory_space=pl.ANY)
    return pl.pallas_call(
        kernel,
        out_shape=sizes,
        in_specs=[away if i < far else near for i in range(len(operands))],
        out_specs=[away if far_out else near for _ in outputs],
        scratch_shapes=list(scratch),
        compiler_params=pltpu.CompilerParams(vmem_limit_bytes=vmem * 1024 * 1024),
        cost_estimate=pl.CostEstimate(flops=flops, bytes_accessed=moved, transcendentals=0),
    )(*operands)


def swap(first, second, axis, closed):
    count = lax.axis_size(axis)
    starts = range(1, count if closed else count - 1, 2)
    far = [(i, (i + 1) % count) for i in starts]
    far = far + [(b, a) for a, b in far]
    near = [(i, i ^ 1) for i in range(count)]
    return lax.ppermute(first, axis, far), lax.ppermute(second, axis, near)


def shards(forward, adjoint, design, node_type):
    members, layers, columns = adjoint.shape
    sites = layers * columns
    devices = lax.axis_size("gx") * lax.axis_size("gy")
    plane = (layers, columns)
    face = (2 * ROWS, columns)
    side = (layers + ROWS, 256)
    tiles = layers // ROWS
    field = pltpu.VMEM((members,) + plane, jnp.float32)
    end = pltpu.VMEM((members, ROWS, columns), jnp.float32)

    def border(near):
        (message,) = run(
            functools.partial(border_kernel, near),
            [face],
            forward,
            adjoint,
            node_type,
            far=3,
            scratch=[
                end,
                end,
                pltpu.VMEM((ROWS, columns), jnp.int32),
                pltpu.SemaphoreType.DMA((7,)),
            ],
            flops=40 * sites,
        )
        return message

    own_z = border(False)
    own_s = border(True)
    got_z, got_s = swap(own_z, own_s, "gx", True)
    got_z = lax.optimization_barrier(got_z)
    partial, edges = run(
        collide_kernel,
        [plane, (layers, 512)],
        forward,
        adjoint,
        node_type,
        far=3,
        scratch=[
            field,
            field,
            pltpu.VMEM(plane, jnp.int32),
            pltpu.SemaphoreType.DMA((tiles, 3)),
        ],
        flops=150 * sites,
    )
    given = (partial, edges, own_s, own_z, got_s, got_z)
    across = (layers + ROWS, columns)
    (out_z,) = run(
        functools.partial(faces_kernel, False),
        [side],
        *given,
        scratch=[pltpu.VMEM(across, jnp.float32)],
        flops=10 * sites,
    )
    out_s, wide = run(
        functools.partial(faces_kernel, True), [side, across], *given, flops=10 * sites
    )
    side_z, side_s = swap(out_z, out_s, "gy", False)
    side_z = lax.optimization_barrier(side_z)
    basis, shares = run(
        krylov_kernel,
        [(ITERS,) + plane, (devices, 128)],
        wide,
        out_s,
        out_z,
        side_s,
        side_z,
        flops=60 * sites,
    )
    spread = lax.all_to_all(shares.reshape(devices, 1, 128), ("gx", "gy"), 0, 0)
    (adjoint_new,) = run(
        adjoint_kernel,
        [adjoint.shape],
        forward,
        adjoint,
        design,
        node_type,
        got_s,
        got_z,
        side_s,
        side_z,
        far=4,
        far_out=True,
        scratch=[
            field,
            field,
            pltpu.VMEM(plane, jnp.float32),
            pltpu.VMEM(plane, jnp.int32),
            field,
            pltpu.SemaphoreType.DMA((tiles, 4)),
            pltpu.SemaphoreType.DMA((tiles,)),
        ],
        flops=400 * sites,
    )
    (filtered,) = run(
        combine_kernel, [plane], spread.reshape(devices, 128), basis, flops=10 * sites
    )
    return (adjoint_new, filtered)


def solution(mesh):
    placed = (P(None, "gx", "gy"), P(None, "gx", "gy"), P("gx", "gy"), P("gx", "gy"))
    return jax.shard_map(
        shards,
        mesh=mesh,
        in_specs=placed,
        out_specs=(P(None, "gx", "gy"), P("gx", "gy")),
        check_vma=False,
    )
```

```python
import functools

import jax
import jax.numpy as jnp
from jax import lax
from jax.experimental import pallas as pl
from jax.experimental.pallas import tpu as pltpu
from jax.sharding import PartitionSpec as P

NZ = 16
ITERS = 3
PAIRS = (
    (1, 0, 0),
    (0, 1, 0),
    (0, 0, 1),
    (1, 1, 0),
    (1, -1, 0),
    (1, 0, 1),
    (1, 0, -1),
    (0, 1, 1),
    (0, 1, -1),
)
WEIGHTS = (1.0 / 18.0,) * 3 + (1.0 / 36.0,) * 6
REST_WEIGHT = 1.0 / 3.0
X_PAIRS = (0, 3, 4, 5, 6)
Y_PAIRS = (1, 3, 4, 7, 8)
relax_rate = 1.25
radius_sq = 4.0
ROWS = 8
READS = 128
EDGE = 208
SPARE = 80
CENTRES = (0.0, 1.0, 2.0)


def iota(shape, axis):
    return lax.broadcasted_iota(jnp.int32, shape, axis)


def roll(value, shift, axis):
    shift = shift % value.shape[axis]
    return value if shift == 0 else pltpu.roll(value, shift, axis)


def signed_sum(terms):
    total = None
    for sign, value in terms:
        if total is None:
            total = value if sign > 0 else -value
        else:
            total = total + value if sign > 0 else total - value
    return total


def dot_velocity(velocity, vector):
    return signed_sum([(c, v) for c, v in zip(velocity, vector) if c != 0])


def momentum_of(differences):
    return [
        signed_sum([(PAIRS[k][axis], differences[k]) for k in range(9) if PAIRS[k][axis] != 0])
        for axis in range(3)
    ]


def member_of(k, sign):
    return 2 * k + 1 if sign > 0 else 2 * k + 2


def row_tile(ref, member, tile, step, above=None, below=None):
    start = tile * ROWS
    layers = ref.shape[1]
    if step == 0:
        return ref[member, start : start + ROWS, :]
    if 0 <= start + step and start + step + ROWS <= layers:
        return ref[member, start + step : start + step + ROWS, :]
    value = ref[member, start : start + ROWS, :]
    row = iota(value.shape, 0)
    if step > 0:
        return jnp.where(row < ROWS - 1, roll(value, ROWS - 1, 0), 0.0 if above is None else above)
    return jnp.where(row > 0, roll(value, 1, 0), 0.0 if below is None else below)


def slide(value, step_y, step_z):
    columns = value.shape[1]
    if step_y == 0 and step_z == 0:
        return value
    moved = roll(value, -(step_y * NZ + step_z), 1)
    column = iota(value.shape, 1)
    keep = None
    if step_y != 0:
        keep = column < columns - NZ if step_y > 0 else column >= NZ
    if step_z != 0:
        depth = column & (NZ - 1)
        inner = depth < NZ - 1 if step_z > 0 else depth > 0
        keep = inner if keep is None else keep & inner
    return jnp.where(keep, moved, 0.0)


def leaves_depth(shape, step_z):
    depth = iota(shape, 1) & (NZ - 1)
    return depth == NZ - 1 if step_z > 0 else depth == 0


def block_at(lane, start):
    return (lane >= start) & (lane < start + NZ)


def pack_edge(gains, populations, high):
    origin = 0 if not high else 128 - NZ
    shape = (ROWS, 128)
    lane = iota(shape, 1)
    halves = [jnp.zeros(shape, jnp.float32), jnp.zeros(shape, jnp.float32)]
    for half, values in enumerate((gains, populations)):
        for place, value in enumerate(values):
            columns = value.shape[1]
            part = value[:, :128] if not high else value[:, columns - 128 :]
            moved = roll(part, place * NZ - origin, 1)
            halves[half] = jnp.where(block_at(lane, place * NZ), moved, halves[half])
    return jnp.concatenate(halves, axis=1)


def gains_of(forward, kinds):
    differences = [forward(2 * k + 1) - forward(2 * k + 2) for k in range(9)]
    momentum = momentum_of(differences)
    fluid = kinds != 1
    gains = []
    for k in range(9):
        gain = (relax_rate - 1.0) * differences[k]
        gain = gain - (6.0 * relax_rate * WEIGHTS[k]) * dot_velocity(PAIRS[k], momentum)
        gains.append(jnp.where(fluid, gain, 0.0))
    return gains


def inner_sensitivity(gains, rows_of):
    total = None
    for k in range(9):
        reads = []
        for sign in (1, -1):
            step = [sign * c for c in PAIRS[k]]
            read = slide(rows_of(member_of(k, sign), step[0]), step[1], step[2])
            if step[2] != 0:
                bounce = rows_of(member_of(k, -sign), 0)
                read = jnp.where(leaves_depth(read.shape, step[2]), bounce, read)
            reads.append(read)
        term = (reads[0] - reads[1]) * gains[k]
        total = term if total is None else total + term
    return total


def pack_edges(gains, adjoint):
    packed = []
    for high in (False, True):
        way = -1 if high else 1
        populations = [adjoint(member_of(k, way * PAIRS[k][1])) for k in Y_PAIRS]
        packed.append(pack_edge([gains[k] for k in Y_PAIRS], populations, high))
    return jnp.concatenate(packed, axis=1)


def fourth(up, high):
    place = 1 if up == high else 2
    return READS + place * NZ


def stow(edge, up):
    half = edge.shape[1] // 2
    lane = iota((ROWS, half), 1)
    sides = []
    for high in (False, True):
        part = edge[:, half : 2 * half] if high else edge[:, :half]
        below = roll(roll(part, 1, 0), SPARE - fourth(True, high), 1)
        above = roll(roll(part, -1, 0), SPARE - fourth(False, high), 1)
        sides.append(jnp.where(block_at(lane, SPARE), jnp.where(up, below, above), part))
    return jnp.concatenate(sides, axis=1)


def unstow(halo):
    half = halo.shape[1] // 2
    lane = iota((ROWS, half), 1)
    row = iota((ROWS, half), 0)
    sides = []
    for high in (False, True):
        part = halo[:, half : 2 * half] if high else halo[:, :half]
        result = part
        for up, at, step in ((False, 3, 1), (True, 4, -1)):
            start = fourth(up, high)
            moved = roll(roll(part, step, 0), start - SPARE, 1)
            result = jnp.where((row == at) & block_at(lane, start), moved, result)
        sides.append(result)
    return jnp.concatenate(sides, axis=1)


def border_kernel(near, forward, adjoint, node_type, out, moving, carried, kinds, sems):
    layers, columns = node_type.shape
    odd = lax.axis_index("gx") & 1
    up = 1 - odd if near else odd
    half = ROWS // 2
    rows = pl.ds(pl.multiple_of(up * (layers - half), half), half)
    held = pl.ds(pl.multiple_of(up * half, half), half)
    cuts = (1, 7, 13, 19)
    copies = [pltpu.make_async_copy(node_type.at[rows, :], kinds.at[held, :], sems.at[0])]
    for source, target in ((forward, moving), (adjoint, carried)):
        for low, high in zip(cuts, cuts[1:]):
            members = pl.ds(low, high - low)
            copies.append(
                pltpu.make_async_copy(
                    source.at[members, rows, :], target.at[members, held, :], sems.at[len(copies)]
                )
            )
    for copy in copies:
        copy.start()
    for copy in copies[:4]:
        copy.wait()
    gains = gains_of(lambda member: moving[member], kinds[...])
    for copy in copies[4:]:
        copy.wait()
    row = iota((ROWS, columns), 0)

    def rows_of(member, step):
        value = carried[member]
        if step == 0:
            return value
        if step > 0:
            return jnp.where(row < ROWS - 1, roll(value, ROWS - 1, 0), 0.0)
        return jnp.where(row > 0, roll(value, 1, 0), 0.0)

    def border(value):
        return jnp.where(up == 1, value[ROWS - 1 :, :], value[:1, :])

    top = inner_sensitivity(gains, rows_of)
    edge = stow(pack_edges(gains, lambda member: carried[member]), up == 1)
    base = 3 * (1 - up)
    for index, k in enumerate(X_PAIRS):
        top = jnp.where(row == base + index, border(gains[k]), top)
        outward = jnp.where(
            up == 1, carried[2 * k + 2, ROWS - 1 :, :], carried[2 * k + 1, :1, :]
        )
        edge = jnp.where(row == base + index, outward, edge)
    out[:ROWS, :] = top
    out[ROWS:, :] = edge


def fetch_tiles(sources, targets, sems):
    tiles = sources[-1].shape[-2] // ROWS
    groups = []
    for tile in range(tiles):
        rows = pl.ds(tile * ROWS, ROWS)
        group = []
        for index, (source, target) in enumerate(zip(sources, targets)):
            at = (slice(None), rows) if len(source.shape) == 3 else (rows,)
            group.append(
                pltpu.make_async_copy(source.at[at], target.at[at], sems.at[tile, index])
            )
        for copy in group:
            copy.start()
        groups.append(group)
    return groups


def take(groups, tile):
    for ready in ((0, 1) if tile == 0 else (tile + 1,)):
        if ready < len(groups):
            for copy in groups[ready]:
                copy.wait()


def collide_kernel(forward, adjoint, node_type, partial, edges):
    layers, columns = partial.shape
    for tile in range(layers // ROWS):
        rows = slice(tile * ROWS, tile * ROWS + ROWS)
        gains = gains_of(lambda member: forward[member, rows, :], node_type[rows, :])
        partial[rows, :] = inner_sensitivity(
            gains, lambda member, step: row_tile(adjoint, member, tile, step)
        )
        edges[rows, :] = pack_edges(gains, lambda member: adjoint[member, rows, :])


def face_reads(faces, sign):
    row = iota(faces.shape, 0)
    result = faces
    for place, k in enumerate(X_PAIRS):
        step_y, step_z = sign * PAIRS[k][1], sign * PAIRS[k][2]
        if step_y or step_z:
            result = jnp.where(row == place, slide(faces, step_y, step_z), result)
    return result


def outgoing(edge, way):
    lane = iota(edge.shape, 1)
    result = edge
    for place, k in enumerate(Y_PAIRS):
        sign = way * PAIRS[k][1]
        step_x, step_z = sign * PAIRS[k][0], sign * PAIRS[k][2]
        start = READS + place * NZ
        if step_x:
            result = jnp.where(block_at(lane, start), roll(edge, -step_x, 0), result)
        if step_z:
            moved = jnp.where(leaves_depth(edge.shape, step_z), 0.0, roll(edge, -step_z, 1))
            result = jnp.where(block_at(lane, start), moved, result)
    return result


def faces_kernel(near, partial, edges, own_s, own_z, got_s, got_z, out, wide):
    layers, columns = partial.shape
    even = (lax.axis_index("gx") & 1) == 0

    def pick(first, second, part):
        rows = slice(part * ROWS, part * ROWS + ROWS)
        return jnp.where(even, first[rows, :], second[rows, :])

    up = [pick(own_s, own_z, part) for part in range(2)]
    down = [pick(own_z, own_s, part) for part in range(2)]
    above = [pick(got_s, got_z, part) for part in range(2)]
    below = [pick(got_z, got_s, part) for part in range(2)]
    row = iota((ROWS, columns), 0)

    def completion(reads, gains):
        product = jnp.where(row < len(X_PAIRS), reads * gains, 0.0)
        return jnp.sum(product, axis=0, keepdims=True)

    own_last = completion(face_reads(roll(above[1], -3, 0), 1), up[0])
    own_first = completion(face_reads(below[1], -1), roll(down[0], -3, 0))
    far_first = completion(face_reads(up[1], -1), roll(above[0], -3, 0))
    far_last = completion(face_reads(roll(down[1], -3, 0), 1), below[0])
    last = ROWS - 1
    top = partial[:ROWS, :] - jnp.where(row == 0, own_first, 0.0)
    bottom = partial[layers - ROWS :, :] + jnp.where(row == last, own_last, 0.0)
    halo = jnp.where(row < ROWS // 2, above[0], below[0])
    halo = halo - jnp.where(row == 0, far_first, 0.0) + jnp.where(row == last, far_last, 0.0)
    for start in range(0, columns, 128):
        if near or start in (0, columns - 128):
            lanes = slice(start, start + 128)
            wide[:ROWS, lanes] = top[:, lanes]
            wide[ROWS : layers - ROWS, lanes] = partial[ROWS : layers - ROWS, lanes]
            wide[layers - ROWS : layers, lanes] = bottom[:, lanes]
            wide[layers:, lanes] = halo[:, lanes]

    halo = unstow(jnp.where(row < ROWS // 2, above[1], below[1]))
    edge = jnp.concatenate([edges[...], halo], axis=0)
    half = edge.shape[1] // 2
    low = outgoing(edge[:, :half], 1)
    high = outgoing(edge[:, half:], -1)
    low_field = roll(wide[:, :128], EDGE - 128, 1)
    high_field = roll(wide[:, columns - 128 :], EDGE - 128 - (128 - 3 * NZ), 1)
    lane = iota(low_field.shape, 1)
    held = (lane >= EDGE - 128) & (lane < EDGE - 128 + 3 * NZ)
    to_left = [low[:, :128], jnp.where(held, low_field, low[:, 128:])]
    to_right = [high[:, :128], jnp.where(held, high_field, high[:, 128:])]
    even_y = (lax.axis_index("gy") & 1) == 0
    for part in range(2):
        lanes = slice(part * 128, part * 128 + 128)
        out[:, lanes] = jnp.where(even_y == near, to_right[part], to_left[part])


def hand_on_kernel(first, second, out):
    out[...] = first[...]


def signed_products(reads, gains, way):
    product = reads[:, READS:] * gains[:, :128]
    lane = iota(product.shape, 1)
    for place, k in enumerate(Y_PAIRS):
        if way * PAIRS[k][1] < 0:
            product = jnp.where(block_at(lane, place * NZ), -product, product)
    return product


def fold(first, second):
    lane = iota(first.shape, 1)
    total = jnp.where(lane < 64, first, roll(second, 64, 1))
    total = total + roll(total, -NZ, 1)
    total = total + roll(total, -2 * NZ, 1)
    total = total + jnp.where(lane < 64, roll(first, 64, 1), second)
    low = jnp.where(lane < NZ, total, 0.0)
    return low, jnp.where(lane >= 128 - NZ, roll(total, 64 - NZ, 1), 0.0)


def laplace(field, depth):
    rows, lanes = field.shape
    total = roll(field, 1, 0) + roll(field, -1, 0)
    total = total + (roll(field, NZ, 1) + roll(field, -NZ, 1))
    total = total + jnp.where(depth > 0, roll(field, 1, 1), 0.0)
    total = total + jnp.where(depth < NZ - 1, roll(field, -1, 1), 0.0)
    return field - total * (1.0 / 6.0)


def tree_sum(parts):
    while len(parts) > 1:
        half = (len(parts) + 1) // 2
        parts = [
            parts[i] + parts[i + half] if i + half < len(parts) else parts[i] for i in range(half)
        ]
    return parts[0]


def sum_all(value):
    rows, lanes = value.shape
    parts = [
        value[r : r + ROWS, c : c + 128] for r in range(0, rows, ROWS) for c in range(0, lanes, 128)
    ]
    folded = tree_sum(parts)
    return jnp.sum(jnp.sum(folded, axis=0, keepdims=True), axis=1, keepdims=True)


def krylov_kernel(wide, own_s, own_z, got_s, got_z, basis, shares):
    rows, columns = wide.shape
    place = lax.axis_index("gy")
    last_place = lax.axis_size("gy") - 1
    even = (place & 1) == 0

    def pick(first, second):
        return jnp.where(even, first[...], second[...])

    to_right = pick(own_s, own_z)
    to_left = pick(own_z, own_s)
    right = pick(got_s, got_z)
    left = pick(got_z, got_s)
    lane = iota((rows, 128), 1)
    field = wide[...]
    low, high = fold(signed_products(left, to_left, -1), signed_products(right, to_right, 1))
    low_end = field[:, :128] + low
    high_end = field[:, columns - 128 :] + high
    right_halo = jnp.where(lane < 3 * NZ, roll(right[:, 128:], 128 - EDGE, 1), 0.0)
    left_halo = jnp.where(
        lane >= 128 - 3 * NZ, roll(left[:, 128:], 128 - 3 * NZ - (EDGE - 128), 1), 0.0
    )
    low, high = fold(signed_products(to_right, right, -1), signed_products(to_left, left, 1))
    halo = (right_halo + low) + (left_halo + high)
    field = jnp.concatenate([low_end, field[:, 128 : columns - 128], high_end, halo], axis=1)
    depth = iota(field.shape, 1) & (NZ - 1)
    inside = ((lane < 64) & (place < last_place)) | ((lane >= 64) & (place > 0))

    def within(value):
        halo = jnp.where(inside, value[:, columns:], 0.0)
        return jnp.concatenate([value[:, :columns], halo], axis=1)

    first = within(laplace(field, depth))
    second = within(laplace(first, depth))
    third = laplace(second, depth)
    cores = [v[: basis.shape[1], :columns] for v in (field, first, second, third)]
    for power in range(ITERS):
        basis[power] = cores[power]
    row = jnp.zeros((1, 128), jnp.float32)
    lane = iota((1, 128), 1)
    for index, centre in enumerate(CENTRES):
        vectors = about(cores, centre)
        for power in range(2 * ITERS):
            value = sum_all(vectors[power // 2] * vectors[(power + 1) // 2])
            row = jnp.where(lane == index * 2 * ITERS + power, value, row)
    shares[...] = jnp.broadcast_to(row, shares.shape)


def about(vectors, centre):
    if isinstance(centre, float) and centre == 0.0:
        return list(vectors)
    result = [vectors[0]]
    level = list(vectors)
    while len(level) > 1:
        level = [level[k + 1] - centre * level[k] for k in range(len(level) - 1)]
        result.append(level[0])
    return result


def times_h(poly, centre):
    out = [entry * (1.0 + 6.0 * radius_sq * centre) for entry in poly] + [0.0]
    for power, entry in enumerate(poly):
        out[power + 1] = out[power + 1] + (6.0 * radius_sq) * entry
    return out


def dot_poly(p, q, moments):
    total = 0.0
    for power in range(len(p) + len(q) - 1):
        terms = [p[i] * q[power - i] for i in range(len(p)) if 0 <= power - i < len(q)]
        total = total + tree_sum(terms) * moments[power]
    return total


def entry_of(poly, power):
    return poly[power] if power < len(poly) else 0.0


def combination(moments, centre):
    upper = 1.0 + 12.0 * radius_sq
    growth = (upper - 1.0) ** 2 / (4.0 * upper) * 1.001
    one = jnp.ones_like(moments[0])
    solved, residual, direction = [], [one], [one]
    norm_now = moments[0]
    for iteration in range(ITERS):
        image = times_h(direction, centre)
        step = norm_now / dot_poly(direction, image, moments)
        step = jnp.clip(step, 1.0 / upper, 1.0)
        solved = [entry_of(solved, k) + step * direction[k] for k in range(len(direction))]
        if iteration < ITERS - 1:
            residual = [entry_of(residual, k) - step * image[k] for k in range(len(image))]
            norm_next = jnp.maximum(dot_poly(residual, residual, moments), 0.0)
            ratio = jnp.clip(norm_next / norm_now, 0.0, growth)
            direction = [
                residual[k] + ratio * entry_of(direction, k) for k in range(len(residual))
            ]
            norm_now = norm_next
    return solved


def combine_kernel(shares, basis, filtered):
    count = shares.shape[0]
    total = tree_sum([shares[r : r + ROWS, :] for r in range(0, count, ROWS)])
    total = jnp.sum(total, axis=0, keepdims=True)
    lane = iota(total.shape, 1)
    moments = [
        jnp.sum(jnp.where(lane == place, total, 0.0), axis=1, keepdims=True)
        for place in range(2 * ITERS * len(CENTRES))
    ]
    chosen = moments[: 2 * ITERS]
    centre = jnp.zeros_like(moments[0]) + CENTRES[0]
    for index in range(1, len(CENTRES)):
        border = 0.5 * (CENTRES[index - 1] + CENTRES[index])
        beyond = moments[1] > border * moments[0]
        centre = jnp.where(beyond, CENTRES[index], centre)
        for power in range(2 * ITERS):
            other = moments[index * 2 * ITERS + power]
            chosen[power] = jnp.where(beyond, other, chosen[power])
    weights = combination(chosen, centre)
    vectors = about([basis[power] for power in range(ITERS)], centre)
    result = vectors[0] * weights[0]
    for power in range(1, ITERS):
        result = result + vectors[power] * weights[power]
    filtered[...] = result


def adjoint_kernel(
    forward_far,
    adjoint_far,
    design_far,
    node_far,
    got_s,
    got_z,
    side_s,
    side_z,
    result,
    forward,
    adjoint,
    design,
    node_type,
    adjoint_new,
    sems,
    out_sems,
):
    layers, columns = design.shape
    groups = fetch_tiles(
        (forward_far, adjoint_far, design_far, node_far),
        (forward, adjoint, design, node_type),
        sems,
    )
    sent = []
    tiles = layers // ROWS
    shape = (ROWS, columns)
    even = (lax.axis_index("gx") & 1) == 0
    even_y = (lax.axis_index("gy") & 1) == 0
    faces = slice(ROWS, 2 * ROWS)
    above = jnp.where(even, got_s[faces, :], got_z[faces, :])
    below = jnp.where(even, got_z[faces, :], got_s[faces, :])
    column = iota(shape, 1)
    for tile in range(tiles):
        rows = slice(tile * ROWS, tile * ROWS + ROWS)
        right = jnp.where(even_y, side_s[rows, :], side_z[rows, :])
        left = jnp.where(even_y, side_z[rows, :], side_s[rows, :])
        take(groups, tile)
        density = forward[0, rows, :]
        differences = []
        for k in range(9):
            one, other = forward[2 * k + 1, rows, :], forward[2 * k + 2, rows, :]
            density = density + (one + other)
            differences.append(one - other)
        inverse = 1.0 / density
        velocity = [part * inverse for part in momentum_of(differences)]
        speed_sq = velocity[0] * velocity[0] + velocity[1] * velocity[1]
        speed_sq = speed_sq + velocity[2] * velocity[2]
        kind = node_type[rows, :]
        wall = kind == 1
        source = jnp.where(kind == 2, 1.0, jnp.where(kind == 3, -1.0, 0.0))
        blend = 1.0 - 2.0 * design[rows, :]
        rest = adjoint[0, rows, :]
        zeroth = REST_WEIGHT * rest
        quadratic = None
        vector = [None, None, None]
        kept = []
        for k in range(9):
            reads = []
            for sign in (1, -1):
                step = [sign * c for c in PAIRS[k]]
                member = member_of(k, sign)
                place = X_PAIRS.index(k) if k in X_PAIRS else 0
                read = row_tile(
                    adjoint,
                    member,
                    tile,
                    step[0],
                    above[3 + place : 4 + place, :],
                    below[place : place + 1, :],
                )
                if step[1] or step[2]:
                    read = roll(read, -(step[1] * NZ + step[2]), 1)
                if step[1]:
                    start = READS + Y_PAIRS.index(k) * NZ
                    side = right if step[1] > 0 else left
                    target = columns - NZ if step[1] > 0 else 0
                    part = side[:, start // 128 * 128 : start // 128 * 128 + 128]
                    part = roll(part, target - start, 1)
                    border = column >= columns - NZ if step[1] > 0 else column < NZ
                    spread = jnp.concatenate([part] * (columns // 128), axis=1)
                    read = jnp.where(border, spread, read)
                if step[2]:
                    bounce = adjoint[member_of(k, -sign), rows, :]
                    read = jnp.where(leaves_depth(shape, step[2]), bounce, read)
                reads.append(read)
            both = reads[0] + reads[1]
            odd = blend * (reads[0] - reads[1])
            projected = dot_velocity(PAIRS[k], velocity)
            even_part = WEIGHTS[k] * both
            zeroth = zeroth + even_part
            moved = even_part * projected
            square = moved * projected
            quadratic = square if quadratic is None else quadratic + square
            pull = (3.0 * WEIGHTS[k]) * odd + 9.0 * moved
            for axis in range(3):
                if PAIRS[k][axis]:
                    vector[axis] = (
                        signed_sum([(PAIRS[k][axis], pull)])
                        if vector[axis] is None
                        else signed_sum([(1, vector[axis]), (PAIRS[k][axis], pull)])
                    )
            kept.append((reads[0], reads[1], both, odd))
        scaled = relax_rate * zeroth
        base = scaled * (1.0 + 1.5 * speed_sq) - (4.5 * relax_rate) * quadratic + source
        vector = [
            relax_rate * part - (3.0 * scaled) * speed for part, speed in zip(vector, velocity)
        ]
        keep = relax_rate - 1.0
        adjoint_new[0, rows, :] = jnp.where(wall, rest, base - keep * rest)
        for k in range(9):
            one, other, both, odd = kept[k]
            level = base - (0.5 * keep) * both
            slope = dot_velocity(PAIRS[k], vector) - (0.5 * keep) * odd
            adjoint_new[2 * k + 1, rows, :] = jnp.where(wall, other, level + slope)
            adjoint_new[2 * k + 2, rows, :] = jnp.where(wall, one, level - slope)
        part = pl.ds(tile * ROWS, ROWS)
        sent.append(
            pltpu.make_async_copy(
                adjoint_new.at[:, part, :], result.at[:, part, :], out_sems.at[tile]
            )
        )
        sent[-1].start()
    for copy in sent:
        copy.wait()


def run(kernel, outputs, *operands, flops, far=0, far_out=False, scratch=(), vmem=32):
    sizes = [jax.ShapeDtypeStruct(shape, jnp.float32) for shape in outputs]
    moved = 4 * sum(a.size for a in operands) + 4 * sum(s.size for s in sizes)
    operands = [
        pltpu.with_memory_space_constraint(a, pltpu.HBM) if i < far else a
        for i, a in enumerate(operands)
    ]
    near = pl.BlockSpec(memory_space=pltpu.VMEM)
    away = pl.BlockSpec(memory_space=pl.ANY)
    return pl.pallas_call(
        kernel,
        out_shape=sizes,
        in_specs=[away if i < far else near for i in range(len(operands))],
        out_specs=[away if far_out else near for _ in outputs],
        scratch_shapes=list(scratch),
        compiler_params=pltpu.CompilerParams(vmem_limit_bytes=vmem * 1024 * 1024),
        cost_estimate=pl.CostEstimate(flops=flops, bytes_accessed=moved, transcendentals=0),
    )(*operands)


def swap(first, second, axis, closed):
    count = lax.axis_size(axis)
    starts = range(1, count if closed else count - 1, 2)
    far = [(i, (i + 1) % count) for i in starts]
    far = far + [(b, a) for a, b in far]
    near = [(i, i ^ 1) for i in range(count)]
    return lax.ppermute(first, axis, far), lax.ppermute(second, axis, near)


def shards(forward, adjoint, design, node_type):
    members, layers, columns = adjoint.shape
    sites = layers * columns
    devices = lax.axis_size("gx") * lax.axis_size("gy")
    plane = (layers, columns)
    face = (2 * ROWS, columns)
    side = (layers + ROWS, 256)
    tiles = layers // ROWS
    field = pltpu.VMEM((members,) + plane, jnp.float32)
    end = pltpu.VMEM((members, ROWS, columns), jnp.float32)

    def border(near):
        (message,) = run(
            functools.partial(border_kernel, near),
            [face],
            forward,
            adjoint,
            node_type,
            far=3,
            scratch=[
                end,
                end,
                pltpu.VMEM((ROWS, columns), jnp.int32),
                pltpu.SemaphoreType.DMA((7,)),
            ],
            flops=40 * sites,
        )
        return message

    own_z = border(False)
    own_s = border(True)
    got_z, got_s = swap(own_z, own_s, "gx", True)
    got_z = lax.optimization_barrier(got_z)
    partial, edges = run(
        collide_kernel,
        [plane, (layers, 512)],
        forward,
        adjoint,
        node_type,
        flops=150 * sites,
    )
    given = (partial, edges, own_s, own_z, got_s, got_z)
    across = (layers + ROWS, columns)
    (out_z,) = run(
        functools.partial(faces_kernel, False),
        [side],
        *given,
        scratch=[pltpu.VMEM(across, jnp.float32)],
        flops=10 * sites,
    )
    out_s, wide = run(
        functools.partial(faces_kernel, True), [side, across], *given, flops=10 * sites
    )
    side_z, side_s = swap(out_z, out_s, "gy", False)
    side_z = lax.optimization_barrier(side_z)
    basis, shares = run(
        krylov_kernel,
        [(ITERS,) + plane, (devices, 128)],
        wide,
        out_s,
        out_z,
        side_s,
        side_z,
        flops=60 * sites,
    )
    spread = lax.all_to_all(shares.reshape(devices, 1, 128), ("gx", "gy"), 0, 0)
    (adjoint_new,) = run(
        adjoint_kernel,
        [adjoint.shape],
        forward,
        adjoint,
        design,
        node_type,
        got_s,
        got_z,
        side_s,
        side_z,
        far=4,
        far_out=True,
        scratch=[
            field,
            field,
            pltpu.VMEM(plane, jnp.float32),
            pltpu.VMEM(plane, jnp.int32),
            field,
            pltpu.SemaphoreType.DMA((tiles, 4)),
            pltpu.SemaphoreType.DMA((tiles,)),
        ],
        flops=400 * sites,
    )
    (filtered,) = run(
        combine_kernel, [plane], spread.reshape(devices, 128), basis, flops=10 * sites
    )
    return (adjoint_new, filtered)


def solution(mesh):
    placed = (P(None, "gx", "gy"), P(None, "gx", "gy"), P("gx", "gy"), P("gx", "gy"))
    return jax.shard_map(
        shards,
        mesh=mesh,
        in_specs=placed,
        out_specs=(P(None, "gx", "gy"), P("gx", "gy")),
        check_vma=False,
    )
```
